32 devices in a mesh: section: 4 (over y, x), dp: 8 (over z, core).
Axes of the slice: x: 2, y: 2, z: 4, core: 2. Of those that a mesh axis runs over, the one named last changes fastest.
Arguments:
- inputs: bfloat16 [8, 8, 256, 768], P('section', 'dp'), may hold values from -6 to 6
- cotangent: bfloat16 [8, 8, 256, 768], P('section', 'dp'), may hold values from -6 to 6
- segments: int32 [8, 8, 256], P(None, 'dp'), may hold values from 0 to 255, as said below
- matrices: bfloat16 [4, 3, 768, 768], P('section')
- attn_vectors: float32 [2, 4, 768], replicated
- ffn_vectors: float32 [2, 5, 768], replicated
Outputs:
- outputs: bfloat16 [8, 8, 256, 768], P('section', 'dp')
- grad_inputs: bfloat16 [8, 8, 256, 768], P('section', 'dp')
- grad_matrices: float32 [4, 3, 768, 768], P('section')
- grad_attn_vectors: float32 [2, 4, 768], replicated
- grad_ffn_vectors: float32 [2, 5, 768], replicated
The draws below stay inside these ranges and needn't reach their ends.
Inputs may be any that keep to these rules, and one draw needn't show every extreme that they name: `segments`: along each packed row the ids never fall; tokens of a row with equal ids form one molecule and attend only to each other. A row's first id is 0 and its last token forms a molecule of its own with id 256 - 1.
All inputs are finite; a program needn't handle non-finite values.
Results may differ from the reference program's by a relative error of at most 0.015.
Values may be sent and summed in bfloat16 or wider, within the bound.
No kernel may reach another device: no remote copies, remote signals or barrier semaphores. Data moves between devices by JAX's collectives and lax.ppermute only.
A program may use at most 192 MiB of HBM per device.

```python
import math
import jax
import jax.numpy as jnp
from jax import lax

D = 768
HEADS = 32
ROW_LEN = 256
MICRO = 8
LAYERS = 2
ROWS_MB = 8


def draw_segments(key, part):
    key = jax.random.fold_in(key, 11)
    key_start, key_large, key_place = jax.random.split(key, 3)
    full_shape = (MICRO, ROWS_MB, ROW_LEN)
    position = lax.broadcasted_iota(jnp.int32, full_shape, 2)
    starts = jax.random.randint(key_start, full_shape, 0, 24) == 0
    has_large = jax.random.randint(key_large, (MICRO, ROWS_MB, 1), 0, 6) == 0
    large_span = 3 * ROW_LEN // 4
    large_start = jax.random.randint(key_place, (MICRO, ROWS_MB, 1), 1, ROW_LEN - large_span)
    inside = has_large & (position > large_start) & (position < large_start + large_span)
    starts = starts & jnp.logical_not(inside) | (position == 0) | (position == ROW_LEN - 1)
    return lax.cummax(jnp.where(starts, position, 0), axis=2)


def draw_matrices(key, part):
    key = jax.random.fold_in(key, 5)
    full_shape = (2 * LAYERS, 3, D, D)
    entries = jax.random.normal(key, full_shape, jnp.float32)
    section_ids = lax.broadcasted_iota(jnp.int32, full_shape, 0)
    slot_ids = lax.broadcasted_iota(jnp.int32, full_shape, 1)
    boost = jnp.where((section_ids % 2 == 1) & (slot_ids == 0), 3.0, 1.0)
    return (entries * boost / math.sqrt(D)).astype(jnp.bfloat16)


def draw_attn_vectors(key, part):
    key = jax.random.fold_in(key, 7)
    key_gain, key_bias = jax.random.split(key)
    full_shape = (LAYERS, 4, D)
    gain_draw = jax.random.uniform(key_gain, full_shape, jnp.float32, 0.6, 1.4)
    biases = 0.3 * jax.random.normal(key_bias, full_shape, jnp.float32)
    slot_ids = lax.broadcasted_iota(jnp.int32, full_shape, 1)
    return jnp.where(slot_ids == 0, gain_draw, biases)


def draw_ffn_vectors(key, part):
    key = jax.random.fold_in(key, 9)
    key_gain, key_bias = jax.random.split(key)
    full_shape = (LAYERS, 5, D)
    gain_draw = jax.random.uniform(key_gain, full_shape, jnp.float32, 0.6, 1.4)
    biases = 0.3 * jax.random.normal(key_bias, full_shape, jnp.float32)
    slot_ids = lax.broadcasted_iota(jnp.int32, full_shape, 1)
    return jnp.where(slot_ids == 1, gain_draw, biases)


def block_scale(own_key, extent, cuts, smallest, high):
    level, own = 1.0, jax.random.fold_in(own_key, 6)
    for dim, parts in cuts:
        heights = jnp.exp(jax.random.uniform(jax.random.fold_in(own, dim), (parts,), jnp.float32, smallest / len(cuts), high / len(cuts)))
        level = level * jnp.repeat(heights, extent[dim] // parts).reshape([-1 if axis == dim else 1 for axis in range(len(extent))])
    return level


def centred(stream_key, dims, scale, bound, cuts=(), dtype=jnp.bfloat16):
    values = scale * jax.random.normal(stream_key, dims, jnp.float32)
    if cuts:
        values = values * block_scale(stream_key, dims, cuts, -0.22, 0.18)
    return jnp.clip(values, -bound, bound).astype(dtype)


def setup_inputs(seed: int = 0) -> dict:
    seeds = jax.random.split(jax.random.key(seed), 7)
    inputs = centred(seeds[0], (MICRO, ROWS_MB, ROW_LEN, D), 1.0, 6.0, ((0, 4), (1, 8)))
    cotangent = centred(seeds[1], (MICRO, ROWS_MB, ROW_LEN, D), 1.0, 6.0, ((0, 4), (1, 8)))
    segments = draw_segments(jax.random.fold_in(seeds[6], 71), 0)
    matrices = draw_matrices(jax.random.fold_in(seeds[6], 71), 0)
    attn_vectors = draw_attn_vectors(jax.random.fold_in(seeds[6], 71), 0)
    ffn_vectors = draw_ffn_vectors(jax.random.fold_in(seeds[6], 71), 0)
    return dict(inputs=inputs, cotangent=cotangent, segments=segments, matrices=matrices, attn_vectors=attn_vectors, ffn_vectors=ffn_vectors)


@jax.custom_vjp
def low(v):
    return lax.optimization_barrier(v.astype(jnp.bfloat16)).astype(jnp.float32)

@jax.custom_vjp
def low_back(v):
    return v

def low_keep(v):
    return (low(v), None)

def low_pass(kept, grad):
    return (grad,)

def back_keep(v):
    return (v, None)

def back_low(kept, grad):
    return (low(grad),)
low.defvjp(low_keep, low_pass)
low_back.defvjp(back_keep, back_low)
epsilon = 1e-05
highest = lax.Precision.HIGHEST

def both_ways(tensor):
    return low_back(low(tensor))

def layer_norm(tensor, ln_gain, offset):
    center = tensor - lax.optimization_barrier(jnp.mean(tensor, axis=-1, keepdims=True))
    spread = lax.optimization_barrier(jnp.mean(center * center, axis=-1, keepdims=True))
    return center * lax.rsqrt(spread + epsilon) * ln_gain + offset

def project(tensor, matrix):
    return jnp.einsum('rsd,de->rse', tensor, matrix, precision=highest)

def attend_block(block_in):
    queries, key_rows, value_rows, labels = block_in
    row_count, length, model_width = queries.shape
    head_size = model_width // HEADS
    head_shape = (row_count, length, HEADS, head_size)
    scores = jnp.einsum('gqhe,gkhe->ghqk', queries.reshape(head_shape), key_rows.reshape(head_shape), precision=highest)
    scores = low_back(scores * (1.0 / math.sqrt(head_size)))
    same_mol = labels[:, None, :, None] == labels[:, None, None, :]
    scores = jnp.where(same_mol, scores, -1e+30)
    top_score = lax.optimization_barrier(jnp.max(scores, axis=-1, keepdims=True))
    exp_scores = jnp.exp(scores - top_score)
    prob_rows = low(exp_scores / lax.optimization_barrier(jnp.sum(exp_scores, axis=-1, keepdims=True)))
    context = jnp.einsum('ghqk,gkhe->gqhe', prob_rows, value_rows.reshape(head_shape), precision=highest)
    return context.reshape(row_count, length, model_width)

def attention(queries, key_rows, value_rows, labels):
    row_count, length, model_width = queries.shape
    block_rows = math.gcd(row_count, max(1, 512 // length))

    def split_rows(tensor):
        return tensor.reshape((row_count // block_rows, block_rows) + tensor.shape[1:])
    context = lax.map(jax.checkpoint(attend_block), (split_rows(queries), split_rows(key_rows), split_rows(value_rows), split_rows(labels)))
    return context.reshape(row_count, length, model_width)

def forward(inputs_f, labels, matrices, attn_vectors, ffn_vectors):
    residual = inputs_f
    normed = low(layer_norm(inputs_f, attn_vectors[0, 0], attn_vectors[0, 1]))
    for layer_id in range(LAYERS):
        attn_mats = matrices[2 * layer_id]
        ffn_mats = matrices[2 * layer_id + 1]
        attn_part = attn_vectors[layer_id]
        ffn_part = ffn_vectors[layer_id]
        queries = both_ways(project(normed, attn_mats[0]) + attn_part[2])
        key_rows = both_ways(project(normed, attn_mats[1]))
        value_rows = both_ways(project(normed, attn_mats[2]) + attn_part[3])
        context = both_ways(attention(queries, key_rows, value_rows, labels))
        branch = low_back(project(context, ffn_mats[0]) + ffn_part[0])
        hidden = low_back(residual) + branch
        middle = low(layer_norm(hidden, ffn_part[1], ffn_part[2]))
        raised = low_back(project(middle, ffn_mats[1]) + ffn_part[3])
        active = low(jax.nn.gelu(raised, approximate=False))
        lowered = low_back(project(active, ffn_mats[2]) + ffn_part[4])
        summed = hidden + lowered
        residual = low(summed)
        if layer_id + 1 < LAYERS:
            normed = both_ways(layer_norm(summed, attn_vectors[layer_id + 1, 0], attn_vectors[layer_id + 1, 1]))
    return residual

def reference(inputs, cotangent, segments, matrices, attn_vectors, ffn_vectors):
    row_total = MICRO * ROWS_MB
    group_rows = math.gcd(row_total, max(1, 4096 // ROW_LEN))
    grid_shape = (row_total // group_rows, group_rows, ROW_LEN, D)
    input_rows = inputs.astype(jnp.float32).reshape(grid_shape)
    cot_rows = cotangent.astype(jnp.float32).reshape(grid_shape)
    label_rows = segments.reshape(grid_shape[:3])
    mats_f = matrices.astype(jnp.float32)

    def scan_step(carried, block_in):
        x_block, c_block, l_block = block_in

        def run_layers(x_in, mats_in, attn_in, ffn_in):
            return forward(x_in, l_block, mats_in, attn_in, ffn_in)
        result, pullback = jax.vjp(run_layers, x_block, mats_f, attn_vectors, ffn_vectors)
        grad_in, grad_mats, grad_attn, grad_ffn = pullback(c_block)
        carried = (carried[0] + grad_mats, carried[1] + grad_attn, carried[2] + grad_ffn)
        return (carried, (result.astype(jnp.bfloat16), grad_in.astype(jnp.bfloat16)))
    initial = (jnp.zeros_like(mats_f), jnp.zeros_like(attn_vectors), jnp.zeros_like(ffn_vectors))
    sums, rows_out = lax.scan(scan_step, initial, (input_rows, cot_rows, label_rows))
    return (rows_out[0].reshape(inputs.shape), rows_out[1].reshape(inputs.shape), sums[0], sums[1], sums[2])
```

```python
import functools
import math

import jax
import jax.numpy as jnp
from jax import lax
from jax.experimental import pallas as pl
from jax.experimental.pallas import tpu as pltpu
from jax.sharding import PartitionSpec as P

HEADS = 32
HD = 24
D = 768
L = 256
R = 2
T = R * L
EPS = 1e-05
LOG2E = math.log2(math.e)
SCALE = 1.0 / math.sqrt(HD)
C2 = LOG2E * SCALE
NEG = -1e30 * math.sqrt(HD)
BF = jnp.bfloat16
F32 = jnp.float32
GROUP = 16
GW = GROUP * HD
ROWS = 128

PIECES = [(c, p) for c in (0, 1) for p in (0, 1)]
N_PIECES = 3 * len(PIECES)
RIDE = 16

NN = (((1,), (0,)), ((), ()))
NT = (((1,), (1,)), ((), ()))


def dot(a, b, dims=NN):
    return lax.dot_general(a, b, dims, preferred_element_type=F32)


def cost(us):
    return pl.CostEstimate(flops=int(us * 1.1e9), bytes_accessed=1 << 20, transcendentals=0)


def params(mb=16):
    return pltpu.CompilerParams(vmem_limit_bytes=mb * 1024 * 1024)


def ln_stats(v):
    center = v - jnp.mean(v, axis=-1, keepdims=True)
    spread = jnp.mean(center * center, axis=-1, keepdims=True)
    r = lax.rsqrt(spread + EPS)
    return center * r, r


def ln_back(v, gain, dy):
    xhat, r = ln_stats(v)
    e = dy * gain
    dv = r * (e - jnp.mean(e, axis=-1, keepdims=True) - xhat * jnp.mean(e * xhat, axis=-1, keepdims=True))
    return dv, dy * xhat


def fold(v):
    return jnp.sum(v.reshape(v.shape[0] // 8, 8, v.shape[1]), axis=0)


def row_loop(fn, init=0):
    def step(i, c):
        return fn(pl.ds(pl.multiple_of(i * ROWS, ROWS), ROWS), c)

    return lax.fori_loop(0, T // ROWS, step, init)


def head_window(i):
    start = HD * i
    lane0 = start // 128 * 128
    width = 128 if start + HD <= lane0 + 128 else 256
    sub0 = start // 16 * 16
    return lane0, width, start - lane0, sub0, start - sub0


def lane_mask(width, at):
    pos = lax.broadcasted_iota(jnp.int32, (1, width), 1)
    return jnp.where((pos >= at) & (pos < at + HD), 1.0, 0.0).astype(BF)


def row_ones(off):
    pos = lax.broadcasted_iota(jnp.int32, (32, L), 0)
    own = jnp.where((pos >= off) & (pos < off + HD), 1.0, 0.0)
    return own.astype(BF), (1.0 - own).astype(BF)


def dense_cols(lhs, w, fn, dims=NN, m_rows=256, n_cols=256):
    for n in range(0, D, n_cols):
        block = w[:, n:n + n_cols] if dims is NN else w[n:n + n_cols, :]
        for m in range(0, T, m_rows):
            fn(slice(m, m + m_rows), slice(n, n + n_cols), dot(lhs[m:m + m_rows, :], block, dims))


def fetch(place_ref, own_ref, piece_refs, w_s, sems, order):
    which, core, par = place_ref[0], place_ref[1], place_ref[2]

    @pl.when(which == 0)
    def _():
        for m in order:
            pltpu.make_async_copy(own_ref.at[m], w_s.at[m], sems.at[m]).start()

    for k in range(1, 4):
        @pl.when(which == k)
        def _(k=k):
            for m in order:
                for n, (c, p) in enumerate(PIECES):
                    at = (core ^ c) * (D // 2) + (par ^ p) * (D // 4)
                    rows = pl.ds(pl.multiple_of(at, D // 4), D // 4)
                    src = piece_refs[(k - 1) * len(PIECES) + n]
                    pltpu.make_async_copy(src.at[m], w_s.at[m, rows], sems.at[m]).start()


def arrived(own_ref, w_s, sems, m):
    pltpu.make_async_copy(own_ref.at[m], w_s.at[m], sems.at[m]).wait()


def staggered(first, second, third, lead1, lead2):
    one, two = {}, {}
    for i in range(GROUP + lead1 + lead2):
        if i < GROUP:
            one[i] = first(i)
        if 0 <= i - lead1 < GROUP:
            two[i - lead1] = second(i - lead1, *one.pop(i - lead1))
        if 0 <= i - lead1 - lead2 < GROUP:
            third(i - lead1 - lead2, *two.pop(i - lead1 - lead2))


def fill_mask(segc_ref, segr_ref, mask_s):
    for r in range(R):
        mask_s[r] = jnp.where(segc_ref[r] == segr_ref[r], 1, 0)


def attn_fwd_body(first, place_ref, x_ref, vec_ref, segc_ref, segr_ref, own_ref, *rest):
    pieces, rest = rest[:N_PIECES], rest[N_PIECES:]
    w_s, sems = rest[-2:]
    rest = rest[:-2]
    fetch(place_ref, own_ref, pieces, w_s, sems, (0, 1, 2))
    if first:
        normed_ref, q_ref, k_ref, v_ref, ctx_ref, lse_ref, vt_s, ct_s, mask_s = rest

        def norm(rows, c):
            xhat, _ = ln_stats(x_ref[rows, :].astype(F32))
            normed_ref[rows, :] = (xhat * vec_ref[0:1, :] + vec_ref[1:2, :]).astype(BF)
            return c

        row_loop(norm)
    else:
        normed_ref = x_ref
        q_ref, k_ref, v_ref, ctx_ref, lse_ref, vt_s, ct_s, mask_s = rest
    fill_mask(segc_ref, segr_ref, mask_s)
    cq, cv = vec_ref[2:3, :], vec_ref[3:4, :]

    def put_q(rows, cols, y):
        q_ref[rows, cols] = (y + cq[:, cols]).astype(BF)

    def put_k(rows, cols, y):
        k_ref[rows, cols] = y.astype(BF)

    def put_v(rows, cols, y):
        y = (y + cv[:, cols]).astype(BF)
        v_ref[rows, cols] = y
        vt_s[cols, rows] = y.T

    for m, put in enumerate((put_q, put_k, put_v)):
        arrived(own_ref, w_s, sems, m)
        dense_cols(normed_ref, w_s.at[m], put)

    def heads(t, c):
        r, g = t // 2, t % 2
        tok = pl.ds(pl.multiple_of(r * L, L), L)
        base = g * GW

        def score(i):
            lane0, width, at, _, _ = head_window(i)
            lanes = pl.ds(pl.multiple_of(base + lane0, 128), width)
            return (dot(k_ref[tok, lanes], q_ref[tok, lanes] * lane_mask(width, at), NT),)

        def soften(i, s):
            s = jnp.where(mask_s[r] != 0, s, NEG)
            top = jnp.max(s, axis=0, keepdims=True)
            return jnp.exp2((s - top) * C2).astype(BF), top

        def mix(i, e, top):
            _, _, _, sub0, off = head_window(i)
            own, ones = row_ones(off)
            out = dot(vt_s[pl.ds(pl.multiple_of(base + sub0, 16), 32), tok] * own + ones, e)
            tot = out[24:25] if off == 0 else out[0:1]
            ct_s[pl.ds(pl.multiple_of(base + HD * i, 8), HD), tok] = out[off:off + HD] * (1.0 / tot)
            lse_ref[pl.ds(g * GROUP + i, 1), tok] = top * C2 + jnp.log(tot) * LOG2E

        staggered(score, soften, mix, 3, 2)
        return c

    lax.fori_loop(0, 2 * R, heads, 0)
    for m in range(0, T, 256):
        for n in range(0, D, 128):
            ctx_ref[m:m + 256, n:n + 128] = ct_s[n:n + 128, m:m + 256].T.astype(BF)


VM = pl.BlockSpec(memory_space=pltpu.VMEM)
SM = pl.BlockSpec(memory_space=pltpu.SMEM)
HB = pl.BlockSpec(memory_space=pl.ANY)
TOK = jax.ShapeDtypeStruct((T, D), BF)
TOK_F = jax.ShapeDtypeStruct((T, D), F32)
HALF = jax.ShapeDtypeStruct((3, D // 2, D), BF)
VEC = jax.ShapeDtypeStruct((8, D), F32)
S_TOK = pltpu.VMEM((T, D), BF)
S_TOK_F = pltpu.VMEM((T, D), F32)
S_TOK_T = pltpu.VMEM((D, T), BF)
S_TOK_TF = pltpu.VMEM((D, T), F32)
S_MASK = pltpu.VMEM((R, L, L), jnp.int32)
S_W = [pltpu.VMEM((3, D, D), BF), pltpu.SemaphoreType.DMA((3,))]


def call(body, name, place, ins, weights, outs, scratch, us):
    return pl.pallas_call(
        body,
        out_shape=outs,
        in_specs=[SM] + [VM] * len(ins) + [HB] * len(weights),
        out_specs=[VM] * len(outs),
        scratch_shapes=scratch + S_W,
        compiler_params=params(),
        cost_estimate=cost(us),
        name=name,
    )(place, *ins, *weights)


def attn_fwd(first, place, x, vec, segc, segr, weights):
    outs = ((TOK,) if first else ()) + (TOK, TOK, TOK, TOK, jax.ShapeDtypeStruct((HEADS, T), F32))
    name = "attn_fwd_first" if first else "attn_fwd"
    return call(functools.partial(attn_fwd_body, first), name, place, (x, vec, segc, segr), weights, outs,
                [S_TOK_T, S_TOK_TF, S_MASK], 9)


def attn_bwd_body(group, place_ref, normed_ref, q_ref, k_ref, v_ref, lse_ref, do_ref, segc_ref, segr_ref,
                  keep_ref, send_ref, gvec_ref, dq_ref, dk_ref, dv_ref,
                  nt_s, qt_s, kt_s, dot_s, dqf_s, dkf_s, dvf_s, mask_s):
    cols = slice(group * GW, group * GW + GW)
    q_ref, k_ref, v_ref, do_ref = (ref.at[:, cols] for ref in (q_ref, k_ref, v_ref, do_ref))
    fill_mask(segc_ref, segr_ref, mask_s)
    for src, dst in ((normed_ref, nt_s), (q_ref, qt_s), (k_ref, kt_s), (do_ref, dot_s)):
        for m in range(0, T, 256):
            for n in range(0, src.shape[1], 128):
                dst[n:n + 128, m:m + 256] = src[m:m + 256, n:n + 128].T

    def heads(r, c):
        tok = pl.ds(pl.multiple_of(r * L, L), L)

        def score(i):
            lane0, width, at, _, _ = head_window(i)
            lanes = slice(lane0, lane0 + width)
            own = lane_mask(width, at)
            return (dot(k_ref[tok, lanes], q_ref[tok, lanes] * own, NT),
                    dot(v_ref[tok, lanes], do_ref[tok, lanes] * own, NT))

        def soften(i, s, dp):
            head = group * GROUP + i
            s = jnp.where(mask_s[r] != 0, s, NEG)
            p = jnp.exp2(s * C2 - lse_ref[head:head + 1, tok])
            t1 = p * dp
            delta = jnp.sum(t1, axis=0, keepdims=True)
            return p.astype(BF), (t1 - p * delta).astype(BF)

        def mix(i, p, ds):
            _, _, _, sub0, off = head_window(i)
            sub = slice(sub0, sub0 + 32)
            out = slice(HD * i, HD * i + HD)
            dvf_s[out, tok] = dot(dot_s[sub, tok], p, NT)[off:off + HD]
            dkf_s[out, tok] = dot(qt_s[sub, tok], ds, NT)[off:off + HD] * SCALE
            dqf_s[out, tok] = dot(kt_s[sub, tok], ds, NN)[off:off + HD] * SCALE

        staggered(score, soften, mix, 1, 1)
        return c

    lax.fori_loop(0, R, heads, 0)

    def shorten(i, c):
        rows = pl.ds(pl.multiple_of(i * 64, 64), 64)
        dq_ref[rows, :] = dqf_s[rows, :].astype(BF)
        dk_ref[rows, :] = dkf_s[rows, :].astype(BF)
        dv_ref[rows, :] = dvf_s[rows, :].astype(BF)
        return c

    lax.fori_loop(0, GW // 64, shorten, 0)
    core = place_ref[1]
    mine = pl.ds(pl.multiple_of(core * 384, 128), 384)
    other = pl.ds(pl.multiple_of((1 - core) * 384, 128), 384)
    for j, grad in enumerate((dq_ref, dk_ref, dv_ref)):
        send_ref[j] = dot(nt_s[other, :], grad[...], NT).astype(BF)
        keep_ref[j] = dot(nt_s[mine, :], grad[...], NT).astype(BF)
    ones = jnp.ones((8, T), BF)
    gvec_ref[0:1, :] = dot(ones, dq_ref[...], NT)[0:1]
    gvec_ref[1:2, :] = dot(ones, dv_ref[...], NT)[0:1]


def grad_normed(own_ref, w_s, sems, grads, put):
    for m in range(3):
        arrived(own_ref, w_s, sems, m)
    for m in range(0, D, 256):
        for n in range(0, T, 256):
            y = 0.0
            for j in range(6):
                cols = slice(j // 3 * GW, j // 3 * GW + GW)
                y += dot(w_s[j % 3, m:m + 256, cols], grads[j][:, n:n + 256])
            put(slice(n, n + 256), slice(m, m + 256), y.T)


def attn_bwd(group, place, normed, q, k, v, lse, grad_ctx, segc, segr, name):
    part = jax.ShapeDtypeStruct((3, D // 2, GW), BF)
    grad = jax.ShapeDtypeStruct((GW, T), BF)
    s_part, s_part_f = pltpu.VMEM((GW, T), BF), pltpu.VMEM((GW, T), F32)
    return pl.pallas_call(
        functools.partial(attn_bwd_body, group),
        out_shape=(part, part, jax.ShapeDtypeStruct((8, GW), F32), grad, grad, grad),
        in_specs=[SM] + [VM] * 8,
        out_specs=(VM,) * 6,
        scratch_shapes=[S_TOK_T] + [s_part] * 3 + [s_part_f] * 3 + [S_MASK],
        compiler_params=params(),
        cost_estimate=cost(8),
        name=name,
    )(place, normed, q, k, v, lse, grad_ctx, segc, segr)


def normed_bwd_body(place_ref, *rest):
    grads, (own_ref, *rest) = rest[:6], rest[6:]
    pieces, (gx_ref, w_s, sems) = rest[:N_PIECES], rest[N_PIECES:]
    fetch(place_ref, own_ref, pieces, w_s, sems, (0, 1, 2))

    def put(rows, cols, y):
        gx_ref[rows, cols] = y.astype(BF)

    grad_normed(own_ref, w_s, sems, grads, put)


def normed_bwd(place, grads, weights):
    return call(normed_bwd_body, "normed_bwd", place, grads, weights, (TOK,), [], 3)[0]


def inputs_bwd_body(place_ref, *rest):
    grads, (x_ref, branch_ref, vec_ref, *rest) = rest[:6], rest[6:]
    own_ref, pieces, outs, scratch, w_s, sems = split_refs(rest, 2)
    gx_ref, gvec_ref = outs
    gn_s = scratch[0]
    fetch(place_ref, own_ref, pieces, w_s, sems, (0, 1, 2))

    def put(rows, cols, y):
        gn_s[rows, cols] = y

    grad_normed(own_ref, w_s, sems, grads, put)

    def norm_back(rows, c):
        dy = gn_s[rows, :]
        dv, dg = ln_back(x_ref[rows, :].astype(F32), vec_ref[0:1, :], dy)
        gx_ref[rows, :] = (branch_ref[rows, :].astype(F32) + dv).astype(BF)
        return c[0] + fold(dg), c[1] + fold(dy)

    zero = jnp.zeros((8, D), F32)
    dg, db = row_loop(norm_back, (zero, zero))
    gvec_ref[...] = jnp.zeros(gvec_ref.shape, F32)
    gvec_ref[0:1, :] = jnp.sum(dg, axis=0, keepdims=True)
    gvec_ref[1:2, :] = jnp.sum(db, axis=0, keepdims=True)


def inputs_bwd(place, grads, x, branch, vec, weights):
    return call(inputs_bwd_body, "inputs_bwd", place, (*grads, x, branch, vec), weights, (TOK, VEC), [S_TOK_F], 4)


def ffn_forward(ready, res_ref, ctx_ref, w_ref, vec_ref, hid_s, mid_s, raised_s, act_s, gp_s, sum_put):
    co, gf, bf, c1, c2 = (vec_ref[i:i + 1, :] for i in range(5))

    def put_hidden(rows, cols, y):
        hid_s[rows, cols] = res_ref[rows, cols].astype(F32) + (y + co[:, cols])

    ready(0)
    dense_cols(ctx_ref, w_ref.at[0], put_hidden)

    def norm(rows, c):
        xhat, _ = ln_stats(hid_s[rows, :])
        mid_s[rows, :] = (xhat * gf + bf).astype(BF)
        return c

    row_loop(norm)

    def put_raised(rows, cols, y):
        raised_s[rows, cols] = y + c1[:, cols]

    ready(1)
    dense_cols(mid_s, w_ref.at[1], put_raised)

    def activate(rows, c):
        a = raised_s[rows, :]
        phi = 0.5 + 0.5 * lax.erf(a * (1.0 / math.sqrt(2.0)))
        act_s[rows, :] = (a * phi).astype(BF)
        density = jnp.exp2(a * a * (-0.5 * LOG2E)) * (1.0 / math.sqrt(2.0 * math.pi))
        gp_s[rows, :] = phi + a * density
        return c

    row_loop(activate)

    def put_summed(rows, cols, y):
        sum_put(rows, cols, hid_s[rows, cols] + (y + c2[:, cols]))

    ready(2)
    dense_cols(act_s, w_ref.at[2], put_summed)


def ffn_backward(ready, place_ref, gsum_s, glow_s, hid_s, gp_s, mid_s, act_s, ctx_ref, w_ref, vec_ref,
                 gbranch_ref, gctx_ref, keep_ref, send_ref, gvec_ref, graise_s, gmid_s, t_s):
    gf = vec_ref[1:2, :]
    core = place_ref[1]
    mine = pl.ds(pl.multiple_of(core * 384, 128), 384)
    other = pl.ds(pl.multiple_of((1 - core) * 384, 128), 384)
    zero = jnp.zeros((8, D), F32)

    def weight_grad(j, x_ref, grad_ref):
        for m in range(0, T, 256):
            for n in range(0, D, 256):
                t_s[n:n + 256, m:m + 256] = x_ref[m:m + 256, n:n + 256].T
        for n in range(0, D, 256):
            block = grad_ref[:, n:n + 256]
            send_ref[j, :, n:n + 256] = dot(t_s[other, :], block).astype(BF)
            keep_ref[j, :, n:n + 256] = dot(t_s[mine, :], block).astype(BF)

    def put_raised(rows, cols, y):
        graise_s[rows, cols] = (y * gp_s[rows, cols]).astype(BF)

    ready(2)
    dense_cols(glow_s, w_ref.at[2], put_raised, NT)
    weight_grad(2, act_s, glow_s)

    def put_mid(rows, cols, y):
        gmid_s[rows, cols] = y

    ready(1)
    dense_cols(graise_s, w_ref.at[1], put_mid, NT)
    weight_grad(1, mid_s, graise_s)

    def norm_back(rows, c):
        dy = gmid_s[rows, :]
        dv, dg = ln_back(hid_s[rows, :], gf, dy)
        branch = (gsum_s[rows, :].astype(F32) + dv).astype(BF)
        gbranch_ref[rows, :] = branch
        return (c[0] + fold(branch.astype(F32)), c[1] + fold(dg), c[2] + fold(dy),
                c[3] + fold(graise_s[rows, :].astype(F32)), c[4] + fold(glow_s[rows, :].astype(F32)))

    sums = row_loop(norm_back, (zero,) * 5)
    for i in range(5):
        gvec_ref[i:i + 1, :] = jnp.sum(sums[i], axis=0, keepdims=True)

    def put_ctx(rows, cols, y):
        gctx_ref[rows, cols] = y.astype(BF)

    ready(0)
    dense_cols(gbranch_ref, w_ref.at[0], put_ctx, NT)
    weight_grad(0, ctx_ref, gbranch_ref)


def split_refs(rest, outs):
    at = 1 + N_PIECES
    return rest[0], rest[1:at], rest[at:at + outs], rest[at + outs:-2], rest[-2], rest[-1]


def ffn_fwd_body(place_ref, res_ref, ctx_ref, vec_ref, next_ref, *rest):
    own_ref, pieces, outs, scratch, w_s, sems = split_refs(rest, 7)
    stream_ref, normed_ref, hid_ref, mid_ref, act_ref, gp_ref, sum_ref = outs
    fetch(place_ref, own_ref, pieces, w_s, sems, (0, 1, 2))

    def put(rows, cols, y):
        sum_ref[rows, cols] = y

    ffn_forward(functools.partial(arrived, own_ref, w_s, sems), res_ref, ctx_ref, w_s, vec_ref,
                hid_ref, mid_ref, scratch[0], act_ref, gp_ref, put)

    def norm(rows, c):
        v = sum_ref[rows, :]
        stream_ref[rows, :] = v.astype(BF)
        xhat, _ = ln_stats(v)
        normed_ref[rows, :] = (xhat * next_ref[0:1, :] + next_ref[1:2, :]).astype(BF)
        return c

    row_loop(norm)


def ffn_fwd(place, res, ctx, vec, nxt, weights):
    return call(ffn_fwd_body, "ffn_fwd", place, (res, ctx, vec, nxt), weights,
                (TOK, TOK, TOK_F, TOK, TOK, TOK_F, TOK_F), [S_TOK_F], 6)


def ffn_last_body(place_ref, res_ref, ctx_ref, vec_ref, cot_ref, *rest):
    own_ref, pieces, outs, scratch, w_s, sems = split_refs(rest, 6)
    out_ref, gbranch_ref, gctx_ref, keep_ref, send_ref, gvec_ref = outs
    hid_s, mid_s, raised_s, act_s, gp_s, graise_s, t_s = scratch
    fetch(place_ref, own_ref, pieces, w_s, sems, (0, 1, 2))

    def put(rows, cols, y):
        out_ref[rows, cols] = y.astype(BF)

    ffn_forward(functools.partial(arrived, own_ref, w_s, sems), res_ref, ctx_ref, w_s, vec_ref,
                hid_s, mid_s, raised_s, act_s, gp_s, put)
    gvec_ref[...] = jnp.zeros(gvec_ref.shape, F32)
    ffn_backward(lambda m: None, place_ref, cot_ref, cot_ref, hid_s, gp_s, mid_s, act_s, ctx_ref, w_s, vec_ref,
                 gbranch_ref, gctx_ref, keep_ref, send_ref, gvec_ref, graise_s, raised_s, t_s)


def ffn_last(place, res, ctx, vec, cot, weights):
    return call(ffn_last_body, "ffn_last", place, (res, ctx, vec, cot), weights, (TOK, TOK, TOK, HALF, HALF, VEC),
                [S_TOK_F, S_TOK, S_TOK_F, S_TOK, S_TOK_F, S_TOK, S_TOK_T], 12)


def ffn_bwd_body(place_ref, gstream_ref, gnormed_ref, sum_ref, next_ref, hid_ref, gp_ref, mid_ref, act_ref, ctx_ref, vec_ref, *rest):
    own_ref, pieces, outs, scratch, w_s, sems = split_refs(rest, 6)
    gbranch_ref, gctx_ref, keep_ref, send_ref, gvec_ref, gnext_ref = outs
    gsum_s, glow_s, graise_s, gmid_s, t_s = scratch
    fetch(place_ref, own_ref, pieces, w_s, sems, (2, 1, 0))
    zero = jnp.zeros((8, D), F32)

    def norm_back(rows, c):
        dy = gnormed_ref[rows, :].astype(F32)
        dv, dg = ln_back(sum_ref[rows, :], next_ref[0:1, :], dy)
        total = gstream_ref[rows, :].astype(F32) + dv
        gsum_s[rows, :] = total
        glow_s[rows, :] = total.astype(BF)
        return c[0] + fold(dg), c[1] + fold(dy)

    dg, db = row_loop(norm_back, (zero, zero))
    gvec_ref[...] = jnp.zeros(gvec_ref.shape, F32)
    gnext_ref[...] = jnp.zeros(gnext_ref.shape, F32)
    gnext_ref[0:1, :] = jnp.sum(dg, axis=0, keepdims=True)
    gnext_ref[1:2, :] = jnp.sum(db, axis=0, keepdims=True)
    ffn_backward(functools.partial(arrived, own_ref, w_s, sems), place_ref, gsum_s, glow_s, hid_ref, gp_ref, mid_ref, act_ref,
                 ctx_ref, w_s, vec_ref, gbranch_ref, gctx_ref, keep_ref, send_ref, gvec_ref, graise_s, gmid_s, t_s)


def ffn_bwd(place, gstream, gnormed, summed, nxt, hid, gp, mid, act, ctx, vec, weights):
    return call(ffn_bwd_body, "ffn_bwd", place, (gstream, gnormed, summed, nxt, hid, gp, mid, act, ctx, vec), weights,
                (TOK, TOK, HALF, HALF, VEC, VEC), [S_TOK_F, S_TOK, S_TOK, S_TOK_F, S_TOK_T], 10)


def split_low(v):
    high = v.astype(BF)
    return high, (v - high.astype(F32)).astype(BF)


def combine_body(tasks, place_ref, *refs):
    refs = list(refs)
    ins = [[refs.pop(0) for _ in range(2 * pairs + rider)] for _, pairs, rider, _ in tasks]
    outs = [[refs.pop(0) for _ in range((bit is not None) + 1 + rider)] for bit, _, rider, _ in tasks]
    for (bit, pairs, rider, riding), arrays, results in zip(tasks, ins, outs):
        rows_in = arrays[0].shape[1] - (RIDE if riding == 2 else 0)
        half = rows_in // (1 if bit is None else 2)
        sent = results[0]
        for n, out_ref in enumerate(results[:2] if bit is not None else results[:1]):
            at = 0
            if bit is not None:
                at = (place_ref[bit] ^ (1 - n)) * half
            rows = pl.ds(at if bit is None else pl.multiple_of(at, half), half)
            col = 0
            for p in range(pairs):
                a_ref, b_ref = arrays[2 * p], arrays[2 * p + 1]
                width = a_ref.shape[2]
                out_ref[:, 0:half, col:col + width] = a_ref[:, rows, :] + b_ref[:, rows, :]
                col += width
        if rider:
            vec = arrays[-1][...]
            if riding:
                got = arrays[1]
                for j in range(3):
                    low = got[j, rows_in:rows_in + RIDE, :].astype(F32)
                    vec_j = vec[8 * j:8 * j + 8] + low[0:8] + low[8:16]
                    results[-1][8 * j:8 * j + 8, :] = vec_j
            else:
                results[-1][...] = vec
            for j in range(3):
                high, low = split_low(results[-1][8 * j:8 * j + 8, :])
                sent[j, half:half + RIDE, :] = jnp.concatenate([high.astype(F32), low.astype(F32)], axis=0).astype(BF)


def combine(place, *tasks):
    outs, kinds, ins = [], [], []
    for bit, pairs, vec, riding in tasks:
        a = pairs[0][0]
        width = sum(mine.shape[2] for mine, _ in pairs)
        rows = (a.shape[1] - (RIDE if riding == 2 else 0)) // (1 if bit is None else 2)
        ride = 0 if vec is None else RIDE
        outs.append(jax.ShapeDtypeStruct((3, rows + ride, width), BF))
        if bit is not None:
            outs.append(jax.ShapeDtypeStruct((3, rows, width), BF))
        if vec is not None:
            outs.append(jax.ShapeDtypeStruct(vec.shape, F32))
        kinds.append((bit, len(pairs), vec is not None, riding))
        ins += [x for pair in pairs for x in pair] + ([] if vec is None else [vec])
    parts = list(pl.pallas_call(
        functools.partial(combine_body, kinds),
        out_shape=tuple(outs),
        in_specs=[SM] + [VM] * len(ins),
        out_specs=tuple([VM] * len(outs)),
        compiler_params=params(),
        cost_estimate=cost(0.5 * len(tasks)),
        name="combine",
    )(place, *ins))
    results = []
    for bit, _, rider, _ in kinds:
        count = (bit is not None) + 1 + rider
        results.append(tuple(parts[:count]) if count > 1 else parts[0])
        parts = parts[count:]
    return results


def add(bit, mine, got):
    return (bit, [(mine, got)], None, 0)


def join_rows(place_ref, out_ref, mine_ref, other_ref):
    half = D // 16
    for flipped, ref in ((0, mine_ref), (1, other_ref)):
        rows = pl.ds(pl.multiple_of((place_ref[5] ^ flipped) * half, half), half)
        out_ref[:, rows, :] = ref[:, 0:half, :]


def pick_body(place_ref, *refs):
    outs = refs[8:]
    for k in range(4):
        for j in range(4):
            @pl.when((place_ref[0] ^ k) == j)
            def _(k=k, j=j):
                join_rows(place_ref, outs[k], refs[2 * j], refs[2 * j + 1])


def pick(place, *ins):
    shape = jax.ShapeDtypeStruct((3, D // 8, D), BF)
    return pl.pallas_call(
        pick_body,
        out_shape=(shape,) * 4,
        in_specs=[SM] + [VM] * 8,
        out_specs=(VM,) * 4,
        compiler_params=params(),
        name="pick",
    )(place, *ins)


def assemble_body(c, place_ref, *refs):
    parts, out_ref, wide_s, sems = refs[:4], refs[-3], refs[-2], refs[-1]
    core = place_ref[1] ^ c
    copies = []
    for k, ref in enumerate(parts):
        section = place_ref[0] ^ k
        x_bit, y_bit = section % 2, section // 2
        row = jnp.where(core == 0, 2 * x_bit + y_bit, 2 * y_bit + x_bit)
        at = pl.multiple_of(core * (D // 2) + row * (D // 8), D // 8)
        wide_s[k] = ref[...].astype(F32)
        copies.append(pltpu.make_async_copy(wide_s.at[k], out_ref.at[:, pl.ds(at, D // 8), :], sems.at[k]))
        copies[-1].start()
    for copy in copies:
        copy.wait()


def assemble(place, c, parts, whole=None):
    extra = [] if whole is None else [whole]
    return pl.pallas_call(
        functools.partial(assemble_body, c),
        out_shape=jax.ShapeDtypeStruct((3, D, D), F32),
        in_specs=[SM] + [VM] * 4 + [HB] * len(extra),
        out_specs=HB,
        scratch_shapes=[pltpu.VMEM((4, 3, D // 8, D), F32), pltpu.SemaphoreType.DMA((4,))],
        input_output_aliases={5: 0} if extra else {},
        compiler_params=params(),
        name="assemble",
    )(place, *parts, *extra)


def stack_body(norm0_ref, a0_ref, b0_ref, norm1_ref, a1_ref, b1_ref, ffn0_ref, ffn1_ref, out_ref):
    for at, norm_ref, a_ref, b_ref in ((0, norm0_ref, a0_ref, b0_ref), (4, norm1_ref, a1_ref, b1_ref)):
        out_ref[at:at + 2, :] = norm_ref[0:2, :]
        out_ref[at + 2:at + 4, 0:GW] = a_ref[0:2, :]
        out_ref[at + 2:at + 4, GW:D] = b_ref[0:2, :]
    out_ref[8:13, :] = ffn0_ref[0:5, :]
    out_ref[13:18, :] = ffn1_ref[0:5, :]
    out_ref[18:24, :] = jnp.zeros((6, D), F32)


def stack_vectors(*parts):
    return pl.pallas_call(
        stack_body,
        out_shape=jax.ShapeDtypeStruct((24, D), F32),
        in_specs=[VM] * len(parts),
        out_specs=VM,
        compiler_params=params(),
        name="stack_vectors",
    )(*parts)


def unstack_body(mine_ref, other_ref, attn_ref, ffn_ref):
    for i in range(2):
        attn_ref[i] = mine_ref[4 * i:4 * i + 4, :] + other_ref[4 * i:4 * i + 4, :]
        ffn_ref[i] = mine_ref[8 + 5 * i:13 + 5 * i, :] + other_ref[8 + 5 * i:13 + 5 * i, :]


def unstack(mine, other):
    return pl.pallas_call(
        unstack_body,
        out_shape=(jax.ShapeDtypeStruct((2, 4, D), F32), jax.ShapeDtypeStruct((2, 5, D), F32)),
        in_specs=[VM] * 2,
        out_specs=(VM,) * 2,
        compiler_params=params(),
        name="unstack",
    )(mine, other)


def swap_cores(value):
    count = lax.axis_size("dp")
    return lax.ppermute(value, "dp", [(i, i ^ 1) for i in range(count)])


def next_chip(value, bits):
    count = lax.axis_size("dp")
    return lax.ppermute(value, "dp", [(i, i ^ 2 * bits) for i in range(count)])


def plane_swap(value, step):
    count, sections = lax.axis_size("dp"), lax.axis_size("section")
    pairs = []
    for s in range(sections):
        for i in range(count):
            other = s ^ (1 if step == i % 2 else 2)
            pairs.append((s * count + i, other * count + i))
    return lax.ppermute(value, ("section", "dp"), pairs)


def flip(value, bits):
    count = lax.axis_size("section")
    return lax.ppermute(value, "section", [(i, i ^ bits) for i in range(count)])


def gather_pieces(own, core, par, ready):
    def part(p):
        return lax.dynamic_slice(own, (0, core * (D // 2) + p * (D // 4), 0), (3, D // 4, D))

    near, down = flip(part(par), 1), flip(part(1 - par), 2)
    near, down, *ready = together(near, down, *ready)
    far_a, far_b = flip(near, 2), flip(down, 1)
    near_z, down_z = next_chip(near, 1), next_chip(down, 1)
    mine = [[near, near_z], [down_z, down], [far_a, far_b]]
    return [piece for group in mine for piece in group + [swap_cores(x) for x in group]], ready


def line_groups():
    count = lax.axis_size("dp")
    return [[r * 8 + i for r in range(count // 8)] for i in range(8)]


def across_lines(value):
    if lax.axis_size("dp") == 8:
        return value
    return lax.psum(value.astype(F32), "dp", axis_index_groups=line_groups()).astype(value.dtype)


def together(*values):
    return lax.optimization_barrier(values)


def shards(inputs, cotangent, segments, matrices, attn_vectors, ffn_vectors):
    section = lax.axis_index("section")
    dp = lax.axis_index("dp")
    core, position = dp % 2, dp // 2
    par = position % 2
    x_bit, y_bit = section % 2, section // 2
    first = jnp.where(core == 0, x_bit, y_bit)
    second = jnp.where(core == 0, y_bit, x_bit)
    own = matrices[0]
    turn = dp // 2 % 2
    places = [jnp.stack([section ^ j, core, par, first, second, turn]).astype(jnp.int32) for j in range(4)]
    seg = lax.dynamic_slice(segments, (R * section, 0, 0), (R, 1, L))
    ready = (*places, seg.reshape(R, L, 1), seg, jnp.pad(attn_vectors, ((0, 0), (0, 4), (0, 0))),
             jnp.pad(ffn_vectors, ((0, 0), (0, 3), (0, 0))))
    pieces, ready = gather_pieces(own, core, par, ready)
    weights = (own, *pieces)
    *places, segc, segr, av, fv = ready
    here = places[0]
    x = inputs.reshape(T, D)
    cot = cotangent.reshape(T, D)

    n0, q0, k0, v0, c0, l0 = attn_fwd(True, places[0], x, av[0], segc, segr, weights)
    stream, n1, hid, mid, act, gp, summed = ffn_fwd(places[1], x, c0, fv[0], av[1], weights)
    q1, k1, v1, c1, l1 = attn_fwd(False, places[2], n1, av[1], segc, segr, weights)
    out, gb1, gc1, keep3, send3, gv3 = ffn_last(places[3], stream, c1, fv[1], cot, weights)
    got3 = swap_cores(send3)

    keep2a, send2a, gv2a, *grads2 = attn_bwd(0, here, n1, q1, k1, v1, l1, gc1, segc, segr, "attn_bwd_1a")
    ((send3, keep3),) = combine(here, add(3, keep3, got3))
    send2a, send3 = together(send2a, send3)
    got3, got2a = plane_swap(send3, 0), swap_cores(send2a)
    gc1, keep3 = together(gc1, keep3)

    keep2b, send2b, gv2b, *grads2b = attn_bwd(1, here, n1, q1, k1, v1, l1, gc1, segc, segr, "attn_bwd_1b")
    got2b = swap_cores(send2b)
    gn1 = normed_bwd(places[2], (*grads2, *grads2b), weights)
    gn1, got2a, got2b, got3 = together(gn1, got2a, got2b, got3)
    (send3, keep3), (send2, keep2) = combine(here, add(4, keep3, got3), (3, [(keep2a, got2a), (keep2b, got2b)], None, 0))
    got3, got2 = plane_swap(send3, 1), plane_swap(send2, 0)
    gb1, keep3 = together(gb1, keep3)

    gb0, gc0, keep1, send1, gv1, gnext = ffn_bwd(places[1], gb1, gn1, summed, av[1], hid, gp, mid, act, c0, fv[0], weights)
    ((send3, keep3),) = combine(here, add(5, keep3, got3))
    send1, send3 = together(send1, send3)
    got3, got1 = next_chip(send3, 1), swap_cores(send1)
    gc0, keep3 = together(gc0, keep3)

    keep0a, send0a, gv0a, *grads0 = attn_bwd(0, here, n0, q0, k0, v0, l0, gc0, segc, segr, "attn_bwd_0a")
    (send2, keep2), (send1, keep1) = combine(here, add(4, keep2, got2), add(3, keep1, got1))
    send0a, send1 = together(send0a, send1)
    got2, got1, got0a = plane_swap(send2, 1), plane_swap(send1, 0), swap_cores(send0a)
    gc0, keep2 = together(gc0, keep2)

    keep0b, send0b, gv0b, *grads0b = attn_bwd(1, here, n0, q0, k0, v0, l0, gc0, segc, segr, "attn_bwd_0b")
    keep3, (send2, keep2) = combine(here, add(None, keep3, got3), add(5, keep2, got2))
    send0b, send2 = together(send0b, send2)
    got3, got2, got0b = next_chip(keep3, 2), next_chip(send2, 1), swap_cores(send0b)
    grads0b[0], keep3 = together(grads0b[0], keep3)

    gx, gv0n = inputs_bwd(places[0], (*grads0, *grads0b), x, gb0, av[0], weights)
    vec = stack_vectors(gv0n, gv0a, gv0b, gnext, gv2a, gv2b, gv1, gv3)
    (send0, keep0, vec), (send1, keep1) = combine(
        here, (3, [(keep0a, got0a), (keep0b, got0b)], vec, 0), add(4, keep1, got1))
    got0, got1 = plane_swap(send0, 0), plane_swap(send1, 1)

    (send0, keep0, vec), (send1, keep1), keep2, keep3 = combine(
        here, (4, [(keep0, got0)], vec, 1), add(5, keep1, got1), add(None, keep2, got2), add(None, keep3, got3))
    got0, got1, got2, got3 = plane_swap(send0, 1), next_chip(send1, 1), next_chip(keep2, 2), next_chip(keep3, 1)

    got3, got2 = together(got3, got2)
    (send0, keep0, vec), keep1, keep2 = combine(
        here, (5, [(keep0, got0)], vec, 1), add(None, keep1, got1), add(None, keep2, got2))
    got0, got1, got2 = next_chip(send0, 1), next_chip(keep1, 2), next_chip(keep2, 1)

    got2, got1 = together(got2, got1)
    (sum0, vec), keep1 = combine(here, (None, [(keep0, got0)], vec, 1), add(None, keep1, got1))
    got0, got1 = next_chip(sum0, 2), next_chip(keep1, 1)

    got1, got0 = together(got1, got0)
    ((keep0, vec),) = combine(here, (None, [(sum0, got0)], vec, 2))
    got0 = next_chip(keep0, 1)
    vec = across_lines(vec)
    vec_got = swap_cores(vec)

    parts = pick(here, *(across_lines(v) for v in (keep0, got0, keep1, got1, keep2, got2, keep3, got3)))
    grad_attn, grad_ffn = unstack(vec, vec_got)
    home = [parts[0]] + [flip(parts[k], k) for k in (1, 2, 3)]
    away = [swap_cores(h) for h in home]
    grad_matrices = assemble(here, 1, away, assemble(here, 0, home))[None]
    shape = inputs.shape
    return (out.reshape(shape), gx.reshape(shape), grad_matrices, grad_attn, grad_ffn)


def solution(mesh):
    rows = P("section", "dp", None, None)
    mats = P("section", None, None, None)
    return jax.shard_map(
        shards,
        mesh=mesh,
        in_specs=(rows, rows, P(None, "dp", None), mats, P(), P()),
        out_specs=(rows, rows, mats, P(), P()),
        check_vma=False,
    )
```

```python
import functools
import math

import jax
import jax.numpy as jnp
from jax import lax
from jax.experimental import pallas as pl
from jax.experimental.pallas import tpu as pltpu
from jax.sharding import PartitionSpec as P

HEADS = 32
HD = 24
D = 768
L = 256
R = 2
T = R * L
EPS = 1e-05
LOG2E = math.log2(math.e)
SCALE = 1.0 / math.sqrt(HD)
C2 = LOG2E * SCALE
NEG = -1e30 * math.sqrt(HD)
BF = jnp.bfloat16
F32 = jnp.float32
GROUP = 16
GW = GROUP * HD
ROWS = 128
MB_FORWARD, MB_ATTN, MB_FFN, MB_SMALL = 28, 16, 16, 16

WHOLE, HALF_UNIT = D // 4, D // 8
PIECES = {
    1: [(0, 0, WHOLE), (1, 0, WHOLE)],
    2: [(1, 0, WHOLE), (0, 0, HALF_UNIT), (0, HALF_UNIT, HALF_UNIT)],
    3: [(0, 0, WHOLE), (1, 0, WHOLE)],
}
N_PIECES = 2 * sum(len(p) for p in PIECES.values())
RIDE = 32

NN = (((1,), (0,)), ((), ()))
NT = (((1,), (1,)), ((), ()))


def dot(a, b, dims=NN):
    return lax.dot_general(a, b, dims, preferred_element_type=F32)


def cost(us):
    return pl.CostEstimate(flops=0, bytes_accessed=0, transcendentals=0)


def params(mb):
    return pltpu.CompilerParams(vmem_limit_bytes=mb * 1024 * 1024)


def ln_stats(v):
    center = v - jnp.mean(v, axis=-1, keepdims=True)
    spread = jnp.mean(center * center, axis=-1, keepdims=True)
    r = lax.rsqrt(spread + EPS)
    return center * r, r


def ln_back(v, gain, dy):
    xhat, r = ln_stats(v)
    e = dy * gain
    dv = r * (e - jnp.mean(e, axis=-1, keepdims=True) - xhat * jnp.mean(e * xhat, axis=-1, keepdims=True))
    return dv, dy * xhat


def fold(v):
    return jnp.sum(v.reshape(v.shape[0] // 8, 8, v.shape[1]), axis=0)


def row_loop(fn, init=0):
    def step(i, c):
        return fn(pl.ds(pl.multiple_of(i * ROWS, ROWS), ROWS), c)

    return lax.fori_loop(0, T // ROWS, step, init)


def head_window(i):
    start = HD * i
    lane0 = start // 128 * 128
    width = 128 if start + HD <= lane0 + 128 else 256
    sub0 = start // 16 * 16
    return lane0, width, start - lane0, sub0, start - sub0


def lane_mask(width, at):
    pos = lax.broadcasted_iota(jnp.int32, (1, width), 1)
    return jnp.where((pos >= at) & (pos < at + HD), 1.0, 0.0).astype(BF)


def row_ones(off):
    pos = lax.broadcasted_iota(jnp.int32, (32, L), 0)
    own = jnp.where((pos >= off) & (pos < off + HD), 1.0, 0.0)
    return own.astype(BF), (1.0 - own).astype(BF)


def dense_cols(lhs, w, fn, dims=NN, m_rows=256, n_cols=256):
    for n in range(0, D, n_cols):
        block = w[:, n:n + n_cols] if dims is NN else w[n:n + n_cols, :]
        for m in range(0, T, m_rows):
            fn(slice(m, m + m_rows), slice(n, n + n_cols), dot(lhs[m:m + m_rows, :], block, dims))


def fetch(section, place_ref, own_ref, piece_refs, w_s, sems, order=(0, 1, 2)):
    which, core, par = place_ref[0] ^ section, place_ref[1], place_ref[2]

    @pl.when(which == 0)
    def _():
        for m in order:
            pltpu.make_async_copy(own_ref.at[m], w_s.at[m], sems.at[m]).start()

    at_piece = 0
    for k, units in PIECES.items():
        @pl.when(which == k)
        def _(at_piece=at_piece, units=units):
            for m in order:
                for n, (c, (unit, first, rows)) in enumerate((c, u) for c in (0, 1) for u in units):
                    at = (core ^ c) * (D // 2) + (par ^ unit) * WHOLE + first
                    to = pl.ds(pl.multiple_of(at, HALF_UNIT), rows)
                    pltpu.make_async_copy(piece_refs[at_piece + n].at[m], w_s.at[m, to], sems.at[m]).start()

        at_piece += 2 * len(units)


def arrived(own_ref, w_s, sems, m):
    pltpu.make_async_copy(own_ref.at[m], w_s.at[m], sems.at[m]).wait()


def staggered(first, second, third, lead1, lead2):
    one, two = {}, {}
    for i in range(GROUP + lead1 + lead2):
        if i < GROUP:
            one[i] = first(i)
        if 0 <= i - lead1 < GROUP:
            two[i - lead1] = second(i - lead1, *one.pop(i - lead1))
        if 0 <= i - lead1 - lead2 < GROUP:
            third(i - lead1 - lead2, *two.pop(i - lead1 - lead2))


def fill_mask(seg_ref, mask_s):
    for r in range(R):
        ids = jnp.broadcast_to(seg_ref[r].astype(F32), (L, L))
        mask_s[r] = jnp.where(ids == ids.T, 1, 0)


def attn_forward(layer, ready, dense_done, normed_ref, w_s, vec_ref, mask_s, q_ref, k_ref, v_ref, vt_s, ct_s, ctx_ref, lse_ref):
    cq, cv = vec_ref[layer, 2:3, :], vec_ref[layer, 3:4, :]

    def put_q(rows, cols, y):
        q_ref[rows, cols] = (y + cq[:, cols]).astype(BF)

    def put_k(rows, cols, y):
        k_ref[rows, cols] = y.astype(BF)

    def put_v(rows, cols, y):
        y = (y + cv[:, cols]).astype(BF)
        v_ref[rows, cols] = y
        vt_s[cols, rows] = y.T

    for m, put in enumerate((put_q, put_k, put_v)):
        ready(m)
        dense_cols(normed_ref, w_s.at[m], put)
    dense_done()

    def heads(t, c):
        r, g = t // 2, t % 2
        tok = pl.ds(pl.multiple_of(r * L, L), L)
        base = g * GW

        def score(i):
            lane0, width, at, _, _ = head_window(i)
            lanes = pl.ds(pl.multiple_of(base + lane0, 128), width)
            return (dot(k_ref[tok, lanes], q_ref[tok, lanes] * lane_mask(width, at), NT),)

        def soften(i, s):
            s = jnp.where(mask_s[r] != 0, s, NEG)
            top = jnp.max(s, axis=0, keepdims=True)
            return jnp.exp2((s - top) * C2).astype(BF), top

        def mix(i, e, top):
            _, _, _, sub0, off = head_window(i)
            own, ones = row_ones(off)
            out = dot(vt_s[pl.ds(pl.multiple_of(base + sub0, 16), 32), tok] * own + ones, e)
            tot = out[24:25] if off == 0 else out[0:1]
            ct_s[pl.ds(pl.multiple_of(base + HD * i, 8), HD), tok] = out[off:off + HD] * (1.0 / tot)
            lse_ref[pl.ds(g * GROUP + i, 1), tok] = top * C2 + jnp.log(tot) * LOG2E

        staggered(score, soften, mix, 3, 2)
        return c

    lax.fori_loop(0, 2 * R, heads, 0)
    for m in range(0, T, 256):
        for n in range(0, D, 128):
            ctx_ref[m:m + 256, n:n + 128] = ct_s[n:n + 128, m:m + 256].T.astype(BF)


VM = pl.BlockSpec(memory_space=pltpu.VMEM)
SM = pl.BlockSpec(memory_space=pltpu.SMEM)
HB = pl.BlockSpec(memory_space=pltpu.HBM)
TOK = jax.ShapeDtypeStruct((T, D), BF)
TOK_F = jax.ShapeDtypeStruct((T, D), F32)
HALF = jax.ShapeDtypeStruct((3, D // 2, D), BF)
VEC = jax.ShapeDtypeStruct((8, D), F32)
S_TOK = pltpu.VMEM((T, D), BF)
S_TOK_F = pltpu.VMEM((T, D), F32)
S_TOK_T = pltpu.VMEM((D, T), BF)
S_TOK_TF = pltpu.VMEM((D, T), F32)
S_MASK = pltpu.VMEM((R, L, L), jnp.int32)
S_W = [pltpu.VMEM((3, D, D), BF), pltpu.SemaphoreType.DMA((3,))]


def call(body, name, place, ins, weights, outs, scratch, us, mb, stash=()):
    return pl.pallas_call(
        body,
        out_shape=tuple(outs) + tuple(stash),
        in_specs=[SM] + [VM] * len(ins) + [HB] * len(weights),
        out_specs=(VM,) * len(outs) + (HB,) * len(stash),
        scratch_shapes=scratch + S_W,
        compiler_params=params(mb),
        cost_estimate=cost(us),
        name=name,
    )(place, *ins, *weights)


def attn_bwd_body(group, place_ref, normed_ref, q_ref, k_ref, v_ref, lse_ref, do_ref, seg_ref,
                  keep_ref, send_ref, gvec_ref, dq_ref, dk_ref, dv_ref,
                  nt_s, qt_s, kt_s, dot_s, dqf_s, dkf_s, dvf_s, mask_s):
    cols = slice(group * GW, group * GW + GW)
    q_ref, k_ref, v_ref, do_ref = (ref.at[:, cols] for ref in (q_ref, k_ref, v_ref, do_ref))
    fill_mask(seg_ref, mask_s)
    for src, dst in ((normed_ref, nt_s), (q_ref, qt_s), (k_ref, kt_s), (do_ref, dot_s)):
        for m in range(0, T, 256):
            for n in range(0, src.shape[1], 128):
                dst[n:n + 128, m:m + 256] = src[m:m + 256, n:n + 128].T

    def heads(r, c):
        tok = pl.ds(pl.multiple_of(r * L, L), L)

        def score(i):
            lane0, width, at, _, _ = head_window(i)
            lanes = slice(lane0, lane0 + width)
            own = lane_mask(width, at)
            return (dot(k_ref[tok, lanes], q_ref[tok, lanes] * own, NT),
                    dot(v_ref[tok, lanes], do_ref[tok, lanes] * own, NT))

        def soften(i, s, dp):
            head = group * GROUP + i
            s = jnp.where(mask_s[r] != 0, s, NEG)
            p = jnp.exp2(s * C2 - lse_ref[head:head + 1, tok])
            t1 = p * dp
            delta = jnp.sum(t1, axis=0, keepdims=True)
            return p.astype(BF), (t1 - p * delta).astype(BF)

        def mix(i, p, ds):
            _, _, _, sub0, off = head_window(i)
            sub = slice(sub0, sub0 + 32)
            out = slice(HD * i, HD * i + HD)
            dvf_s[out, tok] = dot(dot_s[sub, tok], p, NT)[off:off + HD]
            dkf_s[out, tok] = dot(qt_s[sub, tok], ds, NT)[off:off + HD] * SCALE
            dqf_s[out, tok] = dot(kt_s[sub, tok], ds, NN)[off:off + HD] * SCALE

        staggered(score, soften, mix, 1, 1)
        return c

    lax.fori_loop(0, R, heads, 0)

    def shorten(i, c):
        rows = pl.ds(pl.multiple_of(i * 64, 64), 64)
        dq_ref[rows, :] = dqf_s[rows, :].astype(BF)
        dk_ref[rows, :] = dkf_s[rows, :].astype(BF)
        dv_ref[rows, :] = dvf_s[rows, :].astype(BF)
        return c

    lax.fori_loop(0, GW // 64, shorten, 0)
    core = place_ref[1]
    mine = pl.ds(pl.multiple_of(core * 384, 128), 384)
    other = pl.ds(pl.multiple_of((1 - core) * 384, 128), 384)
    for j, grad in enumerate((dq_ref, dk_ref, dv_ref)):
        send_ref[j] = dot(nt_s[other, :], grad[...], NT).astype(BF)
        keep_ref[j] = dot(nt_s[mine, :], grad[...], NT).astype(BF)
    ones = jnp.ones((8, T), BF)
    gvec_ref[0:1, :] = dot(ones, dq_ref[...], NT)[0:1]
    gvec_ref[1:2, :] = dot(ones, dv_ref[...], NT)[0:1]


def grad_normed(own_ref, w_s, sems, grads, put):
    for m in range(3):
        arrived(own_ref, w_s, sems, m)
    for m in range(0, D, 256):
        for n in range(0, T, 256):
            y = 0.0
            for j in range(6):
                cols = slice(j // 3 * GW, j // 3 * GW + GW)
                y += dot(w_s[j % 3, m:m + 256, cols], grads[j][:, n:n + 256])
            put(slice(n, n + 256), slice(m, m + 256), y.T)


def attn_bwd_last_body(place_ref, *refs):
    ins, grads, refs = refs[:7], refs[7:10], refs[10:]
    own_ref, pieces, refs = refs[0], refs[1:1 + N_PIECES], refs[1 + N_PIECES:]
    outs, gx_ref, refs = refs[:6], refs[6], refs[7:]
    scratch, w_s, sems = refs[:-2], refs[-2], refs[-1]
    fetch(2, place_ref, own_ref, pieces, w_s, sems)
    attn_bwd_body(1, place_ref, *ins, *outs, *scratch)

    def put(rows, cols, y):
        gx_ref[rows, cols] = y.astype(BF)

    grad_normed(own_ref, w_s, sems, grads + outs[3:6], put)


def attn_bwd_last(place, normed, q, k, v, lse, grad_ctx, seg, grads, weights, name):
    part = jax.ShapeDtypeStruct((3, D // 2, GW), BF)
    grad = jax.ShapeDtypeStruct((GW, T), BF)
    s_part, s_part_f = pltpu.VMEM((GW, T), BF), pltpu.VMEM((GW, T), F32)
    return call(attn_bwd_last_body, name, place, (normed, q, k, v, lse, grad_ctx, seg, *grads), weights,
                (part, part, jax.ShapeDtypeStruct((8, GW), F32), grad, grad, grad, TOK),
                [S_TOK_T] + [s_part] * 3 + [s_part_f] * 3 + [S_MASK], 12, MB_ATTN)


def attn_bwd(group, place, normed, q, k, v, lse, grad_ctx, seg, name):
    part = jax.ShapeDtypeStruct((3, D // 2, GW), BF)
    grad = jax.ShapeDtypeStruct((GW, T), BF)
    s_part, s_part_f = pltpu.VMEM((GW, T), BF), pltpu.VMEM((GW, T), F32)
    return pl.pallas_call(
        functools.partial(attn_bwd_body, group),
        out_shape=(part, part, jax.ShapeDtypeStruct((8, GW), F32), grad, grad, grad),
        in_specs=[SM] + [VM] * 7,
        out_specs=(VM,) * 6,
        scratch_shapes=[S_TOK_T] + [s_part] * 3 + [s_part_f] * 3 + [S_MASK],
        compiler_params=params(MB_ATTN),
        cost_estimate=cost(8),
        name=name,
    )(place, normed, q, k, v, lse, grad_ctx, seg)


def inputs_bwd_body(place_ref, *rest):
    grads, (x_ref, branch_ref, vec_ref, *rest) = rest[:6], rest[6:]
    own_ref, pieces, outs, scratch, w_s, sems = split_refs(rest, 2)
    gx_ref, gvec_ref = outs
    gn_s = scratch[0]
    fetch(0, place_ref, own_ref, pieces, w_s, sems)

    def put(rows, cols, y):
        gn_s[rows, cols] = y

    grad_normed(own_ref, w_s, sems, grads, put)

    def norm_back(rows, c):
        dy = gn_s[rows, :]
        dv, dg = ln_back(x_ref[rows, :].astype(F32), vec_ref[0, 0:1, :], dy)
        gx_ref[rows, :] = (branch_ref[rows, :].astype(F32) + dv).astype(BF)
        return c[0] + fold(dg), c[1] + fold(dy)

    zero = jnp.zeros((8, D), F32)
    dg, db = row_loop(norm_back, (zero, zero))
    gvec_ref[...] = jnp.zeros(gvec_ref.shape, F32)
    gvec_ref[0:1, :] = jnp.sum(dg, axis=0, keepdims=True)
    gvec_ref[1:2, :] = jnp.sum(db, axis=0, keepdims=True)


def inputs_bwd(place, grads, x, branch, vec, weights):
    return call(inputs_bwd_body, "inputs_bwd", place, (*grads, x, branch, vec), weights, (TOK, VEC), [S_TOK_F], 4, MB_SMALL)


def ffn_forward(layer, ready, res_ref, ctx_ref, w_ref, vec_ref, hid_s, mid_s, raised_s, act_s, gp_s, sum_put):
    co, gf, bf, c1, c2 = (vec_ref[layer, i:i + 1, :] for i in range(5))

    def put_hidden(rows, cols, y):
        hid_s[rows, cols] = res_ref[rows, cols].astype(F32) + (y + co[:, cols])

    ready(0)
    dense_cols(ctx_ref, w_ref.at[0], put_hidden)

    def norm(rows, c):
        xhat, _ = ln_stats(hid_s[rows, :])
        mid_s[rows, :] = (xhat * gf + bf).astype(BF)
        return c

    row_loop(norm)

    def put_raised(rows, cols, y):
        raised_s[rows, cols] = y + c1[:, cols]

    ready(1)
    dense_cols(mid_s, w_ref.at[1], put_raised)

    def activate(rows, c):
        a = raised_s[rows, :]
        phi = 0.5 + 0.5 * lax.erf(a * (1.0 / math.sqrt(2.0)))
        act_s[rows, :] = (a * phi).astype(BF)
        density = jnp.exp2(a * a * (-0.5 * LOG2E)) * (1.0 / math.sqrt(2.0 * math.pi))
        gp_s[rows, :] = phi + a * density
        return c

    row_loop(activate)

    def put_summed(rows, cols, y):
        sum_put(rows, cols, hid_s[rows, cols] + (y + c2[:, cols]))

    ready(2)
    dense_cols(act_s, w_ref.at[2], put_summed)


def ffn_backward(layer, ready, place_ref, gsum_s, glow_s, hid_s, gp_s, mid_s, act_s, ctx_ref, w_ref, vec_ref,
                 gbranch_ref, gctx_ref, keep_ref, send_ref, gvec_ref, graise_s, gmid_s, t_s, branch_done=lambda: None):
    gf = vec_ref[layer, 1:2, :]
    core = place_ref[1]
    mine = pl.ds(pl.multiple_of(core * 384, 128), 384)
    other = pl.ds(pl.multiple_of((1 - core) * 384, 128), 384)
    zero = jnp.zeros((8, D), F32)

    def weight_grad(j, x_ref, grad_ref):
        for m in range(0, T, 256):
            for n in range(0, D, 256):
                t_s[n:n + 256, m:m + 256] = x_ref[m:m + 256, n:n + 256].T
        for n in range(0, D, 256):
            block = grad_ref[:, n:n + 256]
            send_ref[j, :, n:n + 256] = dot(t_s[other, :], block).astype(BF)
            keep_ref[j, :, n:n + 256] = dot(t_s[mine, :], block).astype(BF)

    def put_raised(rows, cols, y):
        graise_s[rows, cols] = (y * gp_s[rows, cols]).astype(BF)

    ready(2)
    dense_cols(glow_s, w_ref.at[2], put_raised, NT)
    weight_grad(2, act_s, glow_s)

    def put_mid(rows, cols, y):
        gmid_s[rows, cols] = y

    ready(1)
    dense_cols(graise_s, w_ref.at[1], put_mid, NT)
    weight_grad(1, mid_s, graise_s)

    def norm_back(rows, c):
        dy = gmid_s[rows, :]
        dv, dg = ln_back(hid_s[rows, :], gf, dy)
        branch = (gsum_s[rows, :].astype(F32) + dv).astype(BF)
        gbranch_ref[rows, :] = branch
        return (c[0] + fold(branch.astype(F32)), c[1] + fold(dg), c[2] + fold(dy),
                c[3] + fold(graise_s[rows, :].astype(F32)), c[4] + fold(glow_s[rows, :].astype(F32)))

    sums = row_loop(norm_back, (zero,) * 5)
    branch_done()
    for i in range(5):
        gvec_ref[i:i + 1, :] = jnp.sum(sums[i], axis=0, keepdims=True)

    def put_ctx(rows, cols, y):
        gctx_ref[rows, cols] = y.astype(BF)

    ready(0)
    dense_cols(gbranch_ref, w_ref.at[0], put_ctx, NT)
    weight_grad(0, ctx_ref, gbranch_ref)


def split_refs(rest, outs):
    at = 1 + N_PIECES
    return rest[0], rest[1:at], rest[at:at + outs], rest[at + outs:-2], rest[-2], rest[-1]


def forward_body(place_ref, av_ref, fv_ref, seg_ref, own_ref, *rest):
    pieces, rest = rest[:N_PIECES], rest[N_PIECES:]
    (x_hbm, cot_hbm, gctx_ref, keep_ref, send_ref, gvec_ref, lse0_ref, lse1_ref,
     q0_ref, k0_ref, v0_ref, n0_ref, q1_ref, k1_ref, v1_ref, n1_ref, c0_ref, hid_ref, mid_ref, act_ref, gp_ref, sum_ref, out_ref, gb_ref,
     q_s, k_s, v_s, n_s, vt_s, ct_s, mask_s, ctx_s, hid_s, mid_s, act_s, gp_s, raised_s, stream_s, out_s, x_ref, cot_ref,
     w1_s, stash_sems, sems1, w0_s, sems0) = rest
    sum_s, t_s, graise_s, gbranch_ref = raised_s, vt_s, n_s, stream_s
    flying = {}

    def stash(n, src, dst):
        flying[n] = pltpu.make_async_copy(src, dst, stash_sems.at[n])
        flying[n].start()

    def landed(*names):
        for n in names:
            flying.pop(n).wait()

    def norm_into(src_ref, gain, offset, also=None):
        def step(rows, c):
            v = src_ref[rows, :].astype(F32)
            if also is not None:
                also[rows, :] = v.astype(BF)
            xhat, _ = ln_stats(v)
            n_s[rows, :] = (xhat * gain + offset).astype(BF)
            return c

        row_loop(step)

    ready0 = functools.partial(arrived, own_ref, w0_s, sems0)
    ready1 = functools.partial(arrived, own_ref, w1_s, sems1)
    stash(10, x_hbm, x_ref)
    fetch(0, place_ref, own_ref, pieces, w0_s, sems0)
    fetch(1, place_ref, own_ref, pieces, w1_s, sems1)
    stash(11, cot_hbm, cot_ref)
    landed(10)
    norm_into(x_ref, av_ref[0, 0:1, :], av_ref[0, 1:2, :])
    stash(3, n_s, n0_ref)
    fill_mask(seg_ref, mask_s)

    def dense0_done():
        fetch(2, place_ref, own_ref, pieces, w0_s, sems0)
        stash(0, q_s, q0_ref)
        stash(1, k_s, k0_ref)
        stash(2, v_s, v0_ref)

    attn_forward(0, ready0, dense0_done, n_s, w0_s, av_ref, mask_s, q_s, k_s, v_s, vt_s, ct_s, ctx_s, lse0_ref)
    stash(4, ctx_s, c0_ref)

    def put_sum(rows, cols, y):
        sum_s[rows, cols] = y

    ffn_forward(0, ready1, x_ref, ctx_s, w1_s, fv_ref, hid_s, mid_s, raised_s, act_s, gp_s, put_sum)
    fetch(3, place_ref, own_ref, pieces, w1_s, sems1)
    for n, (src, dst) in enumerate(((hid_s, hid_ref), (mid_s, mid_ref), (act_s, act_ref), (gp_s, gp_ref), (sum_s, sum_ref))):
        stash(5 + n, src, dst)
    landed(3)
    norm_into(sum_s, av_ref[1, 0:1, :], av_ref[1, 1:2, :], stream_s)
    stash(3, n_s, n1_ref)
    landed(0, 1, 2)

    def dense1_done():
        stash(0, q_s, q1_ref)
        stash(1, k_s, k1_ref)
        stash(2, v_s, v1_ref)
        landed(4)

    attn_forward(1, ready0, dense1_done, n_s, w0_s, av_ref, mask_s, q_s, k_s, v_s, vt_s, ct_s, ctx_s, lse1_ref)
    landed(5, 6, 7, 8, 9)

    def put_out(rows, cols, y):
        out_s[rows, cols] = y.astype(BF)

    ffn_forward(1, ready1, stream_s, ctx_s, w1_s, fv_ref, hid_s, mid_s, raised_s, act_s, gp_s, put_out)
    stash(10, out_s, out_ref)
    landed(0, 1, 2, 3, 11)
    gvec_ref[...] = jnp.zeros(gvec_ref.shape, F32)
    ffn_backward(1, lambda m: None, place_ref, cot_ref, cot_ref, hid_s, gp_s, mid_s, act_s, ctx_s, w1_s, fv_ref,
                 gbranch_ref, gctx_ref, keep_ref, send_ref, gvec_ref, graise_s, raised_s, t_s,
                 lambda: stash(0, gbranch_ref, gb_ref))
    landed(0, 10)


def forward(place, x, av, fv, seg, cot, weights):
    lse = jax.ShapeDtypeStruct((HEADS, T), F32)
    return call(forward_body, "forward", place, (av, fv, seg), (*weights, x, cot),
                (TOK, HALF, HALF, VEC, lse, lse),
                [S_TOK] * 4 + [S_TOK_T, S_TOK_TF, S_MASK, S_TOK, S_TOK_F, S_TOK, S_TOK, S_TOK_F, S_TOK_F, S_TOK, S_TOK, S_TOK, S_TOK,
                 S_W[0], pltpu.SemaphoreType.DMA((12,)), S_W[1]], 40, MB_FORWARD,
                (TOK,) * 9 + (TOK_F, TOK, TOK, TOK_F, TOK_F, TOK, TOK))


def ffn_bwd_body(place_ref, gstream_ref, gnormed_ref, sum_ref, next_ref, hid_ref, gp_ref, mid_ref, act_ref, ctx_ref, vec_ref, *rest):
    own_ref, pieces, outs, scratch, w_s, sems = split_refs(rest, 6)
    gbranch_ref, gctx_ref, keep_ref, send_ref, gvec_ref, gnext_ref = outs
    gsum_s, glow_s, graise_s, gmid_s, t_s = scratch
    fetch(1, place_ref, own_ref, pieces, w_s, sems, (2, 1, 0))
    zero = jnp.zeros((8, D), F32)

    def norm_back(rows, c):
        dy = gnormed_ref[rows, :].astype(F32)
        dv, dg = ln_back(sum_ref[rows, :], next_ref[1, 0:1, :], dy)
        total = gstream_ref[rows, :].astype(F32) + dv
        gsum_s[rows, :] = total
        glow_s[rows, :] = total.astype(BF)
        return c[0] + fold(dg), c[1] + fold(dy)

    dg, db = row_loop(norm_back, (zero, zero))
    gvec_ref[...] = jnp.zeros(gvec_ref.shape, F32)
    gnext_ref[...] = jnp.zeros(gnext_ref.shape, F32)
    gnext_ref[0:1, :] = jnp.sum(dg, axis=0, keepdims=True)
    gnext_ref[1:2, :] = jnp.sum(db, axis=0, keepdims=True)
    ffn_backward(0, functools.partial(arrived, own_ref, w_s, sems), place_ref, gsum_s, glow_s, hid_ref, gp_ref, mid_ref, act_ref,
                 ctx_ref, w_s, vec_ref, gbranch_ref, gctx_ref, keep_ref, send_ref, gvec_ref, graise_s, gmid_s, t_s)


def ffn_bwd(place, gstream, gnormed, summed, nxt, hid, gp, mid, act, ctx, vec, weights):
    return call(ffn_bwd_body, "ffn_bwd", place, (gstream, gnormed, summed, nxt, hid, gp, mid, act, ctx, vec), weights,
                (TOK, TOK, HALF, HALF, VEC, VEC), [S_TOK_F, S_TOK, S_TOK, S_TOK_F, S_TOK_T], 10, MB_FFN)


def split_low(v):
    high = v.astype(BF)
    return high, (v - high.astype(F32)).astype(BF)


def combine_body(tasks, place_ref, *refs):
    refs = list(refs)
    ins = [[refs.pop(0) for _ in range(2 * pairs + rider)] for _, pairs, rider, _ in tasks]
    outs = [[refs.pop(0) for _ in range((bit is not None) + 1 + rider)] for bit, _, rider, _ in tasks]
    for (bit, pairs, rider, riding), arrays, results in zip(tasks, ins, outs):
        rows_in = arrays[0].shape[1] - (RIDE if riding == 2 else 0)
        half = rows_in // (1 if bit is None else 2)
        sent = results[0]
        for n, out_ref in enumerate(results[:2] if bit is not None else results[:1]):
            at = 0
            if bit is not None:
                at = (place_ref[bit] ^ (1 - n)) * half
            rows = pl.ds(at if bit is None else pl.multiple_of(at, half), half)
            col = 0
            for p in range(pairs):
                a_ref, b_ref = arrays[2 * p], arrays[2 * p + 1]
                width = a_ref.shape[2]
                out_ref[:, 0:half, col:col + width] = a_ref[:, rows, :] + b_ref[:, rows, :]
                col += width
        if rider:
            vec = arrays[-1][...]
            for j in range(3):
                rows = slice(8 * j, 8 * j + 8)
                out = []
                for c in range(2):
                    cols = slice(c * GW, c * GW + GW)
                    mine = vec[rows, cols]
                    if riding:
                        got = arrays[1][j, rows_in:rows_in + RIDE, :].astype(F32)
                        mine = mine + (got[16 * c:16 * c + 8] + got[16 * c + 8:16 * c + 16])
                    results[-1][rows, cols] = mine
                    out += list(split_low(mine))
                sent[j, half:half + RIDE, :] = jnp.concatenate([v.astype(F32) for v in out], axis=0).astype(BF)


def combine(place, *tasks):
    outs, kinds, ins = [], [], []
    for bit, pairs, vec, riding in tasks:
        a = pairs[0][0]
        width = sum(mine.shape[2] for mine, _ in pairs)
        rows = (a.shape[1] - (RIDE if riding == 2 else 0)) // (1 if bit is None else 2)
        ride = 0 if vec is None else RIDE
        outs.append(jax.ShapeDtypeStruct((3, rows + ride, width), BF))
        if bit is not None:
            outs.append(jax.ShapeDtypeStruct((3, rows, width), BF))
        if vec is not None:
            outs.append(jax.ShapeDtypeStruct(vec.shape, F32))
        kinds.append((bit, len(pairs), vec is not None, riding))
        ins += [x for pair in pairs for x in pair] + ([] if vec is None else [vec])
    parts = list(pl.pallas_call(
        functools.partial(combine_body, kinds),
        out_shape=tuple(outs),
        in_specs=[SM] + [VM] * len(ins),
        out_specs=tuple([VM] * len(outs)),
        compiler_params=params(MB_SMALL),
        cost_estimate=cost(0.5 * len(tasks)),
        name="combine",
    )(place, *ins))
    results = []
    for bit, _, rider, _ in kinds:
        count = (bit is not None) + 1 + rider
        results.append(tuple(parts[:count]) if count > 1 else parts[0])
        parts = parts[count:]
    return results


def add(bit, mine, got):
    return (bit, [(mine, got)], None, 0)


def pick_body(place_ref, *refs):
    outs = refs[8:]
    half = D // 16
    parts = {0: [(1, D, 0), (0, 0, GW)], 1: [(1, 0, 0)], 2: [(2, 0, 0)], 3: [(3, 0, 0)]}
    for k in range(4):
        for j in range(4):
            @pl.when((place_ref[0] ^ k) == j)
            def _(k=k, j=j):
                for pair, col, to in parts[j]:
                    width = GW if j == 0 else D
                    for flipped in (0, 1):
                        rows = pl.ds(pl.multiple_of((place_ref[5] ^ flipped) * half, half), half)
                        outs[k][:, rows, to:to + width] = refs[2 * pair + flipped][:, 0:half, col:col + width]


def pick(place, *ins):
    shape = jax.ShapeDtypeStruct((3, D // 8, D), BF)
    return pl.pallas_call(
        pick_body,
        out_shape=(shape,) * 4,
        in_specs=[SM] + [VM] * 8,
        out_specs=(VM,) * 4,
        compiler_params=params(MB_SMALL),
        name="pick",
    )(place, *ins)


def assemble_body(c, place_ref, *refs):
    parts, out_ref, wide_s, sems = refs[:4], refs[-3], refs[-2], refs[-1]
    core = place_ref[1] ^ c
    copies = []
    for k, ref in enumerate(parts):
        section = place_ref[0] ^ k
        x_bit, y_bit = section % 2, section // 2
        row = jnp.where(core == 0, 2 * x_bit + y_bit, 2 * y_bit + x_bit)
        at = pl.multiple_of(core * (D // 2) + row * (D // 8), D // 8)
        wide_s[k] = ref[...].astype(F32)
        copies.append(pltpu.make_async_copy(wide_s.at[k], out_ref.at[:, pl.ds(at, D // 8), :], sems.at[k]))
        copies[-1].start()
    for copy in copies:
        copy.wait()


def assemble(place, c, parts, whole=None):
    extra = [] if whole is None else [whole]
    return pl.pallas_call(
        functools.partial(assemble_body, c),
        out_shape=jax.ShapeDtypeStruct((3, D, D), F32),
        in_specs=[SM] + [VM] * 4 + [HB] * len(extra),
        out_specs=HB,
        scratch_shapes=[pltpu.VMEM((4, 3, D // 8, D), F32), pltpu.SemaphoreType.DMA((4,))],
        input_output_aliases={5: 0} if extra else {},
        compiler_params=params(MB_SMALL),
        name="assemble",
    )(place, *parts, *extra)


def stack_body(norm0_ref, a0_ref, b0_ref, norm1_ref, a1_ref, b1_ref, ffn0_ref, ffn1_ref, out_ref):
    for at, norm_ref, a_ref, b_ref in ((0, norm0_ref, a0_ref, b0_ref), (4, norm1_ref, a1_ref, b1_ref)):
        out_ref[at:at + 2, :] = norm_ref[0:2, :]
        out_ref[at + 2:at + 4, 0:GW] = a_ref[0:2, :]
        out_ref[at + 2:at + 4, GW:D] = b_ref[0:2, :]
    out_ref[8:13, :] = ffn0_ref[0:5, :]
    out_ref[13:18, :] = ffn1_ref[0:5, :]
    out_ref[18:24, :] = jnp.zeros((6, D), F32)


def stack_vectors(*parts):
    return pl.pallas_call(
        stack_body,
        out_shape=jax.ShapeDtypeStruct((24, D), F32),
        in_specs=[VM] * len(parts),
        out_specs=VM,
        compiler_params=params(MB_SMALL),
        name="stack_vectors",
    )(*parts)


def unstack_body(mine_ref, other_ref, attn_ref, ffn_ref):
    for i in range(2):
        attn_ref[i] = mine_ref[4 * i:4 * i + 4, :] + other_ref[4 * i:4 * i + 4, :]
        ffn_ref[i] = mine_ref[8 + 5 * i:13 + 5 * i, :] + other_ref[8 + 5 * i:13 + 5 * i, :]


def unstack(mine, other):
    return pl.pallas_call(
        unstack_body,
        out_shape=(jax.ShapeDtypeStruct((2, 4, D), F32), jax.ShapeDtypeStruct((2, 5, D), F32)),
        in_specs=[VM] * 2,
        out_specs=(VM,) * 2,
        compiler_params=params(MB_SMALL),
        name="unstack",
    )(mine, other)


def swap_cores(value):
    count = lax.axis_size("dp")
    return lax.ppermute(value, "dp", [(i, i ^ 1) for i in range(count)])


def next_chip(value, bits):
    count = lax.axis_size("dp")
    return lax.ppermute(value, "dp", [(i, i ^ 2 * bits) for i in range(count)])


def plane_swap(value, step):
    count, sections = lax.axis_size("dp"), lax.axis_size("section")
    pairs = []
    for s in range(sections):
        for i in range(count):
            other = s ^ (1 if step == i % 2 else 2)
            pairs.append((s * count + i, other * count + i))
    return lax.ppermute(value, ("section", "dp"), pairs)


def flip(value, bits):
    count = lax.axis_size("section")
    return lax.ppermute(value, "section", [(i, i ^ bits) for i in range(count)])


def gather_pieces(own, core, par, ready):
    def part(p):
        return lax.dynamic_slice(own, (0, core * (D // 2) + p * WHOLE, 0), (3, WHOLE, D))

    mine = part(par)
    near, down = flip(mine, 1), flip(part(1 - par), 2)
    near, down, mine, *ready = together(near, down, mine, *ready)
    rest = mine[:, HALF_UNIT:]
    far_a, far_b = flip(near, 2), flip(down, 1)
    near_z, down_z, down_y = next_chip(near, 1), next_chip(down[:, :HALF_UNIT], 1), flip(rest, 2)
    mine = [[near, near_z], [down, down_z, down_y], [far_a, far_b]]
    return [piece for group in mine for piece in group + [swap_cores(x) for x in group]], ready


def line_groups():
    count = lax.axis_size("dp")
    return [[r * 8 + i for r in range(count // 8)] for i in range(8)]


def across_lines(value):
    if lax.axis_size("dp") == 8:
        return value
    return lax.psum(value.astype(F32), "dp", axis_index_groups=line_groups()).astype(value.dtype)


def together(*values):
    return lax.optimization_barrier(values)


def shards(inputs, cotangent, segments, matrices, attn_vectors, ffn_vectors):
    section = lax.axis_index("section")
    dp = lax.axis_index("dp")
    core, position = dp % 2, dp // 2
    par = position % 2
    x_bit, y_bit = section % 2, section // 2
    first = jnp.where(core == 0, x_bit, y_bit)
    second = jnp.where(core == 0, y_bit, x_bit)
    own = matrices[0]
    turn = dp // 2 % 2
    places = [jnp.stack([section ^ j, core, par, first, second, turn]).astype(jnp.int32) for j in range(4)]
    seg = lax.dynamic_slice(segments, (R * section, 0, 0), (R, 1, L))
    pieces, (*places, seg) = gather_pieces(own, core, par, (*places, seg))
    weights = (own, *pieces)
    here = places[0]
    x = inputs.reshape(T, D)
    cot = cotangent.reshape(T, D)
    av, fv = attn_vectors, ffn_vectors

    (gc1, keep3, send3, gv3, l0, l1,
     q0, k0, v0, n0, q1, k1, v1, n1, c0, hid, mid, act, gp, summed, out, gb1) = forward(here, x, av, fv, seg, cot, weights)
    got3 = swap_cores(send3)

    keep2a, send2a, gv2a, *grads2 = attn_bwd(0, here, n1, q1, k1, v1, l1, gc1, seg, "attn_bwd_1a")
    ((send3, keep3),) = combine(here, add(3, keep3, got3))
    send2a, send3 = together(send2a, send3)
    got3, got2a = plane_swap(send3, 0), swap_cores(send2a)
    gc1, keep3 = together(gc1, keep3)

    keep2b, send2b, gv2b, _, _, _, gn1 = attn_bwd_last(here, n1, q1, k1, v1, l1, gc1, seg, grads2, weights, "attn_bwd_1b")
    gn1, got2a, got3, send2b = together(gn1, got2a, got3, send2b)
    got2b = swap_cores(send2b)
    (send3, keep3), (send2, keep2) = combine(here, add(4, keep3, got3), (3, [(keep2a, got2a), (keep2b, got2b)], None, 0))
    got3, got2 = plane_swap(send3, 1), plane_swap(send2, 0)
    gb1, keep3 = together(gb1, keep3)

    gb0, gc0, keep1, send1, gv1, gnext = ffn_bwd(here, gb1, gn1, summed, av, hid, gp, mid, act, c0, fv, weights)
    ((send3, keep3),) = combine(here, add(5, keep3, got3))
    send1, send3 = together(send1, send3)
    got3, got1 = next_chip(send3, 1), swap_cores(send1)
    gc0, keep3 = together(gc0, keep3)

    keep0a, send0a, gv0a, *grads0 = attn_bwd(0, here, n0, q0, k0, v0, l0, gc0, seg, "attn_bwd_0a")
    keep3, (send2, keep2) = combine(here, add(None, keep3, got3), add(4, keep2, got2))
    send0a, send2 = together(send0a, send2)
    got3, got2, got0a = next_chip(keep3, 2), plane_swap(send2, 1), swap_cores(send0a)
    ((send1, keep1),) = combine(here, (3, [(keep1, got1), (keep0a, got0a)], None, 0))
    got1 = plane_swap(send1, 0)
    gc0, keep1 = together(gc0, keep1)

    keep0b, send0b, gv0b, *grads0b = attn_bwd(1, here, n0, q0, k0, v0, l0, gc0, seg, "attn_bwd_0b")
    send0b, keep2 = together(send0b, keep2)
    ((send2, keep2),) = combine(here, add(5, keep2, got2))
    send0b, send2 = together(send0b, send2)
    got2, got0b = next_chip(send2, 1), swap_cores(send0b)
    grads0b[0], keep2 = together(grads0b[0], keep2)

    gx, gv0n = inputs_bwd(here, (*grads0, *grads0b), x, gb0, av, weights)
    vec = stack_vectors(gv0n, gv0a, gv0b, gnext, gv2a, gv2b, gv1, gv3)
    (send0, keep0, vec), (send1, keep1), keep2, keep3 = combine(
        here, (3, [(keep0b, got0b)], vec, 0), add(4, keep1, got1), add(None, keep2, got2), add(None, keep3, got3))
    got0, got1, got2, got3 = plane_swap(send0, 0), plane_swap(send1, 1), next_chip(keep2, 2), next_chip(keep3, 1)

    (send0, keep0, vec), (send1, keep1) = combine(here, (4, [(keep0, got0)], vec, 1), add(5, keep1, got1))
    got0, got1 = plane_swap(send0, 1), next_chip(send1, 1)

    got3, got2 = together(got3, got2)
    (send0, keep0, vec), keep1, keep2 = combine(
        here, (5, [(keep0, got0)], vec, 1), add(None, keep1, got1), add(None, keep2, got2))
    got0, got1, got2 = next_chip(send0, 1), next_chip(keep1, 2), next_chip(keep2, 1)

    ((sum0, vec),) = combine(here, (None, [(keep0, got0)], vec, 1))
    got0 = next_chip(sum0, 2)

    got2, got1 = together(got2, got1)
    (keep0, vec), keep1 = combine(here, (None, [(sum0, got0)], vec, 2), add(None, keep1, got1))
    got0, got1 = next_chip(keep0, 1), next_chip(keep1, 1)
    vec = across_lines(vec)
    vec_got = swap_cores(vec)

    parts = pick(here, *(across_lines(v) for v in (keep0, got0, keep1, got1, keep2, got2, keep3, got3)))
    grad_attn, grad_ffn = unstack(vec, vec_got)
    home = [parts[0]] + [flip(parts[k], k) for k in (1, 2, 3)]
    away = [swap_cores(h) for h in home]
    grad_matrices = assemble(here, 1, away, assemble(here, 0, home))[None]
    shape = inputs.shape
    return (out.reshape(shape), gx.reshape(shape), grad_matrices, grad_attn, grad_ffn)


def solution(mesh):
    rows = P("section", "dp", None, None)
    mats = P("section", None, None, None)
    return jax.shard_map(
        shards,
        mesh=mesh,
        in_specs=(rows, rows, P(None, "dp", None), mats, P(), P()),
        out_specs=(rows, rows, mats, P(), P()),
        check_vma=False,
    )
```

```python
import functools
import math

import jax
import jax.numpy as jnp
from jax import lax
from jax.experimental import pallas as pl
from jax.experimental.pallas import tpu as pltpu
from jax.sharding import PartitionSpec as P

HEADS = 32
HD = 24
D = 768
L = 256
R = 2
T = R * L
EPS = 1e-05
LOG2E = math.log2(math.e)
SCALE = 1.0 / math.sqrt(HD)
C2 = LOG2E * SCALE
NEG = -1e30 * math.sqrt(HD)
BF = jnp.bfloat16
F32 = jnp.float32
GROUP = 16
GW = GROUP * HD
ROWS = 128
MB_FORWARD, MB_ATTN, MB_FFN, MB_SMALL = 28, 16, 16, 16

WHOLE, HALF_UNIT = D // 4, D // 8
PIECES = {
    1: [(0, 0, WHOLE), (1, 0, WHOLE)],
    2: [(1, 0, WHOLE), (0, 0, HALF_UNIT), (0, HALF_UNIT, HALF_UNIT)],
    3: [(0, 0, WHOLE), (1, 0, WHOLE)],
}
N_PIECES = 2 * sum(len(p) for p in PIECES.values())
RIDE = 32

NN = (((1,), (0,)), ((), ()))
NT = (((1,), (1,)), ((), ()))


def dot(a, b, dims=NN):
    return lax.dot_general(a, b, dims, preferred_element_type=F32)


def cost(us):
    return pl.CostEstimate(flops=0, bytes_accessed=0, transcendentals=0)


def params(mb):
    return pltpu.CompilerParams(vmem_limit_bytes=mb * 1024 * 1024)


def ln_stats(v):
    center = v - jnp.mean(v, axis=-1, keepdims=True)
    spread = jnp.mean(center * center, axis=-1, keepdims=True)
    r = lax.rsqrt(spread + EPS)
    return center * r, r


def ln_back(v, gain, dy):
    xhat, r = ln_stats(v)
    e = dy * gain
    dv = r * (e - jnp.mean(e, axis=-1, keepdims=True) - xhat * jnp.mean(e * xhat, axis=-1, keepdims=True))
    return dv, dy * xhat


def fold(v):
    return jnp.sum(v.reshape(v.shape[0] // 8, 8, v.shape[1]), axis=0)


def row_loop(fn, init=0):
    def step(i, c):
        return fn(pl.ds(pl.multiple_of(i * ROWS, ROWS), ROWS), c)

    return lax.fori_loop(0, T // ROWS, step, init)


def head_window(i):
    start = HD * i
    lane0 = start // 128 * 128
    width = 128 if start + HD <= lane0 + 128 else 256
    sub0 = start // 16 * 16
    return lane0, width, start - lane0, sub0, start - sub0


def lane_mask(width, at):
    pos = lax.broadcasted_iota(jnp.int32, (1, width), 1)
    return jnp.where((pos >= at) & (pos < at + HD), 1.0, 0.0).astype(BF)


def row_ones(off):
    pos = lax.broadcasted_iota(jnp.int32, (32, L), 0)
    own = jnp.where((pos >= off) & (pos < off + HD), 1.0, 0.0)
    return own.astype(BF), (1.0 - own).astype(BF)


def dense_cols(lhs, w, fn, dims=NN, m_rows=256, n_cols=256):
    for n in range(0, D, n_cols):
        block = w[:, n:n + n_cols] if dims is NN else w[n:n + n_cols, :]
        for m in range(0, T, m_rows):
            fn(slice(m, m + m_rows), slice(n, n + n_cols), dot(lhs[m:m + m_rows, :], block, dims))


def fetch(section, place_ref, own_ref, piece_refs, w_s, sems, order=(0, 1, 2)):
    which, core, par = place_ref[0] ^ section, place_ref[1], place_ref[2]

    @pl.when(which == 0)
    def _():
        for m in order:
            pltpu.make_async_copy(own_ref.at[m], w_s.at[m], sems.at[m]).start()

    at_piece = 0
    for k, units in PIECES.items():
        @pl.when(which == k)
        def _(at_piece=at_piece, units=units):
            for m in order:
                for n, (c, (unit, first, rows)) in enumerate((c, u) for c in (0, 1) for u in units):
                    at = (core ^ c) * (D // 2) + (par ^ unit) * WHOLE + first
                    to = pl.ds(pl.multiple_of(at, HALF_UNIT), rows)
                    pltpu.make_async_copy(piece_refs[at_piece + n].at[m], w_s.at[m, to], sems.at[m]).start()

        at_piece += 2 * len(units)


def arrived(own_ref, w_s, sems, m):
    pltpu.make_async_copy(own_ref.at[m], w_s.at[m], sems.at[m]).wait()


def staggered(first, second, third, lead1, lead2):
    one, two = {}, {}
    for i in range(GROUP + lead1 + lead2):
        if i < GROUP:
            one[i] = first(i)
        if 0 <= i - lead1 < GROUP:
            two[i - lead1] = second(i - lead1, *one.pop(i - lead1))
        if 0 <= i - lead1 - lead2 < GROUP:
            third(i - lead1 - lead2, *two.pop(i - lead1 - lead2))


def fill_mask(seg_ref, mask_s):
    for r in range(R):
        ids = jnp.broadcast_to(seg_ref[r].astype(F32), (L, L))
        mask_s[r] = jnp.where(ids == ids.T, 1, 0)


def attn_forward(layer, ready, dense_done, normed_ref, w_s, vec_ref, mask_s, q_ref, k_ref, v_ref, vt_s, ct_s, ctx_ref, lse_ref):
    cq, cv = vec_ref[layer, 2:3, :], vec_ref[layer, 3:4, :]

    def put_q(rows, cols, y):
        q_ref[rows, cols] = (y + cq[:, cols]).astype(BF)

    def put_k(rows, cols, y):
        k_ref[rows, cols] = y.astype(BF)

    def put_v(rows, cols, y):
        y = (y + cv[:, cols]).astype(BF)
        v_ref[rows, cols] = y
        vt_s[cols, rows] = y.T

    for m, put in enumerate((put_q, put_k, put_v)):
        ready(m)
        dense_cols(normed_ref, w_s.at[m], put)
    dense_done()

    def heads(t, c):
        r, g = t // 2, t % 2
        tok = pl.ds(pl.multiple_of(r * L, L), L)
        base = g * GW

        def score(i):
            lane0, width, at, _, _ = head_window(i)
            lanes = pl.ds(pl.multiple_of(base + lane0, 128), width)
            return (dot(k_ref[tok, lanes], q_ref[tok, lanes] * lane_mask(width, at), NT),)

        def soften(i, s):
            s = jnp.where(mask_s[r] != 0, s, NEG)
            top = jnp.max(s, axis=0, keepdims=True)
            return jnp.exp2((s - top) * C2).astype(BF), top

        def mix(i, e, top):
            _, _, _, sub0, off = head_window(i)
            own, ones = row_ones(off)
            out = dot(vt_s[pl.ds(pl.multiple_of(base + sub0, 16), 32), tok] * own + ones, e)
            tot = out[24:25] if off == 0 else out[0:1]
            ct_s[pl.ds(pl.multiple_of(base + HD * i, 8), HD), tok] = out[off:off + HD] * (1.0 / tot)
            lse_ref[pl.ds(g * GROUP + i, 1), tok] = top * C2 + jnp.log(tot) * LOG2E

        staggered(score, soften, mix, 3, 2)
        return c

    lax.fori_loop(0, 2 * R, heads, 0)
    for m in range(0, T, 256):
        for n in range(0, D, 128):
            ctx_ref[m:m + 256, n:n + 128] = ct_s[n:n + 128, m:m + 256].T.astype(BF)


VM = pl.BlockSpec(memory_space=pltpu.VMEM)
SM = pl.BlockSpec(memory_space=pltpu.SMEM)
HB = pl.BlockSpec(memory_space=pltpu.HBM)
TOK = jax.ShapeDtypeStruct((T, D), BF)
TOK_F = jax.ShapeDtypeStruct((T, D), F32)
HALF = jax.ShapeDtypeStruct((3, D // 2, D), BF)
VEC = jax.ShapeDtypeStruct((8, D), F32)
S_TOK = pltpu.VMEM((T, D), BF)
S_TOK_F = pltpu.VMEM((T, D), F32)
S_TOK_T = pltpu.VMEM((D, T), BF)
S_TOK_TF = pltpu.VMEM((D, T), F32)
S_MASK = pltpu.VMEM((R, L, L), jnp.int32)
S_W = [pltpu.VMEM((3, D, D), BF), pltpu.SemaphoreType.DMA((3,))]


def call(body, name, place, ins, weights, outs, scratch, us, mb, stash=()):
    return pl.pallas_call(
        body,
        out_shape=tuple(outs) + tuple(stash),
        in_specs=[SM] + [VM] * len(ins) + [HB] * len(weights),
        out_specs=(VM,) * len(outs) + (HB,) * len(stash),
        scratch_shapes=scratch + S_W,
        compiler_params=params(mb),
        cost_estimate=cost(us),
        name=name,
    )(place, *ins, *weights)


def attn_bwd_body(group, place_ref, normed_ref, q_ref, k_ref, v_ref, lse_ref, do_ref, seg_ref,
                  keep_ref, send_ref, gvec_ref, dq_ref, dk_ref, dv_ref,
                  nt_s, qt_s, kt_s, dot_s, dqf_s, dkf_s, dvf_s, mask_s):
    cols = slice(group * GW, group * GW + GW)
    q_ref, k_ref, v_ref, do_ref = (ref.at[:, cols] for ref in (q_ref, k_ref, v_ref, do_ref))
    fill_mask(seg_ref, mask_s)
    for src, dst in ((normed_ref, nt_s), (q_ref, qt_s), (k_ref, kt_s), (do_ref, dot_s)):
        for m in range(0, T, 256):
            for n in range(0, src.shape[1], 128):
                dst[n:n + 128, m:m + 256] = src[m:m + 256, n:n + 128].T

    def heads(r, c):
        tok = pl.ds(pl.multiple_of(r * L, L), L)

        def score(i):
            lane0, width, at, _, _ = head_window(i)
            lanes = slice(lane0, lane0 + width)
            own = lane_mask(width, at)
            return (dot(k_ref[tok, lanes], q_ref[tok, lanes] * own, NT),
                    dot(v_ref[tok, lanes], do_ref[tok, lanes] * own, NT))

        def soften(i, s, dp):
            head = group * GROUP + i
            s = jnp.where(mask_s[r] != 0, s, NEG)
            p = jnp.exp2(s * C2 - lse_ref[head:head + 1, tok])
            t1 = p * dp
            delta = jnp.sum(t1, axis=0, keepdims=True)
            return p.astype(BF), (t1 - p * delta).astype(BF)

        def mix(i, p, ds):
            _, _, _, sub0, off = head_window(i)
            sub = slice(sub0, sub0 + 32)
            out = slice(HD * i, HD * i + HD)
            dvf_s[out, tok] = dot(dot_s[sub, tok], p, NT)[off:off + HD]
            dkf_s[out, tok] = dot(qt_s[sub, tok], ds, NT)[off:off + HD] * SCALE
            dqf_s[out, tok] = dot(kt_s[sub, tok], ds, NN)[off:off + HD] * SCALE

        staggered(score, soften, mix, 1, 1)
        return c

    lax.fori_loop(0, R, heads, 0)

    def shorten(i, c):
        rows = pl.ds(pl.multiple_of(i * 64, 64), 64)
        dq_ref[rows, :] = dqf_s[rows, :].astype(BF)
        dk_ref[rows, :] = dkf_s[rows, :].astype(BF)
        dv_ref[rows, :] = dvf_s[rows, :].astype(BF)
        return c

    lax.fori_loop(0, GW // 64, shorten, 0)
    core = place_ref[1]
    mine = pl.ds(pl.multiple_of(core * 384, 128), 384)
    other = pl.ds(pl.multiple_of((1 - core) * 384, 128), 384)
    for j, grad in enumerate((dq_ref, dk_ref, dv_ref)):
        send_ref[j] = dot(nt_s[other, :], grad[...], NT).astype(BF)
        keep_ref[j] = dot(nt_s[mine, :], grad[...], NT).astype(BF)
    ones = jnp.ones((8, T), BF)
    gvec_ref[0:1, :] = dot(ones, dq_ref[...], NT)[0:1]
    gvec_ref[1:2, :] = dot(ones, dv_ref[...], NT)[0:1]


def grad_normed(own_ref, w_s, sems, grads, put):
    for m in range(3):
        arrived(own_ref, w_s, sems, m)
    for m in range(0, D, 256):
        for n in range(0, T, 256):
            y = 0.0
            for j in range(6):
                cols = slice(j // 3 * GW, j // 3 * GW + GW)
                y += dot(w_s[j % 3, m:m + 256, cols], grads[j][:, n:n + 256])
            put(slice(n, n + 256), slice(m, m + 256), y.T)


def attn_bwd_last_body(place_ref, *refs):
    ins, grads, refs = refs[:7], refs[7:10], refs[10:]
    own_ref, pieces, refs = refs[0], refs[1:1 + N_PIECES], refs[1 + N_PIECES:]
    outs, gx_ref, refs = refs[:6], refs[6], refs[7:]
    scratch, w_s, sems = refs[:-2], refs[-2], refs[-1]
    fetch(2, place_ref, own_ref, pieces, w_s, sems)
    attn_bwd_body(1, place_ref, *ins, *outs, *scratch)

    def put(rows, cols, y):
        gx_ref[rows, cols] = y.astype(BF)

    grad_normed(own_ref, w_s, sems, grads + outs[3:6], put)


def attn_bwd_last(place, normed, q, k, v, lse, grad_ctx, seg, grads, weights, name):
    part = jax.ShapeDtypeStruct((3, D // 2, GW), BF)
    grad = jax.ShapeDtypeStruct((GW, T), BF)
    s_part, s_part_f = pltpu.VMEM((GW, T), BF), pltpu.VMEM((GW, T), F32)
    return call(attn_bwd_last_body, name, place, (normed, q, k, v, lse, grad_ctx, seg, *grads), weights,
                (part, part, jax.ShapeDtypeStruct((8, GW), F32), grad, grad, grad, TOK),
                [S_TOK_T] + [s_part] * 3 + [s_part_f] * 3 + [S_MASK], 12, MB_ATTN)


def attn_bwd(group, place, normed, q, k, v, lse, grad_ctx, seg, name):
    part = jax.ShapeDtypeStruct((3, D // 2, GW), BF)
    grad = jax.ShapeDtypeStruct((GW, T), BF)
    s_part, s_part_f = pltpu.VMEM((GW, T), BF), pltpu.VMEM((GW, T), F32)
    return pl.pallas_call(
        functools.partial(attn_bwd_body, group),
        out_shape=(part, part, jax.ShapeDtypeStruct((8, GW), F32), grad, grad, grad),
        in_specs=[SM] + [VM] * 7,
        out_specs=(VM,) * 6,
        scratch_shapes=[S_TOK_T] + [s_part] * 3 + [s_part_f] * 3 + [S_MASK],
        compiler_params=params(MB_ATTN),
        cost_estimate=cost(8),
        name=name,
    )(place, normed, q, k, v, lse, grad_ctx, seg)


def inputs_bwd_body(place_ref, *rest):
    grads, (x_ref, branch_ref, vec_ref, *rest) = rest[:6], rest[6:]
    own_ref, pieces, outs, scratch, w_s, sems = split_refs(rest, 2)
    gx_ref, gvec_ref = outs
    gn_s = scratch[0]
    fetch(0, place_ref, own_ref, pieces, w_s, sems)

    def put(rows, cols, y):
        gn_s[rows, cols] = y

    grad_normed(own_ref, w_s, sems, grads, put)

    def norm_back(rows, c):
        dy = gn_s[rows, :]
        dv, dg = ln_back(x_ref[rows, :].astype(F32), vec_ref[0, 0:1, :], dy)
        gx_ref[rows, :] = (branch_ref[rows, :].astype(F32) + dv).astype(BF)
        return c[0] + fold(dg), c[1] + fold(dy)

    zero = jnp.zeros((8, D), F32)
    dg, db = row_loop(norm_back, (zero, zero))
    gvec_ref[...] = jnp.zeros(gvec_ref.shape, F32)
    gvec_ref[0:1, :] = jnp.sum(dg, axis=0, keepdims=True)
    gvec_ref[1:2, :] = jnp.sum(db, axis=0, keepdims=True)


def inputs_bwd(place, grads, x, branch, vec, weights):
    return call(inputs_bwd_body, "inputs_bwd", place, (*grads, x, branch, vec), weights, (TOK, VEC), [S_TOK_F], 4, MB_SMALL)


def ffn_forward(layer, ready, res_ref, ctx_ref, w_ref, vec_ref, hid_s, mid_s, raised_s, act_s, gp_s, sum_put):
    co, gf, bf, c1, c2 = (vec_ref[layer, i:i + 1, :] for i in range(5))

    def put_hidden(rows, cols, y):
        hid_s[rows, cols] = res_ref[rows, cols].astype(F32) + (y + co[:, cols])

    ready(0)
    dense_cols(ctx_ref, w_ref.at[0], put_hidden)

    def norm(rows, c):
        xhat, _ = ln_stats(hid_s[rows, :])
        mid_s[rows, :] = (xhat * gf + bf).astype(BF)
        return c

    row_loop(norm)

    def put_raised(rows, cols, y):
        raised_s[rows, cols] = y + c1[:, cols]

    ready(1)
    dense_cols(mid_s, w_ref.at[1], put_raised)

    def activate(rows, c):
        a = raised_s[rows, :]
        phi = 0.5 + 0.5 * lax.erf(a * (1.0 / math.sqrt(2.0)))
        act_s[rows, :] = (a * phi).astype(BF)
        density = jnp.exp2(a * a * (-0.5 * LOG2E)) * (1.0 / math.sqrt(2.0 * math.pi))
        gp_s[rows, :] = phi + a * density
        return c

    row_loop(activate)

    def put_summed(rows, cols, y):
        sum_put(rows, cols, hid_s[rows, cols] + (y + c2[:, cols]))

    ready(2)
    dense_cols(act_s, w_ref.at[2], put_summed)


def ffn_backward(layer, ready, place_ref, gsum_s, glow_s, hid_s, gp_s, mid_s, act_s, ctx_ref, w_ref, vec_ref,
                 gbranch_ref, gctx_ref, keep_ref, send_ref, gvec_ref, graise_s, gmid_s, t_s, branch_done=lambda: None):
    gf = vec_ref[layer, 1:2, :]
    core = place_ref[1]
    mine = pl.ds(pl.multiple_of(core * 384, 128), 384)
    other = pl.ds(pl.multiple_of((1 - core) * 384, 128), 384)
    zero = jnp.zeros((8, D), F32)

    def weight_grad(j, x_ref, grad_ref):
        for m in range(0, T, 256):
            for n in range(0, D, 256):
                t_s[n:n + 256, m:m + 256] = x_ref[m:m + 256, n:n + 256].T
        for n in range(0, D, 256):
            block = grad_ref[:, n:n + 256]
            send_ref[j, :, n:n + 256] = dot(t_s[other, :], block).astype(BF)
            keep_ref[j, :, n:n + 256] = dot(t_s[mine, :], block).astype(BF)

    def put_raised(rows, cols, y):
        graise_s[rows, cols] = (y * gp_s[rows, cols]).astype(BF)

    ready(2)
    dense_cols(glow_s, w_ref.at[2], put_raised, NT)
    weight_grad(2, act_s, glow_s)

    def put_mid(rows, cols, y):
        gmid_s[rows, cols] = y

    ready(1)
    dense_cols(graise_s, w_ref.at[1], put_mid, NT)
    weight_grad(1, mid_s, graise_s)

    def norm_back(rows, c):
        dy = gmid_s[rows, :]
        dv, dg = ln_back(hid_s[rows, :], gf, dy)
        branch = (gsum_s[rows, :].astype(F32) + dv).astype(BF)
        gbranch_ref[rows, :] = branch
        return (c[0] + fold(branch.astype(F32)), c[1] + fold(dg), c[2] + fold(dy),
                c[3] + fold(graise_s[rows, :].astype(F32)), c[4] + fold(glow_s[rows, :].astype(F32)))

    sums = row_loop(norm_back, (zero,) * 5)
    branch_done()
    for i in range(5):
        gvec_ref[i:i + 1, :] = jnp.sum(sums[i], axis=0, keepdims=True)

    def put_ctx(rows, cols, y):
        gctx_ref[rows, cols] = y.astype(BF)

    ready(0)
    dense_cols(gbranch_ref, w_ref.at[0], put_ctx, NT)
    weight_grad(0, ctx_ref, gbranch_ref)


def split_refs(rest, outs):
    at = 1 + N_PIECES
    return rest[0], rest[1:at], rest[at:at + outs], rest[at + outs:-2], rest[-2], rest[-1]


def forward_body(place_ref, av_ref, fv_ref, seg_ref, own_ref, *rest):
    pieces, rest = rest[:N_PIECES], rest[N_PIECES:]
    (x_hbm, cot_hbm, gctx_ref, keep_ref, send_ref, gvec_ref, lse0_ref, lse1_ref,
     q0_ref, k0_ref, v0_ref, n0_ref, q1_ref, k1_ref, v1_ref, n1_ref, c0_ref, hid_ref, mid_ref, act_ref, gp_ref, sum_ref, out_ref, gb_ref,
     q_s, k_s, v_s, n_s, vt_s, ct_s, mask_s, ctx_s, hid_s, mid_s, act_s, gp_s, raised_s, stream_s, out_s, x_ref, cot_ref,
     w1_s, stash_sems, sems1, w0_s, sems0) = rest
    sum_s, t_s, graise_s, gbranch_ref = raised_s, vt_s, n_s, stream_s
    flying = {}

    def stash(n, src, dst):
        flying[n] = pltpu.make_async_copy(src, dst, stash_sems.at[n])
        flying[n].start()

    def landed(*names):
        for n in names:
            flying.pop(n).wait()

    def norm_into(src_ref, gain, offset, also=None):
        def step(rows, c):
            v = src_ref[rows, :].astype(F32)
            if also is not None:
                also[rows, :] = v.astype(BF)
            xhat, _ = ln_stats(v)
            n_s[rows, :] = (xhat * gain + offset).astype(BF)
            return c

        row_loop(step)

    ready0 = functools.partial(arrived, own_ref, w0_s, sems0)
    ready1 = functools.partial(arrived, own_ref, w1_s, sems1)
    stash(10, x_hbm, x_ref)
    fetch(0, place_ref, own_ref, pieces, w0_s, sems0)
    fetch(1, place_ref, own_ref, pieces, w1_s, sems1)
    stash(11, cot_hbm, cot_ref)
    landed(10)
    norm_into(x_ref, av_ref[0, 0:1, :], av_ref[0, 1:2, :])
    stash(3, n_s, n0_ref)
    fill_mask(seg_ref, mask_s)

    def dense0_done():
        fetch(2, place_ref, own_ref, pieces, w0_s, sems0)
        stash(0, q_s, q0_ref)
        stash(1, k_s, k0_ref)
        stash(2, v_s, v0_ref)

    attn_forward(0, ready0, dense0_done, n_s, w0_s, av_ref, mask_s, q_s, k_s, v_s, vt_s, ct_s, ctx_s, lse0_ref)
    stash(4, ctx_s, c0_ref)

    def put_sum(rows, cols, y):
        sum_s[rows, cols] = y

    ffn_forward(0, ready1, x_ref, ctx_s, w1_s, fv_ref, hid_s, mid_s, raised_s, act_s, gp_s, put_sum)
    fetch(3, place_ref, own_ref, pieces, w1_s, sems1)
    for n, (src, dst) in enumerate(((hid_s, hid_ref), (mid_s, mid_ref), (act_s, act_ref), (gp_s, gp_ref), (sum_s, sum_ref))):
        stash(5 + n, src, dst)
    landed(3)
    norm_into(sum_s, av_ref[1, 0:1, :], av_ref[1, 1:2, :], stream_s)
    stash(3, n_s, n1_ref)
    landed(0, 1, 2)

    def dense1_done():
        stash(0, q_s, q1_ref)
        stash(1, k_s, k1_ref)
        stash(2, v_s, v1_ref)
        landed(4)

    attn_forward(1, ready0, dense1_done, n_s, w0_s, av_ref, mask_s, q_s, k_s, v_s, vt_s, ct_s, ctx_s, lse1_ref)
    landed(5, 6, 7, 8, 9)

    def put_out(rows, cols, y):
        out_s[rows, cols] = y.astype(BF)

    ffn_forward(1, ready1, stream_s, ctx_s, w1_s, fv_ref, hid_s, mid_s, raised_s, act_s, gp_s, put_out)
    stash(10, out_s, out_ref)
    landed(0, 1, 2, 3, 11)
    gvec_ref[...] = jnp.zeros(gvec_ref.shape, F32)
    ffn_backward(1, lambda m: None, place_ref, cot_ref, cot_ref, hid_s, gp_s, mid_s, act_s, ctx_s, w1_s, fv_ref,
                 gbranch_ref, gctx_ref, keep_ref, send_ref, gvec_ref, graise_s, raised_s, t_s,
                 lambda: stash(0, gbranch_ref, gb_ref))
    landed(0, 10)


def forward(place, x, av, fv, seg, cot, weights):
    lse = jax.ShapeDtypeStruct((HEADS, T), F32)
    return call(forward_body, "forward", place, (av, fv, seg), (*weights, x, cot),
                (TOK, HALF, HALF, VEC, lse, lse),
                [S_TOK] * 4 + [S_TOK_T, S_TOK_TF, S_MASK, S_TOK, S_TOK_F, S_TOK, S_TOK, S_TOK_F, S_TOK_F, S_TOK, S_TOK, S_TOK, S_TOK,
                 S_W[0], pltpu.SemaphoreType.DMA((12,)), S_W[1]], 40, MB_FORWARD,
                (TOK,) * 9 + (TOK_F, TOK, TOK, TOK_F, TOK_F, TOK, TOK))


def ffn_bwd_body(place_ref, gstream_ref, gnormed_ref, sum_ref, next_ref, hid_ref, gp_ref, mid_ref, act_ref, ctx_ref, vec_ref, *rest):
    own_ref, pieces, outs, scratch, w_s, sems = split_refs(rest, 6)
    gbranch_ref, gctx_ref, keep_ref, send_ref, gvec_ref, gnext_ref = outs
    gsum_s, glow_s, graise_s, gmid_s, t_s = scratch
    fetch(1, place_ref, own_ref, pieces, w_s, sems, (2, 1, 0))
    zero = jnp.zeros((8, D), F32)

    def norm_back(rows, c):
        dy = gnormed_ref[rows, :].astype(F32)
        dv, dg = ln_back(sum_ref[rows, :], next_ref[1, 0:1, :], dy)
        total = gstream_ref[rows, :].astype(F32) + dv
        gsum_s[rows, :] = total
        glow_s[rows, :] = total.astype(BF)
        return c[0] + fold(dg), c[1] + fold(dy)

    dg, db = row_loop(norm_back, (zero, zero))
    gvec_ref[...] = jnp.zeros(gvec_ref.shape, F32)
    gnext_ref[...] = jnp.zeros(gnext_ref.shape, F32)
    gnext_ref[0:1, :] = jnp.sum(dg, axis=0, keepdims=True)
    gnext_ref[1:2, :] = jnp.sum(db, axis=0, keepdims=True)
    ffn_backward(0, functools.partial(arrived, own_ref, w_s, sems), place_ref, gsum_s, glow_s, hid_ref, gp_ref, mid_ref, act_ref,
                 ctx_ref, w_s, vec_ref, gbranch_ref, gctx_ref, keep_ref, send_ref, gvec_ref, graise_s, gmid_s, t_s)


def ffn_bwd(place, gstream, gnormed, summed, nxt, hid, gp, mid, act, ctx, vec, weights):
    return call(ffn_bwd_body, "ffn_bwd", place, (gstream, gnormed, summed, nxt, hid, gp, mid, act, ctx, vec), weights,
                (TOK, TOK, HALF, HALF, VEC, VEC), [S_TOK_F, S_TOK, S_TOK, S_TOK_F, S_TOK_T], 10, MB_FFN)


def split_low(v):
    high = v.astype(BF)
    return high, (v - high.astype(F32)).astype(BF)


def combine_body(tasks, place_ref, *refs):
    refs = list(refs)
    ins = [[refs.pop(0) for _ in range(2 * pairs + rider)] for _, pairs, rider, _ in tasks]
    outs = [[refs.pop(0) for _ in range((bit is not None) + 1 + rider)] for bit, _, rider, _ in tasks]
    for (bit, pairs, rider, riding), arrays, results in zip(tasks, ins, outs):
        rows_in = arrays[0].shape[1] - (RIDE if riding == 2 else 0)
        half = rows_in // (1 if bit is None else 2)
        sent = results[0]
        for n, out_ref in enumerate(results[:2] if bit is not None else results[:1]):
            at = 0
            if bit is not None:
                at = (place_ref[bit] ^ (1 - n)) * half
            rows = pl.ds(at if bit is None else pl.multiple_of(at, half), half)
            col = 0
            for p in range(pairs):
                a_ref, b_ref = arrays[2 * p], arrays[2 * p + 1]
                width = a_ref.shape[2]
                out_ref[:, 0:half, col:col + width] = a_ref[:, rows, :] + b_ref[:, rows, :]
                col += width
        if rider:
            vec = arrays[-1][...]
            for j in range(3):
                rows = slice(8 * j, 8 * j + 8)
                out = []
                for c in range(2):
                    cols = slice(c * GW, c * GW + GW)
                    mine = vec[rows, cols]
                    if riding:
                        got = arrays[1][j, rows_in:rows_in + RIDE, :].astype(F32)
                        mine = mine + (got[16 * c:16 * c + 8] + got[16 * c + 8:16 * c + 16])
                    results[-1][rows, cols] = mine
                    out += list(split_low(mine))
                sent[j, half:half + RIDE, :] = jnp.concatenate([v.astype(F32) for v in out], axis=0).astype(BF)


def combine(place, *tasks):
    outs, kinds, ins = [], [], []
    for bit, pairs, vec, riding in tasks:
        a = pairs[0][0]
        width = sum(mine.shape[2] for mine, _ in pairs)
        rows = (a.shape[1] - (RIDE if riding == 2 else 0)) // (1 if bit is None else 2)
        ride = 0 if vec is None else RIDE
        outs.append(jax.ShapeDtypeStruct((3, rows + ride, width), BF))
        if bit is not None:
            outs.append(jax.ShapeDtypeStruct((3, rows, width), BF))
        if vec is not None:
            outs.append(jax.ShapeDtypeStruct(vec.shape, F32))
        kinds.append((bit, len(pairs), vec is not None, riding))
        ins += [x for pair in pairs for x in pair] + ([] if vec is None else [vec])
    parts = list(pl.pallas_call(
        functools.partial(combine_body, kinds),
        out_shape=tuple(outs),
        in_specs=[SM] + [VM] * len(ins),
        out_specs=tuple([VM] * len(outs)),
        compiler_params=params(MB_SMALL),
        cost_estimate=cost(0.5 * len(tasks)),
        name="combine",
    )(place, *ins))
    results = []
    for bit, _, rider, _ in kinds:
        count = (bit is not None) + 1 + rider
        results.append(tuple(parts[:count]) if count > 1 else parts[0])
        parts = parts[count:]
    return results


def add(bit, mine, got):
    return (bit, [(mine, got)], None, 0)


PARTS = {0: [(1, D, 0), (0, 0, GW)], 1: [(1, 0, 0)], 2: [(2, 0, 0)], 3: [(3, 0, 0)]}


def for_section(place_ref, distance, fn):
    for j in range(4):
        @pl.when((place_ref[0] ^ distance) == j)
        def _(j=j):
            for pair, col, to in PARTS[j]:
                width = GW if j == 0 else D
                fn(pair, slice(col, col + width), slice(to, to + width))


def pick_far_body(place_ref, *refs):
    out_ref = refs[-1]

    def put(pair, src, dst):
        out_ref[:, :, dst] = refs[pair][:, 0:D // 16, src]

    for_section(place_ref, 3, put)


def pick_far(place, *ins):
    return pl.pallas_call(
        pick_far_body,
        out_shape=jax.ShapeDtypeStruct((3, D // 16, D), BF),
        in_specs=[SM] + [VM] * 4,
        out_specs=VM,
        compiler_params=params(MB_SMALL),
        name="pick_far",
    )(place, *ins)


def pick_body(place_ref, *refs):
    half = D // 16
    for k, out_ref in enumerate(refs[8:]):
        for flipped in (0, 1):
            rows = pl.ds(pl.multiple_of((place_ref[5] ^ flipped) * half, half), half)

            def put(pair, src, dst, flipped=flipped, rows=rows, out_ref=out_ref):
                out_ref[:, rows, dst] = refs[2 * pair + flipped][:, 0:half, src]

            for_section(place_ref, k, put)


def pick(place, *ins):
    shape = jax.ShapeDtypeStruct((3, D // 8, D), BF)
    return pl.pallas_call(
        pick_body,
        out_shape=(shape,) * 3,
        in_specs=[SM] + [VM] * 8,
        out_specs=(VM,) * 3,
        compiler_params=params(MB_SMALL),
        name="pick",
    )(place, *ins)


def assemble_body(which, place_ref, *refs):
    parts, (out_ref, wide_s, sems) = refs[:len(which)], refs[-3:]
    copies = []
    for n, (c, k, chip) in enumerate(which):
        core = place_ref[1] ^ c
        section = place_ref[0] ^ k
        x_bit, y_bit = section % 2, section // 2
        row = jnp.where(core == 0, 2 * x_bit + y_bit, 2 * y_bit + x_bit)
        count = parts[n].shape[1]
        at = core * (D // 2) + row * (D // 8)
        if chip is not None:
            at = at + (place_ref[5] ^ chip) * count
        rows = pl.ds(pl.multiple_of(at, count), count)
        wide_s[n, :, 0:count, :] = parts[n][...].astype(F32)
        copies.append(pltpu.make_async_copy(wide_s.at[n, :, 0:count, :], out_ref.at[:, rows, :], sems.at[n]))
        copies[-1].start()
    for copy in copies:
        copy.wait()


def assemble(place, which, parts, whole=None):
    extra = [] if whole is None else [whole]
    return pl.pallas_call(
        functools.partial(assemble_body, which),
        out_shape=jax.ShapeDtypeStruct((3, D, D), F32),
        in_specs=[SM] + [VM] * len(parts) + [HB] * len(extra),
        out_specs=HB,
        scratch_shapes=[pltpu.VMEM((len(parts), 3, D // 8, D), F32), pltpu.SemaphoreType.DMA((len(parts),))],
        input_output_aliases={1 + len(parts): 0} if extra else {},
        compiler_params=params(MB_SMALL),
        name="assemble",
    )(place, *parts, *extra)


def stack_body(norm0_ref, a0_ref, b0_ref, norm1_ref, a1_ref, b1_ref, ffn0_ref, ffn1_ref, out_ref):
    for at, norm_ref, a_ref, b_ref in ((0, norm0_ref, a0_ref, b0_ref), (4, norm1_ref, a1_ref, b1_ref)):
        out_ref[at:at + 2, :] = norm_ref[0:2, :]
        out_ref[at + 2:at + 4, 0:GW] = a_ref[0:2, :]
        out_ref[at + 2:at + 4, GW:D] = b_ref[0:2, :]
    out_ref[8:13, :] = ffn0_ref[0:5, :]
    out_ref[13:18, :] = ffn1_ref[0:5, :]
    out_ref[18:24, :] = jnp.zeros((6, D), F32)


def stack_vectors(*parts):
    return pl.pallas_call(
        stack_body,
        out_shape=jax.ShapeDtypeStruct((24, D), F32),
        in_specs=[VM] * len(parts),
        out_specs=VM,
        compiler_params=params(MB_SMALL),
        name="stack_vectors",
    )(*parts)


def unstack_body(mine_ref, other_ref, attn_ref, ffn_ref):
    for i in range(2):
        attn_ref[i] = mine_ref[4 * i:4 * i + 4, :] + other_ref[4 * i:4 * i + 4, :]
        ffn_ref[i] = mine_ref[8 + 5 * i:13 + 5 * i, :] + other_ref[8 + 5 * i:13 + 5 * i, :]


def unstack(mine, other):
    return pl.pallas_call(
        unstack_body,
        out_shape=(jax.ShapeDtypeStruct((2, 4, D), F32), jax.ShapeDtypeStruct((2, 5, D), F32)),
        in_specs=[VM] * 2,
        out_specs=(VM,) * 2,
        compiler_params=params(MB_SMALL),
        name="unstack",
    )(mine, other)


def swap_cores(value):
    count = lax.axis_size("dp")
    return lax.ppermute(value, "dp", [(i, i ^ 1) for i in range(count)])


def next_chip(value, bits):
    count = lax.axis_size("dp")
    return lax.ppermute(value, "dp", [(i, i ^ 2 * bits) for i in range(count)])


def plane_swap(value, step):
    count, sections = lax.axis_size("dp"), lax.axis_size("section")
    pairs = []
    for s in range(sections):
        for i in range(count):
            other = s ^ (1 if step == i % 2 else 2)
            pairs.append((s * count + i, other * count + i))
    return lax.ppermute(value, ("section", "dp"), pairs)


def flip(value, bits):
    count = lax.axis_size("section")
    return lax.ppermute(value, "section", [(i, i ^ bits) for i in range(count)])


def gather_pieces(own, core, par, ready):
    def part(p):
        return lax.dynamic_slice(own, (0, core * (D // 2) + p * WHOLE, 0), (3, WHOLE, D))

    mine = part(par)
    near, down = flip(mine, 1), flip(part(1 - par), 2)
    near, down, mine, *ready = together(near, down, mine, *ready)
    rest = mine[:, HALF_UNIT:]
    far_a, far_b = flip(near, 2), flip(down, 1)
    near_z, down_z, down_y = next_chip(near, 1), next_chip(down[:, :HALF_UNIT], 1), flip(rest, 2)
    mine = [[near, near_z], [down, down_z, down_y], [far_a, far_b]]
    return [piece for group in mine for piece in group + [swap_cores(x) for x in group]], ready


def line_groups():
    count = lax.axis_size("dp")
    return [[r * 8 + i for r in range(count // 8)] for i in range(8)]


def across_lines(value):
    if lax.axis_size("dp") == 8:
        return value
    return lax.psum(value.astype(F32), "dp", axis_index_groups=line_groups()).astype(value.dtype)


def together(*values):
    return lax.optimization_barrier(values)


def shards(inputs, cotangent, segments, matrices, attn_vectors, ffn_vectors):
    section = lax.axis_index("section")
    dp = lax.axis_index("dp")
    core, position = dp % 2, dp // 2
    par = position % 2
    x_bit, y_bit = section % 2, section // 2
    first = jnp.where(core == 0, x_bit, y_bit)
    second = jnp.where(core == 0, y_bit, x_bit)
    own = matrices[0]
    turn = dp // 2 % 2
    places = [jnp.stack([section ^ j, core, par, first, second, turn]).astype(jnp.int32) for j in range(4)]
    seg = lax.dynamic_slice(segments, (R * section, 0, 0), (R, 1, L))
    pieces, (*places, seg) = gather_pieces(own, core, par, (*places, seg))
    weights = (own, *pieces)
    here = places[0]
    x = inputs.reshape(T, D)
    cot = cotangent.reshape(T, D)
    av, fv = attn_vectors, ffn_vectors

    (gc1, keep3, send3, gv3, l0, l1,
     q0, k0, v0, n0, q1, k1, v1, n1, c0, hid, mid, act, gp, summed, out, gb1) = forward(here, x, av, fv, seg, cot, weights)
    got3 = swap_cores(send3)

    keep2a, send2a, gv2a, *grads2 = attn_bwd(0, here, n1, q1, k1, v1, l1, gc1, seg, "attn_bwd_1a")
    ((send3, keep3),) = combine(here, add(3, keep3, got3))
    send2a, send3 = together(send2a, send3)
    got3, got2a = plane_swap(send3, 0), swap_cores(send2a)
    gc1, keep3 = together(gc1, keep3)

    keep2b, send2b, gv2b, _, _, _, gn1 = attn_bwd_last(here, n1, q1, k1, v1, l1, gc1, seg, grads2, weights, "attn_bwd_1b")
    gn1, got2a, got3, send2b = together(gn1, got2a, got3, send2b)
    got2b = swap_cores(send2b)
    (send3, keep3), (send2, keep2) = combine(here, add(4, keep3, got3), (3, [(keep2a, got2a), (keep2b, got2b)], None, 0))
    got3, got2 = plane_swap(send3, 1), plane_swap(send2, 0)
    gb1, keep3 = together(gb1, keep3)

    gb0, gc0, keep1, send1, gv1, gnext = ffn_bwd(here, gb1, gn1, summed, av, hid, gp, mid, act, c0, fv, weights)
    ((send3, keep3),) = combine(here, add(5, keep3, got3))
    send1, send3 = together(send1, send3)
    got3, got1 = next_chip(send3, 1), swap_cores(send1)
    gc0, keep3 = together(gc0, keep3)

    keep0a, send0a, gv0a, *grads0 = attn_bwd(0, here, n0, q0, k0, v0, l0, gc0, seg, "attn_bwd_0a")
    keep3, (send2, keep2) = combine(here, add(None, keep3, got3), add(4, keep2, got2))
    send0a, send2 = together(send0a, send2)
    got3, got2, got0a = next_chip(keep3, 2), plane_swap(send2, 1), swap_cores(send0a)
    ((send1, keep1),) = combine(here, (3, [(keep1, got1), (keep0a, got0a)], None, 0))
    got1 = plane_swap(send1, 0)
    gc0, keep1 = together(gc0, keep1)

    keep0b, send0b, gv0b, *grads0b = attn_bwd(1, here, n0, q0, k0, v0, l0, gc0, seg, "attn_bwd_0b")
    send0b, keep2 = together(send0b, keep2)
    ((send2, keep2),) = combine(here, add(5, keep2, got2))
    send0b, send2 = together(send0b, send2)
    got2, got0b = next_chip(send2, 1), swap_cores(send0b)
    grads0b[0], keep2 = together(grads0b[0], keep2)

    gx, gv0n = inputs_bwd(here, (*grads0, *grads0b), x, gb0, av, weights)
    vec = stack_vectors(gv0n, gv0a, gv0b, gnext, gv2a, gv2b, gv1, gv3)
    (send0, keep0, vec), (send1, keep1), keep2, keep3 = combine(
        here, (3, [(keep0b, got0b)], vec, 0), add(4, keep1, got1), add(None, keep2, got2), add(None, keep3, got3))
    got0, got1, got2, got3 = plane_swap(send0, 0), plane_swap(send1, 1), next_chip(keep2, 2), next_chip(keep3, 1)

    got3, got0 = together(got3, got0)
    (send0, keep0, vec), (send1, keep1), keep2 = combine(
        here, (4, [(keep0, got0)], vec, 1), add(5, keep1, got1), add(None, keep2, got2))
    got0, got1, got2 = plane_swap(send0, 1), next_chip(send1, 1), next_chip(keep2, 1)

    (send0, keep0, vec), keep1 = combine(here, (5, [(keep0, got0)], vec, 1), add(None, keep1, got1))
    got0, got1 = next_chip(send0, 1), next_chip(keep1, 2)

    ((sum0, vec),) = combine(here, (None, [(keep0, got0)], vec, 1))
    got0 = next_chip(sum0, 2)

    got2, got1 = together(got2, got1)
    (keep0, vec), keep1 = combine(here, (None, [(sum0, got0)], vec, 2), add(None, keep1, got1))
    keep0, keep1, keep2, keep3 = (across_lines(v) for v in (keep0, keep1, keep2, keep3))
    far = flip(pick_far(here, keep0, keep1, keep2, keep3), 3)
    got0, got1 = next_chip(keep0, 1), next_chip(keep1, 1)
    vec = across_lines(vec)
    vec_got = swap_cores(vec)
    vec_got, far, got0, got1 = together(vec_got, far, got0, got1)
    grad_attn, grad_ffn = unstack(vec, vec_got)
    if lax.axis_size("dp") > 8:
        got2, got3 = next_chip(keep2, 1), next_chip(keep3, 1)

    own_part, x_part, y_part = pick(here, keep0, got0, keep1, got1, keep2, got2, keep3, got3)
    x_part, y_part = flip(x_part, 1), flip(y_part, 2)
    far_next = next_chip(far, 1)
    whole = assemble(here, ((0, 0, None),), (own_part,))
    x_part, y_part, far_next, own_part = together(x_part, y_part, far_next, own_part)
    others = [swap_cores(v) for v in (own_part, x_part, y_part, far, far_next)]
    whole = assemble(here, ((0, 1, None), (0, 2, None), (0, 3, 0), (0, 3, 1)), (x_part, y_part, far, far_next), whole)
    whole = assemble(here, ((1, 0, None), (1, 1, None), (1, 2, None), (1, 3, 0), (1, 3, 1)), others, whole)
    grad_matrices = whole[None]
    shape = inputs.shape
    return (out.reshape(shape), gx.reshape(shape), grad_matrices, grad_attn, grad_ffn)


def solution(mesh):
    rows = P("section", "dp", None, None)
    mats = P("section", None, None, None)
    return jax.shard_map(
        shards,
        mesh=mesh,
        in_specs=(rows, rows, P(None, "dp", None), mats, P(), P()),
        out_specs=(rows, rows, mats, P(), P()),
        check_vma=False,
    )
```

```python
import functools
import math

import jax
import jax.numpy as jnp
from jax import lax
from jax.experimental import pallas as pl
from jax.experimental.pallas import tpu as pltpu
from jax.sharding import PartitionSpec as P

HEADS = 32
HD = 24
D = 768
L = 256
R = 2
T = R * L
EPS = 1e-05
LOG2E = math.log2(math.e)
SCALE = 1.0 / math.sqrt(HD)
C2 = LOG2E * SCALE
NEG = -1e30 * math.sqrt(HD)
BF = jnp.bfloat16
F32 = jnp.float32
GROUP = 16
GW = GROUP * HD
ROWS = 128
GELU_BLOCK = (128, 256)
MB_FORWARD, MB_ATTN, MB_FFN, MB_SMALL = 27, 16, 16, 16

WHOLE, HALF_UNIT = D // 4, D // 8
PIECES = {
    1: [(0, 0, WHOLE), (1, 0, WHOLE)],
    2: [(1, 0, WHOLE), (0, 0, HALF_UNIT), (0, HALF_UNIT, HALF_UNIT)],
    3: [(0, 0, WHOLE), (1, 0, WHOLE)],
}
N_PIECES = 2 * sum(len(p) for p in PIECES.values())
RIDE = 32

NN = (((1,), (0,)), ((), ()))
NT = (((1,), (1,)), ((), ()))


def dot(a, b, dims=NN):
    return lax.dot_general(a, b, dims, preferred_element_type=F32)


def cost(us):
    return pl.CostEstimate(flops=0, bytes_accessed=0, transcendentals=0)


def params(mb):
    return pltpu.CompilerParams(vmem_limit_bytes=mb * 1024 * 1024)


def ln_stats(v):
    center = v - jnp.mean(v, axis=-1, keepdims=True)
    spread = jnp.mean(center * center, axis=-1, keepdims=True)
    r = lax.rsqrt(spread + EPS)
    return center * r, r


def ln_back(v, gain, dy):
    xhat, r = ln_stats(v)
    e = dy * gain
    dv = r * (e - jnp.mean(e, axis=-1, keepdims=True) - xhat * jnp.mean(e * xhat, axis=-1, keepdims=True))
    return dv, dy * xhat


def fold(v):
    return jnp.sum(v.reshape(v.shape[0] // 8, 8, v.shape[1]), axis=0)


def row_loop(fn, init=0, unroll=1):
    def step(i, c):
        return fn(pl.ds(pl.multiple_of(i * ROWS, ROWS), ROWS), c)

    return lax.fori_loop(0, T // ROWS, step, init, unroll=unroll)


def head_window(i):
    start = HD * i
    lane0 = start // 128 * 128
    width = 128 if start + HD <= lane0 + 128 else 256
    sub0 = start // 16 * 16
    return lane0, width, start - lane0, sub0, start - sub0


def lane_mask(width, at):
    pos = lax.broadcasted_iota(jnp.int32, (1, width), 1)
    return jnp.where((pos >= at) & (pos < at + HD), 1.0, 0.0).astype(BF)


def row_ones(off):
    pos = lax.broadcasted_iota(jnp.int32, (32, L), 0)
    own = jnp.where((pos >= off) & (pos < off + HD), 1.0, 0.0)
    return own.astype(BF), (1.0 - own).astype(BF)


def dense_cols(lhs, w, fn, dims=NN, m_rows=256, n_cols=256):
    for n in range(0, D, n_cols):
        block = w[:, n:n + n_cols] if dims is NN else w[n:n + n_cols, :]
        for m in range(0, T, m_rows):
            fn(slice(m, m + m_rows), slice(n, n + n_cols), dot(lhs[m:m + m_rows, :], block, dims))


def fetch(section, place_ref, own_ref, piece_refs, w_s, sems, order=(0, 1, 2)):
    which, core, par = place_ref[0] ^ section, place_ref[1], place_ref[2]

    @pl.when(which == 0)
    def _():
        for m in order:
            pltpu.make_async_copy(own_ref.at[m], w_s.at[m], sems.at[m]).start()

    at_piece = 0
    for k, units in PIECES.items():
        @pl.when(which == k)
        def _(at_piece=at_piece, units=units):
            for m in order:
                for n, (c, (unit, first, rows)) in enumerate((c, u) for c in (0, 1) for u in units):
                    at = (core ^ c) * (D // 2) + (par ^ unit) * WHOLE + first
                    to = pl.ds(pl.multiple_of(at, HALF_UNIT), rows)
                    pltpu.make_async_copy(piece_refs[at_piece + n].at[m], w_s.at[m, to], sems.at[m]).start()

        at_piece += 2 * len(units)


def arrived(own_ref, w_s, sems, m):
    pltpu.make_async_copy(own_ref.at[m], w_s.at[m], sems.at[m]).wait()


def staggered(first, second, third, lead1, lead2):
    one, two = {}, {}
    for i in range(GROUP + lead1 + lead2):
        if i < GROUP:
            one[i] = first(i)
        if 0 <= i - lead1 < GROUP:
            two[i - lead1] = second(i - lead1, *one.pop(i - lead1))
        if 0 <= i - lead1 - lead2 < GROUP:
            third(i - lead1 - lead2, *two.pop(i - lead1 - lead2))


def fill_mask(seg_ref, mask_s):
    for r in range(R):
        ids = jnp.broadcast_to(seg_ref[r].astype(F32), (L, L))
        mask_s[r] = jnp.where(ids == ids.T, 1, 0)


def attn_forward(layer, ready, dense_done, normed_ref, w_s, vec_ref, mask_s, q_ref, k_ref, v_ref, vt_s, ct_s, ctx_ref, lse_ref):
    cq, cv = vec_ref[layer, 2:3, :], vec_ref[layer, 3:4, :]

    def put_q(rows, cols, y):
        q_ref[rows, cols] = (y + cq[:, cols]).astype(BF)

    def put_k(rows, cols, y):
        k_ref[rows, cols] = y.astype(BF)

    def put_v(rows, cols, y):
        y = (y + cv[:, cols]).astype(BF)
        v_ref[rows, cols] = y
        vt_s[cols, rows] = y.T

    for m, put in enumerate((put_q, put_k, put_v)):
        ready(m)
        dense_cols(normed_ref, w_s.at[m], put)
    dense_done()

    def heads(t, c):
        r, g = t // 2, t % 2
        tok = pl.ds(pl.multiple_of(r * L, L), L)
        base = g * GW

        def score(i):
            lane0, width, at, _, _ = head_window(i)
            lanes = pl.ds(pl.multiple_of(base + lane0, 128), width)
            return (dot(k_ref[tok, lanes], q_ref[tok, lanes] * lane_mask(width, at), NT),)

        def soften(i, s):
            s = jnp.where(mask_s[r] != 0, s, NEG)
            top = jnp.max(s, axis=0, keepdims=True)
            return jnp.exp2((s - top) * C2).astype(BF), top

        def mix(i, e, top):
            _, _, _, sub0, off = head_window(i)
            own, ones = row_ones(off)
            out = dot(vt_s[pl.ds(pl.multiple_of(base + sub0, 16), 32), tok] * own + ones, e)
            tot = out[24:25] if off == 0 else out[0:1]
            ct_s[pl.ds(pl.multiple_of(base + HD * i, 8), HD), tok] = out[off:off + HD] * (1.0 / tot)
            lse_ref[pl.ds(g * GROUP + i, 1), tok] = top * C2 + jnp.log(tot) * LOG2E

        staggered(score, soften, mix, 2, 2)
        return c

    lax.fori_loop(0, 2 * R, heads, 0)
    for m in range(0, T, 256):
        for n in range(0, D, 128):
            ctx_ref[m:m + 256, n:n + 128] = ct_s[n:n + 128, m:m + 256].T.astype(BF)


VM = pl.BlockSpec(memory_space=pltpu.VMEM)
SM = pl.BlockSpec(memory_space=pltpu.SMEM)
HB = pl.BlockSpec(memory_space=pltpu.HBM)
TOK = jax.ShapeDtypeStruct((T, D), BF)
TOK_F = jax.ShapeDtypeStruct((T, D), F32)
HALF = jax.ShapeDtypeStruct((3, D // 2, D), BF)
VEC = jax.ShapeDtypeStruct((8, D), F32)
S_TOK = pltpu.VMEM((T, D), BF)
S_TOK_F = pltpu.VMEM((T, D), F32)
S_TOK_T = pltpu.VMEM((D, T), BF)
S_TOK_TF = pltpu.VMEM((D, T), F32)
S_MASK = pltpu.VMEM((R, L, L), jnp.int32)
S_W = [pltpu.VMEM((3, D, D), BF), pltpu.SemaphoreType.DMA((3,))]


def call(body, name, place, ins, weights, outs, scratch, us, mb, stash=()):
    return pl.pallas_call(
        body,
        out_shape=tuple(outs) + tuple(stash),
        in_specs=[SM] + [VM] * len(ins) + [HB] * len(weights),
        out_specs=(VM,) * len(outs) + (HB,) * len(stash),
        scratch_shapes=scratch + S_W,
        compiler_params=params(mb),
        cost_estimate=cost(us),
        name=name,
    )(place, *ins, *weights)


def attn_bwd_body(group, place_ref, normed_ref, q_ref, k_ref, v_ref, lse_ref, do_ref, seg_ref,
                  keep_ref, send_ref, gvec_ref, dq_ref, dk_ref, dv_ref,
                  nt_s, qt_s, kt_s, dot_s, dqf_s, dkf_s, dvf_s, mask_s):
    cols = slice(group * GW, group * GW + GW)
    q_ref, k_ref, v_ref, do_ref = (ref.at[:, cols] for ref in (q_ref, k_ref, v_ref, do_ref))
    fill_mask(seg_ref, mask_s)
    for src, dst in ((normed_ref, nt_s), (q_ref, qt_s), (k_ref, kt_s), (do_ref, dot_s)):
        for m in range(0, T, 256):
            for n in range(0, src.shape[1], 128):
                dst[n:n + 128, m:m + 256] = src[m:m + 256, n:n + 128].T

    def heads(r, c):
        tok = pl.ds(pl.multiple_of(r * L, L), L)

        def score(i):
            lane0, width, at, _, _ = head_window(i)
            lanes = slice(lane0, lane0 + width)
            own = lane_mask(width, at)
            return (dot(k_ref[tok, lanes], q_ref[tok, lanes] * own, NT),
                    dot(v_ref[tok, lanes], do_ref[tok, lanes] * own, NT))

        def soften(i, s, dp):
            head = group * GROUP + i
            s = jnp.where(mask_s[r] != 0, s, NEG)
            p = jnp.exp2(s * C2 - lse_ref[head:head + 1, tok])
            t1 = p * dp
            delta = jnp.sum(t1, axis=0, keepdims=True)
            return p.astype(BF), (t1 - p * delta).astype(BF)

        def mix(i, p, ds):
            _, _, _, sub0, off = head_window(i)
            sub = slice(sub0, sub0 + 32)
            out = slice(HD * i, HD * i + HD)
            dvf_s[out, tok] = dot(dot_s[sub, tok], p, NT)[off:off + HD]
            dkf_s[out, tok] = dot(qt_s[sub, tok], ds, NT)[off:off + HD] * SCALE
            dqf_s[out, tok] = dot(kt_s[sub, tok], ds, NN)[off:off + HD] * SCALE

        staggered(score, soften, mix, 1, 1)
        return c

    lax.fori_loop(0, R, heads, 0)

    def shorten(i, c):
        rows = pl.ds(pl.multiple_of(i * 64, 64), 64)
        dq_ref[rows, :] = dqf_s[rows, :].astype(BF)
        dk_ref[rows, :] = dkf_s[rows, :].astype(BF)
        dv_ref[rows, :] = dvf_s[rows, :].astype(BF)
        return c

    lax.fori_loop(0, GW // 64, shorten, 0)
    core = place_ref[1]
    mine = pl.ds(pl.multiple_of(core * 384, 128), 384)
    other = pl.ds(pl.multiple_of((1 - core) * 384, 128), 384)
    for j, grad in enumerate((dq_ref, dk_ref, dv_ref)):
        send_ref[j] = dot(nt_s[other, :], grad[...], NT).astype(BF)
        keep_ref[j] = dot(nt_s[mine, :], grad[...], NT).astype(BF)
    ones = jnp.ones((8, T), BF)
    gvec_ref[0:1, :] = dot(ones, dq_ref[...], NT)[0:1]
    gvec_ref[1:2, :] = dot(ones, dv_ref[...], NT)[0:1]


def grad_normed(own_ref, w_s, sems, grads, put):
    for m in range(3):
        arrived(own_ref, w_s, sems, m)
    for m in range(0, D, 256):
        for n in range(0, T, 256):
            y = 0.0
            for j in range(6):
                cols = slice(j // 3 * GW, j // 3 * GW + GW)
                y += dot(w_s[j % 3, m:m + 256, cols], grads[j][:, n:n + 256])
            put(slice(n, n + 256), slice(m, m + 256), y.T)


def attn_bwd_last_body(place_ref, *refs):
    ins, grads, refs = refs[:7], refs[7:10], refs[10:]
    own_ref, pieces, refs = refs[0], refs[1:1 + N_PIECES], refs[1 + N_PIECES:]
    outs, gx_ref, refs = refs[:6], refs[6], refs[7:]
    scratch, w_s, sems = refs[:-2], refs[-2], refs[-1]
    fetch(2, place_ref, own_ref, pieces, w_s, sems)
    attn_bwd_body(1, place_ref, *ins, *outs, *scratch)

    def put(rows, cols, y):
        gx_ref[rows, cols] = y.astype(BF)

    grad_normed(own_ref, w_s, sems, grads + outs[3:6], put)


def attn_bwd_last(place, normed, q, k, v, lse, grad_ctx, seg, grads, weights, name):
    part = jax.ShapeDtypeStruct((3, D // 2, GW), BF)
    grad = jax.ShapeDtypeStruct((GW, T), BF)
    s_part, s_part_f = pltpu.VMEM((GW, T), BF), pltpu.VMEM((GW, T), F32)
    return call(attn_bwd_last_body, name, place, (normed, q, k, v, lse, grad_ctx, seg, *grads), weights,
                (part, part, jax.ShapeDtypeStruct((8, GW), F32), grad, grad, grad, TOK),
                [S_TOK_T] + [s_part] * 3 + [s_part_f] * 3 + [S_MASK], 12, MB_ATTN)


def attn_bwd(group, place, normed, q, k, v, lse, grad_ctx, seg, name):
    part = jax.ShapeDtypeStruct((3, D // 2, GW), BF)
    grad = jax.ShapeDtypeStruct((GW, T), BF)
    s_part, s_part_f = pltpu.VMEM((GW, T), BF), pltpu.VMEM((GW, T), F32)
    return pl.pallas_call(
        functools.partial(attn_bwd_body, group),
        out_shape=(part, part, jax.ShapeDtypeStruct((8, GW), F32), grad, grad, grad),
        in_specs=[SM] + [VM] * 7,
        out_specs=(VM,) * 6,
        scratch_shapes=[S_TOK_T] + [s_part] * 3 + [s_part_f] * 3 + [S_MASK],
        compiler_params=params(MB_ATTN),
        cost_estimate=cost(8),
        name=name,
    )(place, normed, q, k, v, lse, grad_ctx, seg)


def inputs_bwd_body(place_ref, *rest):
    grads, (x_ref, branch_ref, vec_ref, *rest) = rest[:6], rest[6:]
    own_ref, pieces, outs, scratch, w_s, sems = split_refs(rest, 2)
    gx_ref, gvec_ref = outs
    gn_s = scratch[0]
    fetch(0, place_ref, own_ref, pieces, w_s, sems)

    def put(rows, cols, y):
        gn_s[rows, cols] = y

    grad_normed(own_ref, w_s, sems, grads, put)

    def norm_back(rows, c):
        dy = gn_s[rows, :]
        dv, dg = ln_back(x_ref[rows, :].astype(F32), vec_ref[0, 0:1, :], dy)
        gx_ref[rows, :] = (branch_ref[rows, :].astype(F32) + dv).astype(BF)
        return c[0] + fold(dg), c[1] + fold(dy)

    zero = jnp.zeros((8, D), F32)
    dg, db = row_loop(norm_back, (zero, zero))
    gvec_ref[...] = jnp.zeros(gvec_ref.shape, F32)
    gvec_ref[0:1, :] = jnp.sum(dg, axis=0, keepdims=True)
    gvec_ref[1:2, :] = jnp.sum(db, axis=0, keepdims=True)


def inputs_bwd(place, grads, x, branch, vec, weights):
    return call(inputs_bwd_body, "inputs_bwd", place, (*grads, x, branch, vec), weights, (TOK, VEC), [S_TOK_F], 4, MB_SMALL)


def ffn_forward(layer, ready, res_ref, ctx_ref, w_ref, vec_ref, hid_s, mid_s, raised_s, act_s, gp_s, sum_put):
    co, gf, bf, c1, c2 = (vec_ref[layer, i:i + 1, :] for i in range(5))

    def put_hidden(rows, cols, y):
        hid_s[rows, cols] = res_ref[rows, cols].astype(F32) + (y + co[:, cols])

    ready(0)
    dense_cols(ctx_ref, w_ref.at[0], put_hidden)

    def norm(rows, c):
        xhat, _ = ln_stats(hid_s[rows, :])
        mid_s[rows, :] = (xhat * gf + bf).astype(BF)
        return c

    row_loop(norm, unroll=4)

    def put_raised(rows, cols, y):
        a = y + c1[:, cols]
        phi = 0.5 + 0.5 * lax.erf(a * (1.0 / math.sqrt(2.0)))
        act_s[rows, cols] = (a * phi).astype(BF)
        density = jnp.exp2(a * a * (-0.5 * LOG2E)) * (1.0 / math.sqrt(2.0 * math.pi))
        gp_s[rows, cols] = phi + a * density

    ready(1)
    dense_cols(mid_s, w_ref.at[1], put_raised, NN, *GELU_BLOCK)

    def put_summed(rows, cols, y):
        sum_put(rows, cols, hid_s[rows, cols] + (y + c2[:, cols]))

    ready(2)
    dense_cols(act_s, w_ref.at[2], put_summed)


def ffn_backward(layer, ready, place_ref, gsum_s, glow_s, hid_s, gp_s, mid_s, act_s, ctx_ref, w_ref, vec_ref,
                 gbranch_ref, gctx_ref, keep_ref, send_ref, gvec_ref, graise_s, gmid_s, t_s, branch_done=lambda: None, grad_done=lambda j: None):
    gf = vec_ref[layer, 1:2, :]
    core = place_ref[1]
    mine = pl.ds(pl.multiple_of(core * 384, 128), 384)
    other = pl.ds(pl.multiple_of((1 - core) * 384, 128), 384)
    zero = jnp.zeros((8, D), F32)

    def weight_grad(j, x_ref, grad_ref):
        for m in range(0, T, 256):
            for n in range(0, D, 256):
                t_s[n:n + 256, m:m + 256] = x_ref[m:m + 256, n:n + 256].T
        for n in range(0, D, 256):
            block = grad_ref[:, n:n + 256]
            send_ref[j, :, n:n + 256] = dot(t_s[other, :], block).astype(BF)
            keep_ref[j, :, n:n + 256] = dot(t_s[mine, :], block).astype(BF)
        grad_done(j)

    def put_raised(rows, cols, y):
        graise_s[rows, cols] = (y * gp_s[rows, cols]).astype(BF)

    ready(2)
    dense_cols(glow_s, w_ref.at[2], put_raised, NT)
    weight_grad(2, act_s, glow_s)

    def put_mid(rows, cols, y):
        gmid_s[rows, cols] = y

    ready(1)
    dense_cols(graise_s, w_ref.at[1], put_mid, NT)
    weight_grad(1, mid_s, graise_s)

    def norm_back(rows, c):
        dy = gmid_s[rows, :]
        dv, dg = ln_back(hid_s[rows, :], gf, dy)
        branch = (gsum_s[rows, :].astype(F32) + dv).astype(BF)
        gbranch_ref[rows, :] = branch
        return (c[0] + fold(branch.astype(F32)), c[1] + fold(dg), c[2] + fold(dy),
                c[3] + fold(graise_s[rows, :].astype(F32)), c[4] + fold(glow_s[rows, :].astype(F32)))

    sums = row_loop(norm_back, (zero,) * 5)
    branch_done()
    for i in range(5):
        gvec_ref[i:i + 1, :] = jnp.sum(sums[i], axis=0, keepdims=True)

    def put_ctx(rows, cols, y):
        gctx_ref[rows, cols] = y.astype(BF)

    ready(0)
    dense_cols(gbranch_ref, w_ref.at[0], put_ctx, NT)
    weight_grad(0, ctx_ref, gbranch_ref)


def split_refs(rest, outs):
    at = 1 + N_PIECES
    return rest[0], rest[1:at], rest[at:at + outs], rest[at + outs:-2], rest[-2], rest[-1]


def forward_body(place_ref, av_ref, fv_ref, seg_ref, own_ref, *rest):
    pieces, rest = rest[:N_PIECES], rest[N_PIECES:]
    (x_hbm, cot_hbm, gctx_ref, gvec_ref, lse0_ref, lse1_ref,
     q0_ref, k0_ref, v0_ref, n0_ref, q1_ref, k1_ref, v1_ref, n1_ref, c0_ref, hid_ref, mid_ref, act_ref, gp_ref, sum_ref, out_ref, gb_ref,
     keep_ref, send_ref,
     q_s, k_s, v_s, n_s, vt_s, ct_s, mask_s, ctx_s, hid_s, mid_s, act_s, gp_s, raised_s, stream_s,
     w1_s, stash_sems, sems1, w0_s, sems0) = rest
    x_ref, sum_s, t_s, graise_s, gbranch_ref, out_s, cot_ref = stream_s, raised_s, vt_s, n_s, stream_s, q_s, v_s
    flying = {}

    def stash(n, src, dst):
        copy = flying[n] = pltpu.make_async_copy(src, dst, stash_sems.at[n])

        @pl.when(place_ref[0] >= 0)
        def _():
            copy.start()

    def landed(*names):
        for n in names:
            flying.pop(n).wait()

    def norm_into(src_ref, gain, offset, also=None):
        def step(rows, c):
            v = src_ref[rows, :].astype(F32)
            if also is not None:
                also[rows, :] = v.astype(BF)
            xhat, _ = ln_stats(v)
            n_s[rows, :] = (xhat * gain + offset).astype(BF)
            return c

        row_loop(step, unroll=4)

    ready0 = functools.partial(arrived, own_ref, w0_s, sems0)
    ready1 = functools.partial(arrived, own_ref, w1_s, sems1)
    stash(10, x_hbm, x_ref)
    fetch(0, place_ref, own_ref, pieces, w0_s, sems0)
    fetch(1, place_ref, own_ref, pieces, w1_s, sems1)
    landed(10)
    norm_into(x_ref, av_ref[0, 0:1, :], av_ref[0, 1:2, :])
    stash(3, n_s, n0_ref)
    fill_mask(seg_ref, mask_s)

    def dense0_done():
        fetch(2, place_ref, own_ref, pieces, w0_s, sems0)
        stash(0, q_s, q0_ref)
        stash(1, k_s, k0_ref)
        stash(2, v_s, v0_ref)

    attn_forward(0, ready0, dense0_done, n_s, w0_s, av_ref, mask_s, q_s, k_s, v_s, vt_s, ct_s, ctx_s, lse0_ref)
    stash(4, ctx_s, c0_ref)

    def put_sum(rows, cols, y):
        sum_s[rows, cols] = y

    ffn_forward(0, ready1, x_ref, ctx_s, w1_s, fv_ref, hid_s, mid_s, raised_s, act_s, gp_s, put_sum)
    fetch(3, place_ref, own_ref, pieces, w1_s, sems1)
    for n, (src, dst) in enumerate(((hid_s, hid_ref), (mid_s, mid_ref), (act_s, act_ref), (gp_s, gp_ref), (sum_s, sum_ref))):
        stash(5 + n, src, dst)
    landed(3)
    norm_into(sum_s, av_ref[1, 0:1, :], av_ref[1, 1:2, :], stream_s)
    stash(3, n_s, n1_ref)
    landed(0, 1, 2)

    def dense1_done():
        stash(0, q_s, q1_ref)
        stash(1, k_s, k1_ref)
        stash(2, v_s, v1_ref)
        landed(4)

    attn_forward(1, ready0, dense1_done, n_s, w0_s, av_ref, mask_s, q_s, k_s, v_s, vt_s, ct_s, ctx_s, lse1_ref)
    landed(0, 2, 5, 6, 7, 8, 9)
    stash(11, cot_hbm, cot_ref)

    def put_out(rows, cols, y):
        out_s[rows, cols] = y.astype(BF)

    ffn_forward(1, ready1, stream_s, ctx_s, w1_s, fv_ref, hid_s, mid_s, raised_s, act_s, gp_s, put_out)
    stash(10, out_s, out_ref)
    landed(1, 3, 11)
    gvec_ref[...] = jnp.zeros(gvec_ref.shape, F32)

    def grad_done(j):
        stash(12 + 2 * j, w0_s.at[j, 0:D // 2], keep_ref.at[j])
        stash(13 + 2 * j, w0_s.at[j, D // 2:D], send_ref.at[j])

    ffn_backward(1, lambda m: None, place_ref, cot_ref, cot_ref, hid_s, gp_s, mid_s, act_s, ctx_s, w1_s, fv_ref,
                 gbranch_ref, gctx_ref, w0_s.at[:, 0:D // 2], w0_s.at[:, D // 2:D], gvec_ref, graise_s, raised_s, t_s,
                 lambda: stash(0, gbranch_ref, gb_ref), grad_done)
    landed(0, 10, 12, 13, 14, 15, 16, 17)


def forward(place, x, av, fv, seg, cot, weights):
    lse = jax.ShapeDtypeStruct((HEADS, T), F32)
    return call(forward_body, "forward", place, (av, fv, seg), (*weights, x, cot),
                (TOK, VEC, lse, lse),
                [S_TOK] * 4 + [S_TOK_T, S_TOK_TF, S_MASK, S_TOK, S_TOK_F, S_TOK, S_TOK, S_TOK_F, S_TOK_F, S_TOK,
                 S_W[0], pltpu.SemaphoreType.DMA((18,)), S_W[1]], 40, MB_FORWARD,
                (TOK,) * 9 + (TOK_F, TOK, TOK, TOK_F, TOK_F, TOK, TOK, HALF, HALF))


def ffn_bwd_body(place_ref, gstream_ref, gnormed_ref, sum_ref, next_ref, hid_ref, gp_ref, mid_ref, act_ref, ctx_ref, vec_ref, *rest):
    own_ref, pieces, outs, scratch, w_s, sems = split_refs(rest, 6)
    gbranch_ref, gctx_ref, keep_ref, send_ref, gvec_ref, gnext_ref = outs
    gsum_s, glow_s, graise_s, gmid_s, t_s = scratch
    fetch(1, place_ref, own_ref, pieces, w_s, sems, (2, 1, 0))
    zero = jnp.zeros((8, D), F32)

    def norm_back(rows, c):
        dy = gnormed_ref[rows, :].astype(F32)
        dv, dg = ln_back(sum_ref[rows, :], next_ref[1, 0:1, :], dy)
        total = gstream_ref[rows, :].astype(F32) + dv
        gsum_s[rows, :] = total
        glow_s[rows, :] = total.astype(BF)
        return c[0] + fold(dg), c[1] + fold(dy)

    dg, db = row_loop(norm_back, (zero, zero))
    gvec_ref[...] = jnp.zeros(gvec_ref.shape, F32)
    gnext_ref[...] = jnp.zeros(gnext_ref.shape, F32)
    gnext_ref[0:1, :] = jnp.sum(dg, axis=0, keepdims=True)
    gnext_ref[1:2, :] = jnp.sum(db, axis=0, keepdims=True)
    ffn_backward(0, functools.partial(arrived, own_ref, w_s, sems), place_ref, gsum_s, glow_s, hid_ref, gp_ref, mid_ref, act_ref,
                 ctx_ref, w_s, vec_ref, gbranch_ref, gctx_ref, keep_ref, send_ref, gvec_ref, graise_s, gmid_s, t_s)


def ffn_bwd(place, gstream, gnormed, summed, nxt, hid, gp, mid, act, ctx, vec, weights):
    return call(ffn_bwd_body, "ffn_bwd", place, (gstream, gnormed, summed, nxt, hid, gp, mid, act, ctx, vec), weights,
                (TOK, TOK, HALF, HALF, VEC, VEC), [S_TOK_F, S_TOK, S_TOK, S_TOK_F, S_TOK_T], 10, MB_FFN)


def split_low(v):
    high = v.astype(BF)
    return high, (v - high.astype(F32)).astype(BF)


def combine_body(tasks, place_ref, *refs):
    refs = list(refs)
    ins = [[refs.pop(0) for _ in range(2 * pairs + rider)] for _, pairs, rider, _ in tasks]
    outs = [[refs.pop(0) for _ in range((bit is not None) + 1 + rider)] for bit, _, rider, _ in tasks]
    for (bit, pairs, rider, riding), arrays, results in zip(tasks, ins, outs):
        rows_in = arrays[0].shape[1] - (RIDE if riding == 2 else 0)
        half = rows_in // (1 if bit is None else 2)
        sent = results[0]
        for n, out_ref in enumerate(results[:2] if bit is not None else results[:1]):
            at = 0
            if bit is not None:
                at = (place_ref[bit] ^ (1 - n)) * half
            rows = pl.ds(at if bit is None else pl.multiple_of(at, half), half)
            col = 0
            for p in range(pairs):
                a_ref, b_ref = arrays[2 * p], arrays[2 * p + 1]
                width = a_ref.shape[2]
                out_ref[:, 0:half, col:col + width] = a_ref[:, rows, :] + b_ref[:, rows, :]
                col += width
        if rider:
            vec = arrays[-1][...]
            for j in range(3):
                rows = slice(8 * j, 8 * j + 8)
                out = []
                for c in range(2):
                    cols = slice(c * GW, c * GW + GW)
                    mine = vec[rows, cols]
                    if riding:
                        got = arrays[1][j, rows_in:rows_in + RIDE, :].astype(F32)
                        mine = mine + (got[16 * c:16 * c + 8] + got[16 * c + 8:16 * c + 16])
                    results[-1][rows, cols] = mine
                    out += list(split_low(mine))
                sent[j, half:half + RIDE, :] = jnp.concatenate([v.astype(F32) for v in out], axis=0).astype(BF)


def combine(place, *tasks):
    outs, kinds, ins = [], [], []
    for bit, pairs, vec, riding in tasks:
        a = pairs[0][0]
        width = sum(mine.shape[2] for mine, _ in pairs)
        rows = (a.shape[1] - (RIDE if riding == 2 else 0)) // (1 if bit is None else 2)
        ride = 0 if vec is None else RIDE
        outs.append(jax.ShapeDtypeStruct((3, rows + ride, width), BF))
        if bit is not None:
            outs.append(jax.ShapeDtypeStruct((3, rows, width), BF))
        if vec is not None:
            outs.append(jax.ShapeDtypeStruct(vec.shape, F32))
        kinds.append((bit, len(pairs), vec is not None, riding))
        ins += [x for pair in pairs for x in pair] + ([] if vec is None else [vec])
    parts = list(pl.pallas_call(
        functools.partial(combine_body, kinds),
        out_shape=tuple(outs),
        in_specs=[SM] + [VM] * len(ins),
        out_specs=tuple([VM] * len(outs)),
        compiler_params=params(MB_SMALL),
        cost_estimate=cost(0.5 * len(tasks)),
        name="combine",
    )(place, *ins))
    results = []
    for bit, _, rider, _ in kinds:
        count = (bit is not None) + 1 + rider
        results.append(tuple(parts[:count]) if count > 1 else parts[0])
        parts = parts[count:]
    return results


def add(bit, mine, got):
    return (bit, [(mine, got)], None, 0)


PARTS = {0: [(1, D, 0), (0, 0, GW)], 1: [(1, 0, 0)], 2: [(2, 0, 0)], 3: [(3, 0, 0)]}


def for_section(place_ref, distance, fn):
    for j in range(4):
        @pl.when((place_ref[0] ^ distance) == j)
        def _(j=j):
            for pair, col, to in PARTS[j]:
                width = GW if j == 0 else D
                fn(pair, slice(col, col + width), slice(to, to + width))


def pick_far_body(place_ref, *refs):
    out_ref = refs[-1]

    def put(pair, src, dst):
        out_ref[:, :, dst] = refs[pair][:, 0:D // 16, src]

    for_section(place_ref, 3, put)


def pick_far(place, *ins):
    return pl.pallas_call(
        pick_far_body,
        out_shape=jax.ShapeDtypeStruct((3, D // 16, D), BF),
        in_specs=[SM] + [VM] * 4,
        out_specs=VM,
        compiler_params=params(MB_SMALL),
        name="pick_far",
    )(place, *ins)


def pick_body(place_ref, *refs):
    half = D // 16
    for k, out_ref in enumerate(refs[8:]):
        for flipped in (0, 1):
            rows = pl.ds(pl.multiple_of((place_ref[5] ^ flipped) * half, half), half)

            def put(pair, src, dst, flipped=flipped, rows=rows, out_ref=out_ref):
                out_ref[:, rows, dst] = refs[2 * pair + flipped][:, 0:half, src]

            for_section(place_ref, k, put)


def pick(place, *ins):
    shape = jax.ShapeDtypeStruct((3, D // 8, D), BF)
    return pl.pallas_call(
        pick_body,
        out_shape=(shape,) * 3,
        in_specs=[SM] + [VM] * 8,
        out_specs=(VM,) * 3,
        compiler_params=params(MB_SMALL),
        name="pick",
    )(place, *ins)


def assemble_body(which, place_ref, *refs):
    parts, (out_ref, wide_s, sems) = refs[:len(which)], refs[-3:]
    copies = []
    for n, (c, k, chip) in enumerate(which):
        core = place_ref[1] ^ c
        section = place_ref[0] ^ k
        x_bit, y_bit = section % 2, section // 2
        row = jnp.where(core == 0, 2 * x_bit + y_bit, 2 * y_bit + x_bit)
        count = parts[n].shape[1]
        at = core * (D // 2) + row * (D // 8)
        if chip is not None:
            at = at + (place_ref[5] ^ chip) * count
        rows = pl.ds(pl.multiple_of(at, count), count)
        wide_s[n, :, 0:count, :] = parts[n][...].astype(F32)
        copy = pltpu.make_async_copy(wide_s.at[n, :, 0:count, :], out_ref.at[:, rows, :], sems.at[n])
        copies.append(copy)

        @pl.when(place_ref[0] >= 0)
        def _(copy=copy):
            copy.start()

    for copy in copies:
        copy.wait()


def assemble(place, which, parts, whole=None):
    extra = [] if whole is None else [whole]
    return pl.pallas_call(
        functools.partial(assemble_body, which),
        out_shape=jax.ShapeDtypeStruct((3, D, D), F32),
        in_specs=[SM] + [VM] * len(parts) + [HB] * len(extra),
        out_specs=HB,
        scratch_shapes=[pltpu.VMEM((len(parts), 3, D // 8, D), F32), pltpu.SemaphoreType.DMA((len(parts),))],
        input_output_aliases={1 + len(parts): 0} if extra else {},
        compiler_params=params(MB_SMALL),
        name="assemble",
    )(place, *parts, *extra)


def stack_body(norm0_ref, a0_ref, b0_ref, norm1_ref, a1_ref, b1_ref, ffn0_ref, ffn1_ref, out_ref):
    for at, norm_ref, a_ref, b_ref in ((0, norm0_ref, a0_ref, b0_ref), (4, norm1_ref, a1_ref, b1_ref)):
        out_ref[at:at + 2, :] = norm_ref[0:2, :]
        out_ref[at + 2:at + 4, 0:GW] = a_ref[0:2, :]
        out_ref[at + 2:at + 4, GW:D] = b_ref[0:2, :]
    out_ref[8:13, :] = ffn0_ref[0:5, :]
    out_ref[13:18, :] = ffn1_ref[0:5, :]
    out_ref[18:24, :] = jnp.zeros((6, D), F32)


def stack_vectors(*parts):
    return pl.pallas_call(
        stack_body,
        out_shape=jax.ShapeDtypeStruct((24, D), F32),
        in_specs=[VM] * len(parts),
        out_specs=VM,
        compiler_params=params(MB_SMALL),
        name="stack_vectors",
    )(*parts)


def unstack_body(mine_ref, other_ref, attn_ref, ffn_ref):
    for i in range(2):
        attn_ref[i] = mine_ref[4 * i:4 * i + 4, :] + other_ref[4 * i:4 * i + 4, :]
        ffn_ref[i] = mine_ref[8 + 5 * i:13 + 5 * i, :] + other_ref[8 + 5 * i:13 + 5 * i, :]


def unstack(mine, other):
    return pl.pallas_call(
        unstack_body,
        out_shape=(jax.ShapeDtypeStruct((2, 4, D), F32), jax.ShapeDtypeStruct((2, 5, D), F32)),
        in_specs=[VM] * 2,
        out_specs=(VM,) * 2,
        compiler_params=params(MB_SMALL),
        name="unstack",
    )(mine, other)


def swap_cores(value):
    count = lax.axis_size("dp")
    return lax.ppermute(value, "dp", [(i, i ^ 1) for i in range(count)])


def next_chip(value, bits):
    count = lax.axis_size("dp")
    return lax.ppermute(value, "dp", [(i, i ^ 2 * bits) for i in range(count)])


def plane_swap(value, step):
    count, sections = lax.axis_size("dp"), lax.axis_size("section")
    pairs = []
    for s in range(sections):
        for i in range(count):
            other = s ^ (1 if step == i % 2 else 2)
            pairs.append((s * count + i, other * count + i))
    return lax.ppermute(value, ("section", "dp"), pairs)


def flip(value, bits):
    count = lax.axis_size("section")
    return lax.ppermute(value, "section", [(i, i ^ bits) for i in range(count)])


def gather_pieces(own, core, par, ready):
    def part(p):
        return lax.dynamic_slice(own, (0, core * (D // 2) + p * WHOLE, 0), (3, WHOLE, D))

    mine = part(par)
    near, down = flip(mine, 1), flip(part(1 - par), 2)
    near, down, mine, *ready = together(near, down, mine, *ready)
    far_a, far_b = flip(near, 2), flip(down, 1)
    near_z, down_z, down_y = next_chip(near, 1), next_chip(down[:, :HALF_UNIT], 1), flip(mine[:, HALF_UNIT:], 2)
    mine = [[near, near_z], [down, down_z, down_y], [far_a, far_b]]
    return [piece for group in mine for piece in group + [swap_cores(x) for x in group]], ready


def line_groups():
    count = lax.axis_size("dp")
    return [[r * 8 + i for r in range(count // 8)] for i in range(8)]


def across_lines(value):
    if lax.axis_size("dp") == 8:
        return value
    return lax.psum(value.astype(F32), "dp", axis_index_groups=line_groups()).astype(value.dtype)


def together(*values):
    return lax.optimization_barrier(values)


def shards(inputs, cotangent, segments, matrices, attn_vectors, ffn_vectors):
    section = lax.axis_index("section")
    dp = lax.axis_index("dp")
    core, position = dp % 2, dp // 2
    par = position % 2
    x_bit, y_bit = section % 2, section // 2
    first = jnp.where(core == 0, x_bit, y_bit)
    second = jnp.where(core == 0, y_bit, x_bit)
    own = matrices[0]
    turn = dp // 2 % 2
    places = [jnp.stack([section ^ j, core, par, first, second, turn]).astype(jnp.int32) for j in range(4)]
    seg = lax.dynamic_slice(segments, (R * section, 0, 0), (R, 1, L))
    x = inputs.reshape(T, D)
    cot = cotangent.reshape(T, D)
    pieces, (*places, seg, cot) = gather_pieces(own, core, par, (*places, seg, cot))
    weights = (own, *pieces)
    here = places[0]
    av, fv = attn_vectors, ffn_vectors

    (gc1, gv3, l0, l1,
     q0, k0, v0, n0, q1, k1, v1, n1, c0, hid, mid, act, gp, summed, out, gb1, keep3, send3) = forward(here, x, av, fv, seg, cot, weights)
    got3 = swap_cores(send3)

    keep2a, send2a, gv2a, *grads2 = attn_bwd(0, here, n1, q1, k1, v1, l1, gc1, seg, "attn_bwd_1a")
    ((send3, keep3),) = combine(here, add(3, keep3, got3))
    send2a, send3 = together(send2a, send3)
    got3, got2a = plane_swap(send3, 0), swap_cores(send2a)
    gc1, keep3 = together(gc1, keep3)

    keep2b, send2b, gv2b, _, _, _, gn1 = attn_bwd_last(here, n1, q1, k1, v1, l1, gc1, seg, grads2, weights, "attn_bwd_1b")
    gn1, got2a, got3, send2b = together(gn1, got2a, got3, send2b)
    got2b = swap_cores(send2b)
    (send3, keep3), (send2, keep2) = combine(here, add(4, keep3, got3), (3, [(keep2a, got2a), (keep2b, got2b)], None, 0))
    got3, got2 = plane_swap(send3, 1), plane_swap(send2, 0)
    gb1, keep3 = together(gb1, keep3)

    gb0, gc0, keep1, send1, gv1, gnext = ffn_bwd(here, gb1, gn1, summed, av, hid, gp, mid, act, c0, fv, weights)
    got1 = swap_cores(send1)

    keep0a, send0a, gv0a, *grads0 = attn_bwd(0, here, n0, q0, k0, v0, l0, gc0, seg, "attn_bwd_0a")
    keep2, send0a = together(keep2, send0a)
    (send3, keep3), (send2, keep2) = combine(here, add(5, keep3, got3), add(4, keep2, got2))
    send0a, send2 = together(send0a, send2)
    got3, got2, got0a = next_chip(send3, 1), plane_swap(send2, 1), swap_cores(send0a)
    ((send1, keep1),) = combine(here, (3, [(keep1, got1), (keep0a, got0a)], None, 0))
    got1 = plane_swap(send1, 0)
    gc0, keep1 = together(gc0, keep1)

    keep0b, send0b, gv0b, *grads0b = attn_bwd(1, here, n0, q0, k0, v0, l0, gc0, seg, "attn_bwd_0b")
    send0b, keep2 = together(send0b, keep2)
    (send2, keep2), keep3 = combine(here, add(5, keep2, got2), add(None, keep3, got3))
    send0b, send2 = together(send0b, send2)
    got3, got2, got0b = next_chip(keep3, 2), next_chip(send2, 1), swap_cores(send0b)
    grads0b[0], keep2 = together(grads0b[0], keep2)

    gx, gv0n = inputs_bwd(here, (*grads0, *grads0b), x, gb0, av, weights)
    vec = stack_vectors(gv0n, gv0a, gv0b, gnext, gv2a, gv2b, gv1, gv3)
    (send0, keep0, vec), (send1, keep1), keep2, keep3 = combine(
        here, (3, [(keep0b, got0b)], vec, 0), add(4, keep1, got1), add(None, keep2, got2), add(None, keep3, got3))
    got0, got1, got2, got3 = plane_swap(send0, 0), plane_swap(send1, 1), next_chip(keep2, 2), next_chip(keep3, 1)

    got3, got0 = together(got3, got0)
    (send0, keep0, vec), (send1, keep1), keep2 = combine(
        here, (4, [(keep0, got0)], vec, 1), add(5, keep1, got1), add(None, keep2, got2))
    got0, got1, got2 = plane_swap(send0, 1), next_chip(send1, 1), next_chip(keep2, 1)

    (send0, keep0, vec), keep1 = combine(here, (5, [(keep0, got0)], vec, 1), add(None, keep1, got1))
    got0, got1 = next_chip(send0, 1), next_chip(keep1, 2)

    ((sum0, vec),) = combine(here, (None, [(keep0, got0)], vec, 1))
    got0 = next_chip(sum0, 2)

    got2, got1 = together(got2, got1)
    (keep0, vec), keep1 = combine(here, (None, [(sum0, got0)], vec, 2), add(None, keep1, got1))
    keep0, keep1, keep2, keep3 = (across_lines(v) for v in (keep0, keep1, keep2, keep3))
    far = flip(pick_far(here, keep0, keep1, keep2, keep3), 3)
    got0, got1 = next_chip(keep0, 1), next_chip(keep1, 1)
    vec = across_lines(vec)
    vec_got = swap_cores(vec)
    vec_got, far, got0, got1 = together(vec_got, far, got0, got1)
    grad_attn, grad_ffn = unstack(vec, vec_got)
    if lax.axis_size("dp") > 8:
        got2, got3 = next_chip(keep2, 1), next_chip(keep3, 1)

    grad_attn, grad_ffn, keep0 = together(grad_attn, grad_ffn, keep0)
    own_part, x_part, y_part = pick(here, keep0, got0, keep1, got1, keep2, got2, keep3, got3)
    x_part, y_part = flip(x_part, 1), flip(y_part, 2)
    far_next = next_chip(far, 1)
    own_other, far_other = swap_cores(own_part), swap_cores(far)
    far_next_other = swap_cores(far_next)
    whole = assemble(here, ((0, 0, None), (1, 0, None), (0, 3, 0), (0, 3, 1), (1, 3, 0), (1, 3, 1)),
                     (own_part, own_other, far, far_next, far_other, far_next_other))
    x_part, y_part, whole = together(x_part, y_part, whole)
    others = [swap_cores(v) for v in (x_part, y_part)]
    whole = assemble(here, ((0, 1, None), (0, 2, None)), (x_part, y_part), whole)
    whole = assemble(here, ((1, 1, None), (1, 2, None)), others, whole)
    grad_matrices = whole[None]
    shape = inputs.shape
    return (out.reshape(shape), gx.reshape(shape), grad_matrices, grad_attn, grad_ffn)


def solution(mesh):
    rows = P("section", "dp", None, None)
    mats = P("section", None, None, None)
    return jax.shard_map(
        shards,
        mesh=mesh,
        in_specs=(rows, rows, P(None, "dp", None), mats, P(), P()),
        out_specs=(rows, rows, mats, P(), P()),
        check_vma=False,
    )
```

```python
import functools
import math

import jax
import jax.numpy as jnp
from jax import lax
from jax.experimental import pallas as pl
from jax.experimental.pallas import tpu as pltpu
from jax.sharding import PartitionSpec as P

HEADS = 32
HD = 24
D = 768
L = 256
R = 2
T = R * L
EPS = 1e-05
LOG2E = math.log2(math.e)
SCALE = 1.0 / math.sqrt(HD)
C2 = LOG2E * SCALE
NEG = -1e30 * math.sqrt(HD)
BF = jnp.bfloat16
F32 = jnp.float32
GROUP = 16
GW = GROUP * HD
ROWS = 128
GELU_BLOCK = (128, 256)
MB_FORWARD, MB_ATTN, MB_FFN, MB_SMALL = 27, 16, 16, 16

WHOLE, HALF_UNIT = D // 4, D // 8
PIECES = {
    1: [(0, 0, WHOLE), (1, 0, WHOLE)],
    2: [(1, 0, WHOLE), (0, 0, HALF_UNIT), (0, HALF_UNIT, HALF_UNIT)],
    3: [(0, 0, WHOLE), (1, 0, WHOLE)],
}
N_PIECES = 2 * sum(len(p) for p in PIECES.values())
RIDE = 32

NN = (((1,), (0,)), ((), ()))
NT = (((1,), (1,)), ((), ()))


def dot(a, b, dims=NN):
    return lax.dot_general(a, b, dims, preferred_element_type=F32)


def cost(us):
    return pl.CostEstimate(flops=0, bytes_accessed=0, transcendentals=0)


def params(mb):
    return pltpu.CompilerParams(vmem_limit_bytes=mb * 1024 * 1024)


def ln_stats(v):
    center = v - jnp.mean(v, axis=-1, keepdims=True)
    spread = jnp.mean(center * center, axis=-1, keepdims=True)
    r = lax.rsqrt(spread + EPS)
    return center * r, r


def ln_back(v, gain, dy):
    xhat, r = ln_stats(v)
    e = dy * gain
    dv = r * (e - jnp.mean(e, axis=-1, keepdims=True) - xhat * jnp.mean(e * xhat, axis=-1, keepdims=True))
    return dv, dy * xhat


def fold(v):
    return jnp.sum(v.reshape(v.shape[0] // 8, 8, v.shape[1]), axis=0)


def row_loop(fn, init=0, unroll=4):
    def step(i, c):
        return fn(pl.ds(pl.multiple_of(i * ROWS, ROWS), ROWS), c)

    return lax.fori_loop(0, T // ROWS, step, init, unroll=unroll)


def head_window(i):
    start = HD * i
    lane0 = start // 128 * 128
    width = 128 if start + HD <= lane0 + 128 else 256
    sub0 = start // 16 * 16
    return lane0, width, start - lane0, sub0, start - sub0


def lane_mask(width, at):
    pos = lax.broadcasted_iota(jnp.int32, (1, width), 1)
    return jnp.where((pos >= at) & (pos < at + HD), 1.0, 0.0).astype(BF)


def row_ones(off):
    pos = lax.broadcasted_iota(jnp.int32, (32, L), 0)
    own = jnp.where((pos >= off) & (pos < off + HD), 1.0, 0.0)
    return own.astype(BF), (1.0 - own).astype(BF)


def dense_cols(lhs, w, fn, dims=NN, m_rows=256, n_cols=256):
    for n in range(0, D, n_cols):
        block = w[:, n:n + n_cols] if dims is NN else w[n:n + n_cols, :]
        for m in range(0, T, m_rows):
            fn(slice(m, m + m_rows), slice(n, n + n_cols), dot(lhs[m:m + m_rows, :], block, dims))


def fetch(section, place_ref, own_ref, piece_refs, w_s, sems, order=(0, 1, 2)):
    which, core, par = place_ref[0] ^ section, place_ref[1], place_ref[2]

    @pl.when(which == 0)
    def _():
        for m in order:
            pltpu.make_async_copy(own_ref.at[m], w_s.at[m], sems.at[m]).start()

    at_piece = 0
    for k, units in PIECES.items():
        @pl.when(which == k)
        def _(at_piece=at_piece, units=units):
            for m in order:
                for n, (c, (unit, first, rows)) in enumerate((c, u) for c in (0, 1) for u in units):
                    at = (core ^ c) * (D // 2) + (par ^ unit) * WHOLE + first
                    to = pl.ds(pl.multiple_of(at, HALF_UNIT), rows)
                    pltpu.make_async_copy(piece_refs[at_piece + n].at[m], w_s.at[m, to], sems.at[m]).start()

        at_piece += 2 * len(units)


def arrived(own_ref, w_s, sems, m):
    pltpu.make_async_copy(own_ref.at[m], w_s.at[m], sems.at[m]).wait()


def staggered(first, second, third, lead1, lead2):
    one, two = {}, {}
    for i in range(GROUP + lead1 + lead2):
        if i < GROUP:
            one[i] = first(i)
        if 0 <= i - lead1 < GROUP:
            two[i - lead1] = second(i - lead1, *one.pop(i - lead1))
        if 0 <= i - lead1 - lead2 < GROUP:
            third(i - lead1 - lead2, *two.pop(i - lead1 - lead2))


def fill_mask(seg_ref, mask_s):
    for r in range(R):
        ids = jnp.broadcast_to(seg_ref[r].astype(F32), (L, L))
        mask_s[r] = jnp.where(ids == ids.T, 1, 0)


def attn_forward(layer, ready, dense_done, normed_ref, w_s, vec_ref, mask_s, q_ref, k_ref, v_ref, vt_s, ct_s, ctx_ref, lse_ref):
    cq, cv = vec_ref[layer, 2:3, :], vec_ref[layer, 3:4, :]

    def put_q(rows, cols, y):
        q_ref[rows, cols] = (y + cq[:, cols]).astype(BF)

    def put_k(rows, cols, y):
        k_ref[rows, cols] = y.astype(BF)

    def put_v(rows, cols, y):
        y = (y + cv[:, cols]).astype(BF)
        v_ref[rows, cols] = y
        vt_s[cols, rows] = y.T

    for m, put in enumerate((put_q, put_k, put_v)):
        ready(m)
        dense_cols(normed_ref, w_s.at[m], put)
    dense_done()

    def heads(t, c):
        r, g = t // 2, t % 2
        tok = pl.ds(pl.multiple_of(r * L, L), L)
        base = g * GW

        def score(i):
            lane0, width, at, _, _ = head_window(i)
            lanes = pl.ds(pl.multiple_of(base + lane0, 128), width)
            return (dot(k_ref[tok, lanes], q_ref[tok, lanes] * lane_mask(width, at), NT),)

        def soften(i, s):
            s = jnp.where(mask_s[r] != 0, s, NEG)
            top = jnp.max(s, axis=0, keepdims=True)
            return jnp.exp2((s - top) * C2).astype(BF), top

        def mix(i, e, top):
            _, _, _, sub0, off = head_window(i)
            own, ones = row_ones(off)
            out = dot(vt_s[pl.ds(pl.multiple_of(base + sub0, 16), 32), tok] * own + ones, e)
            tot = out[24:25] if off == 0 else out[0:1]
            ct_s[pl.ds(pl.multiple_of(base + HD * i, 8), HD), tok] = out[off:off + HD] * (1.0 / tot)
            lse_ref[pl.ds(g * GROUP + i, 1), tok] = top * C2 + jnp.log(tot) * LOG2E

        staggered(score, soften, mix, 2, 2)
        return c

    lax.fori_loop(0, 2 * R, heads, 0)
    for m in range(0, T, 256):
        for n in range(0, D, 128):
            ctx_ref[m:m + 256, n:n + 128] = ct_s[n:n + 128, m:m + 256].T.astype(BF)


VM = pl.BlockSpec(memory_space=pltpu.VMEM)
SM = pl.BlockSpec(memory_space=pltpu.SMEM)
HB = pl.BlockSpec(memory_space=pltpu.HBM)
TOK = jax.ShapeDtypeStruct((T, D), BF)
TOK_F = jax.ShapeDtypeStruct((T, D), F32)
HALF = jax.ShapeDtypeStruct((3, D // 2, D), BF)
VEC = jax.ShapeDtypeStruct((8, D), F32)
S_TOK = pltpu.VMEM((T, D), BF)
S_TOK_F = pltpu.VMEM((T, D), F32)
S_TOK_T = pltpu.VMEM((D, T), BF)
S_TOK_TF = pltpu.VMEM((D, T), F32)
S_MASK = pltpu.VMEM((R, L, L), jnp.int32)
S_W = [pltpu.VMEM((3, D, D), BF), pltpu.SemaphoreType.DMA((3,))]


def call(body, name, place, ins, weights, outs, scratch, us, mb, stash=()):
    return pl.pallas_call(
        body,
        out_shape=tuple(outs) + tuple(stash),
        in_specs=[SM] + [VM] * len(ins) + [HB] * len(weights),
        out_specs=(VM,) * len(outs) + (HB,) * len(stash),
        scratch_shapes=scratch + S_W,
        compiler_params=params(mb),
        cost_estimate=cost(us),
        name=name,
    )(place, *ins, *weights)


def attn_bwd_body(group, place_ref, normed_ref, q_ref, k_ref, v_ref, lse_ref, do_ref, seg_ref,
                  keep_ref, send_ref, gvec_ref, dq_ref, dk_ref, dv_ref,
                  nt_s, qt_s, kt_s, dot_s, dqf_s, dkf_s, dvf_s, mask_s):
    cols = slice(group * GW, group * GW + GW)
    q_ref, k_ref, v_ref, do_ref = (ref.at[:, cols] for ref in (q_ref, k_ref, v_ref, do_ref))
    fill_mask(seg_ref, mask_s)
    for src, dst in ((normed_ref, nt_s), (q_ref, qt_s), (k_ref, kt_s), (do_ref, dot_s)):
        for m in range(0, T, 256):
            for n in range(0, src.shape[1], 128):
                dst[n:n + 128, m:m + 256] = src[m:m + 256, n:n + 128].T

    def heads(r, c):
        tok = pl.ds(pl.multiple_of(r * L, L), L)

        def score(i):
            lane0, width, at, _, _ = head_window(i)
            lanes = slice(lane0, lane0 + width)
            own = lane_mask(width, at)
            return (dot(k_ref[tok, lanes], q_ref[tok, lanes] * own, NT),
                    dot(v_ref[tok, lanes], do_ref[tok, lanes] * own, NT))

        def soften(i, s, dp):
            head = group * GROUP + i
            s = jnp.where(mask_s[r] != 0, s, NEG)
            p = jnp.exp2(s * C2 - lse_ref[head:head + 1, tok])
            t1 = p * dp
            delta = jnp.sum(t1, axis=0, keepdims=True)
            return p.astype(BF), (t1 - p * delta).astype(BF)

        def mix(i, p, ds):
            _, _, _, sub0, off = head_window(i)
            sub = slice(sub0, sub0 + 32)
            out = slice(HD * i, HD * i + HD)
            dvf_s[out, tok] = dot(dot_s[sub, tok], p, NT)[off:off + HD]
            dkf_s[out, tok] = dot(qt_s[sub, tok], ds, NT)[off:off + HD] * SCALE
            dqf_s[out, tok] = dot(kt_s[sub, tok], ds, NN)[off:off + HD] * SCALE

        staggered(score, soften, mix, 1, 1)
        return c

    lax.fori_loop(0, R, heads, 0)

    def shorten(i, c):
        rows = pl.ds(pl.multiple_of(i * 64, 64), 64)
        dq_ref[rows, :] = dqf_s[rows, :].astype(BF)
        dk_ref[rows, :] = dkf_s[rows, :].astype(BF)
        dv_ref[rows, :] = dvf_s[rows, :].astype(BF)
        return c

    lax.fori_loop(0, GW // 64, shorten, 0)
    core = place_ref[1]
    mine = pl.ds(pl.multiple_of(core * 384, 128), 384)
    other = pl.ds(pl.multiple_of((1 - core) * 384, 128), 384)
    for j, grad in enumerate((dq_ref, dk_ref, dv_ref)):
        send_ref[j] = dot(nt_s[other, :], grad[...], NT).astype(BF)
        keep_ref[j] = dot(nt_s[mine, :], grad[...], NT).astype(BF)
    ones = jnp.ones((8, T), BF)
    gvec_ref[0:1, :] = dot(ones, dq_ref[...], NT)[0:1]
    gvec_ref[1:2, :] = dot(ones, dv_ref[...], NT)[0:1]


def grad_normed(own_ref, w_s, sems, grads, put):
    for m in range(3):
        arrived(own_ref, w_s, sems, m)
    for m in range(0, D, 256):
        for n in range(0, T, 256):
            y = 0.0
            for j in range(6):
                cols = slice(j // 3 * GW, j // 3 * GW + GW)
                y += dot(w_s[j % 3, m:m + 256, cols], grads[j][:, n:n + 256])
            put(slice(n, n + 256), slice(m, m + 256), y.T)


def attn_bwd_last_body(place_ref, *refs):
    ins, grads, refs = refs[:7], refs[7:10], refs[10:]
    own_ref, pieces, refs = refs[0], refs[1:1 + N_PIECES], refs[1 + N_PIECES:]
    outs, gx_ref, refs = refs[:6], refs[6], refs[7:]
    scratch, w_s, sems = refs[:-2], refs[-2], refs[-1]
    fetch(2, place_ref, own_ref, pieces, w_s, sems)
    attn_bwd_body(1, place_ref, *ins, *outs, *scratch)

    def put(rows, cols, y):
        gx_ref[rows, cols] = y.astype(BF)

    grad_normed(own_ref, w_s, sems, grads + outs[3:6], put)


def attn_bwd_last(place, normed, q, k, v, lse, grad_ctx, seg, grads, weights, name):
    part = jax.ShapeDtypeStruct((3, D // 2, GW), BF)
    grad = jax.ShapeDtypeStruct((GW, T), BF)
    s_part, s_part_f = pltpu.VMEM((GW, T), BF), pltpu.VMEM((GW, T), F32)
    return call(attn_bwd_last_body, name, place, (normed, q, k, v, lse, grad_ctx, seg, *grads), weights,
                (part, part, jax.ShapeDtypeStruct((8, GW), F32), grad, grad, grad, TOK),
                [S_TOK_T] + [s_part] * 3 + [s_part_f] * 3 + [S_MASK], 12, MB_ATTN)


def attn_bwd(group, place, normed, q, k, v, lse, grad_ctx, seg, name):
    part = jax.ShapeDtypeStruct((3, D // 2, GW), BF)
    grad = jax.ShapeDtypeStruct((GW, T), BF)
    s_part, s_part_f = pltpu.VMEM((GW, T), BF), pltpu.VMEM((GW, T), F32)
    return pl.pallas_call(
        functools.partial(attn_bwd_body, group),
        out_shape=(part, part, jax.ShapeDtypeStruct((8, GW), F32), grad, grad, grad),
        in_specs=[SM] + [VM] * 7,
        out_specs=(VM,) * 6,
        scratch_shapes=[S_TOK_T] + [s_part] * 3 + [s_part_f] * 3 + [S_MASK],
        compiler_params=params(MB_ATTN),
        cost_estimate=cost(8),
        name=name,
    )(place, normed, q, k, v, lse, grad_ctx, seg)


def inputs_bwd_body(place_ref, *rest):
    grads, (x_ref, branch_ref, vec_ref, *rest) = rest[:6], rest[6:]
    own_ref, pieces, outs, scratch, w_s, sems = split_refs(rest, 2)
    gx_ref, gvec_ref = outs
    gn_s = scratch[0]
    fetch(0, place_ref, own_ref, pieces, w_s, sems)

    def put(rows, cols, y):
        gn_s[rows, cols] = y

    grad_normed(own_ref, w_s, sems, grads, put)

    def norm_back(rows, c):
        dy = gn_s[rows, :]
        dv, dg = ln_back(x_ref[rows, :].astype(F32), vec_ref[0, 0:1, :], dy)
        gx_ref[rows, :] = (branch_ref[rows, :].astype(F32) + dv).astype(BF)
        return c[0] + fold(dg), c[1] + fold(dy)

    zero = jnp.zeros((8, D), F32)
    dg, db = row_loop(norm_back, (zero, zero))
    gvec_ref[...] = jnp.zeros(gvec_ref.shape, F32)
    gvec_ref[0:1, :] = jnp.sum(dg, axis=0, keepdims=True)
    gvec_ref[1:2, :] = jnp.sum(db, axis=0, keepdims=True)


def inputs_bwd(place, grads, x, branch, vec, weights):
    return call(inputs_bwd_body, "inputs_bwd", place, (*grads, x, branch, vec), weights, (TOK, VEC), [S_TOK_F], 4, MB_SMALL)


def ffn_forward(layer, ready, res_ref, ctx_ref, w_ref, vec_ref, hid_s, mid_s, raised_s, act_s, gp_s, sum_put):
    co, gf, bf, c1, c2 = (vec_ref[layer, i:i + 1, :] for i in range(5))

    def put_hidden(rows, cols, y):
        hid_s[rows, cols] = res_ref[rows, cols].astype(F32) + (y + co[:, cols])

    ready(0)
    dense_cols(ctx_ref, w_ref.at[0], put_hidden)

    def norm(rows, c):
        xhat, _ = ln_stats(hid_s[rows, :])
        mid_s[rows, :] = (xhat * gf + bf).astype(BF)
        return c

    row_loop(norm)

    def put_raised(rows, cols, y):
        a = y + c1[:, cols]
        phi = 0.5 + 0.5 * lax.erf(a * (1.0 / math.sqrt(2.0)))
        act_s[rows, cols] = (a * phi).astype(BF)
        density = jnp.exp2(a * a * (-0.5 * LOG2E)) * (1.0 / math.sqrt(2.0 * math.pi))
        gp_s[rows, cols] = phi + a * density

    ready(1)
    dense_cols(mid_s, w_ref.at[1], put_raised, NN, *GELU_BLOCK)

    def put_summed(rows, cols, y):
        sum_put(rows, cols, hid_s[rows, cols] + (y + c2[:, cols]))

    ready(2)
    dense_cols(act_s, w_ref.at[2], put_summed)


def ffn_backward(layer, ready, place_ref, gsum_s, glow_s, hid_s, gp_s, mid_s, act_s, ctx_ref, w_ref, vec_ref,
                 gbranch_ref, gctx_ref, keep_ref, send_ref, gvec_ref, graise_s, gmid_s, t_s, branch_done=lambda: None, grad_done=lambda j: None):
    gf = vec_ref[layer, 1:2, :]
    core = place_ref[1]
    mine = pl.ds(pl.multiple_of(core * 384, 128), 384)
    other = pl.ds(pl.multiple_of((1 - core) * 384, 128), 384)
    zero = jnp.zeros((8, D), F32)

    def weight_grad(j, x_ref, grad_ref):
        for m in range(0, T, 256):
            for n in range(0, D, 256):
                t_s[n:n + 256, m:m + 256] = x_ref[m:m + 256, n:n + 256].T
        for n in range(0, D, 256):
            block = grad_ref[:, n:n + 256]
            send_ref[j, :, n:n + 256] = dot(t_s[other, :], block).astype(BF)
            keep_ref[j, :, n:n + 256] = dot(t_s[mine, :], block).astype(BF)
        grad_done(j)

    def put_raised(rows, cols, y):
        graise_s[rows, cols] = (y * gp_s[rows, cols]).astype(BF)

    ready(2)
    dense_cols(glow_s, w_ref.at[2], put_raised, NT)
    weight_grad(2, act_s, glow_s)

    def put_mid(rows, cols, y):
        gmid_s[rows, cols] = y

    ready(1)
    dense_cols(graise_s, w_ref.at[1], put_mid, NT)
    weight_grad(1, mid_s, graise_s)

    def norm_back(rows, c):
        dy = gmid_s[rows, :]
        dv, dg = ln_back(hid_s[rows, :], gf, dy)
        branch = (gsum_s[rows, :].astype(F32) + dv).astype(BF)
        gbranch_ref[rows, :] = branch
        return (c[0] + fold(branch.astype(F32)), c[1] + fold(dg), c[2] + fold(dy),
                c[3] + fold(graise_s[rows, :].astype(F32)), c[4] + fold(glow_s[rows, :].astype(F32)))

    sums = row_loop(norm_back, (zero,) * 5, 1)
    branch_done()
    for i in range(5):
        gvec_ref[i:i + 1, :] = jnp.sum(sums[i], axis=0, keepdims=True)

    def put_ctx(rows, cols, y):
        gctx_ref[rows, cols] = y.astype(BF)

    ready(0)
    dense_cols(gbranch_ref, w_ref.at[0], put_ctx, NT)
    weight_grad(0, ctx_ref, gbranch_ref)


def split_refs(rest, outs):
    at = 1 + N_PIECES
    return rest[0], rest[1:at], rest[at:at + outs], rest[at + outs:-2], rest[-2], rest[-1]


def forward_body(place_ref, av_ref, fv_ref, seg_ref, own_ref, *rest):
    pieces, rest = rest[:N_PIECES], rest[N_PIECES:]
    (x_hbm, cot_hbm, gctx_ref, gvec_ref, lse0_ref, lse1_ref,
     q0_ref, k0_ref, v0_ref, n0_ref, q1_ref, k1_ref, v1_ref, n1_ref, c0_ref, hid_ref, mid_ref, act_ref, gp_ref, sum_ref, out_ref, gb_ref,
     keep_ref, send_ref,
     q_s, k_s, v_s, n_s, vt_s, ct_s, mask_s, ctx_s, hid_s, mid_s, act_s, gp_s, raised_s, stream_s,
     w1_s, stash_sems, sems1, w0_s, sems0) = rest
    x_ref, sum_s, t_s, graise_s, gbranch_ref, out_s, cot_ref = stream_s, raised_s, vt_s, n_s, stream_s, q_s, v_s
    flying = {}

    def stash(n, src, dst):
        copy = flying[n] = pltpu.make_async_copy(src, dst, stash_sems.at[n])

        @pl.when(place_ref[0] >= 0)
        def _():
            copy.start()

    def landed(*names):
        for n in names:
            flying.pop(n).wait()

    def norm_into(src_ref, gain, offset, also=None):
        def step(rows, c):
            v = src_ref[rows, :].astype(F32)
            if also is not None:
                also[rows, :] = v.astype(BF)
            xhat, _ = ln_stats(v)
            n_s[rows, :] = (xhat * gain + offset).astype(BF)
            return c

        row_loop(step)

    ready0 = functools.partial(arrived, own_ref, w0_s, sems0)
    ready1 = functools.partial(arrived, own_ref, w1_s, sems1)
    stash(10, x_hbm, x_ref)
    fetch(0, place_ref, own_ref, pieces, w0_s, sems0)
    fetch(1, place_ref, own_ref, pieces, w1_s, sems1)
    landed(10)
    norm_into(x_ref, av_ref[0, 0:1, :], av_ref[0, 1:2, :])
    stash(3, n_s, n0_ref)
    fill_mask(seg_ref, mask_s)

    def dense0_done():
        fetch(2, place_ref, own_ref, pieces, w0_s, sems0)
        stash(0, q_s, q0_ref)
        stash(1, k_s, k0_ref)
        stash(2, v_s, v0_ref)

    attn_forward(0, ready0, dense0_done, n_s, w0_s, av_ref, mask_s, q_s, k_s, v_s, vt_s, ct_s, ctx_s, lse0_ref)
    stash(4, ctx_s, c0_ref)

    def put_sum(rows, cols, y):
        sum_s[rows, cols] = y

    ffn_forward(0, ready1, x_ref, ctx_s, w1_s, fv_ref, hid_s, mid_s, raised_s, act_s, gp_s, put_sum)
    fetch(3, place_ref, own_ref, pieces, w1_s, sems1)
    for n, (src, dst) in enumerate(((hid_s, hid_ref), (mid_s, mid_ref), (act_s, act_ref), (gp_s, gp_ref), (sum_s, sum_ref))):
        stash(5 + n, src, dst)
    landed(3)
    norm_into(sum_s, av_ref[1, 0:1, :], av_ref[1, 1:2, :], stream_s)
    stash(3, n_s, n1_ref)
    landed(0, 1, 2)

    def dense1_done():
        stash(0, q_s, q1_ref)
        stash(1, k_s, k1_ref)
        stash(2, v_s, v1_ref)
        landed(4)

    attn_forward(1, ready0, dense1_done, n_s, w0_s, av_ref, mask_s, q_s, k_s, v_s, vt_s, ct_s, ctx_s, lse1_ref)
    landed(0, 2, 5, 6, 7, 8, 9)
    stash(11, cot_hbm, cot_ref)

    def put_out(rows, cols, y):
        out_s[rows, cols] = y.astype(BF)

    ffn_forward(1, ready1, stream_s, ctx_s, w1_s, fv_ref, hid_s, mid_s, raised_s, act_s, gp_s, put_out)
    stash(10, out_s, out_ref)
    landed(1, 3, 11)
    gvec_ref[...] = jnp.zeros(gvec_ref.shape, F32)

    def grad_done(j):
        stash(12 + 2 * j, w0_s.at[j, 0:D // 2], keep_ref.at[j])
        stash(13 + 2 * j, w0_s.at[j, D // 2:D], send_ref.at[j])

    ffn_backward(1, lambda m: None, place_ref, cot_ref, cot_ref, hid_s, gp_s, mid_s, act_s, ctx_s, w1_s, fv_ref,
                 gbranch_ref, gctx_ref, w0_s.at[:, 0:D // 2], w0_s.at[:, D // 2:D], gvec_ref, graise_s, raised_s, t_s,
                 lambda: stash(0, gbranch_ref, gb_ref), grad_done)
    landed(0, 10, 12, 13, 14, 15, 16, 17)


def forward(place, x, av, fv, seg, cot, weights):
    lse = jax.ShapeDtypeStruct((HEADS, T), F32)
    return call(forward_body, "forward", place, (av, fv, seg), (*weights, x, cot),
                (TOK, VEC, lse, lse),
                [S_TOK] * 4 + [S_TOK_T, S_TOK_TF, S_MASK, S_TOK, S_TOK_F, S_TOK, S_TOK, S_TOK_F, S_TOK_F, S_TOK,
                 S_W[0], pltpu.SemaphoreType.DMA((18,)), S_W[1]], 40, MB_FORWARD,
                (TOK,) * 9 + (TOK_F, TOK, TOK, TOK_F, TOK_F, TOK, TOK, HALF, HALF))


def ffn_bwd_body(place_ref, gstream_ref, gnormed_ref, sum_ref, next_ref, hid_ref, gp_ref, mid_ref, act_ref, ctx_ref, vec_ref, *rest):
    own_ref, pieces, outs, scratch, w_s, sems = split_refs(rest, 6)
    gbranch_ref, gctx_ref, keep_ref, send_ref, gvec_ref, gnext_ref = outs
    gsum_s, glow_s, graise_s, gmid_s, t_s = scratch
    fetch(1, place_ref, own_ref, pieces, w_s, sems, (2, 1, 0))
    zero = jnp.zeros((8, D), F32)

    def norm_back(rows, c):
        dy = gnormed_ref[rows, :].astype(F32)
        dv, dg = ln_back(sum_ref[rows, :], next_ref[1, 0:1, :], dy)
        total = gstream_ref[rows, :].astype(F32) + dv
        gsum_s[rows, :] = total
        glow_s[rows, :] = total.astype(BF)
        return c[0] + fold(dg), c[1] + fold(dy)

    dg, db = row_loop(norm_back, (zero, zero))
    gvec_ref[...] = jnp.zeros(gvec_ref.shape, F32)
    gnext_ref[...] = jnp.zeros(gnext_ref.shape, F32)
    gnext_ref[0:1, :] = jnp.sum(dg, axis=0, keepdims=True)
    gnext_ref[1:2, :] = jnp.sum(db, axis=0, keepdims=True)
    ffn_backward(0, functools.partial(arrived, own_ref, w_s, sems), place_ref, gsum_s, glow_s, hid_ref, gp_ref, mid_ref, act_ref,
                 ctx_ref, w_s, vec_ref, gbranch_ref, gctx_ref, keep_ref, send_ref, gvec_ref, graise_s, gmid_s, t_s)


def ffn_bwd(place, gstream, gnormed, summed, nxt, hid, gp, mid, act, ctx, vec, weights):
    return call(ffn_bwd_body, "ffn_bwd", place, (gstream, gnormed, summed, nxt, hid, gp, mid, act, ctx, vec), weights,
                (TOK, TOK, HALF, HALF, VEC, VEC), [S_TOK_F, S_TOK, S_TOK, S_TOK_F, S_TOK_T], 10, MB_FFN)


def split_low(v):
    high = v.astype(BF)
    return high, (v - high.astype(F32)).astype(BF)


def combine_body(tasks, far, place_ref, *refs):
    refs = list(refs)
    far_refs, refs = refs[:far], refs[far:]
    far_out = refs.pop() if far else None
    ins = [[refs.pop(0) for _ in range(2 * pairs + rider)] for _, pairs, rider, _ in tasks]
    outs = [[refs.pop(0) for _ in range((bit is not None) + 1 + rider)] for bit, _, rider, _ in tasks]
    for (bit, pairs, rider, riding), arrays, results in zip(tasks, ins, outs):
        rows_in = arrays[0].shape[1] - (RIDE if riding == 2 else 0)
        half = rows_in // (1 if bit is None else 2)
        sent = results[0]
        for n, out_ref in enumerate(results[:2] if bit is not None else results[:1]):
            at = 0
            if bit is not None:
                at = (place_ref[bit] ^ (1 - n)) * half
            rows = pl.ds(at if bit is None else pl.multiple_of(at, half), half)
            col = 0
            for p in range(pairs):
                a_ref, b_ref = arrays[2 * p], arrays[2 * p + 1]
                width = a_ref.shape[2]
                out_ref[:, 0:half, col:col + width] = a_ref[:, rows, :] + b_ref[:, rows, :]
                col += width
        if rider:
            vec = arrays[-1][...]
            for j in range(3):
                rows = slice(8 * j, 8 * j + 8)
                out = []
                for c in range(2):
                    cols = slice(c * GW, c * GW + GW)
                    mine = vec[rows, cols]
                    if riding:
                        got = arrays[1][j, rows_in:rows_in + RIDE, :].astype(F32)
                        mine = mine + (got[16 * c:16 * c + 8] + got[16 * c + 8:16 * c + 16])
                    results[-1][rows, cols] = mine
                    out += list(split_low(mine))
                sent[j, half:half + RIDE, :] = jnp.concatenate([v.astype(F32) for v in out], axis=0).astype(BF)
    if far:
        sums = [outs[0][0], outs[1][0], *far_refs]

        def put(pair, src, dst):
            far_out[:, :, dst] = sums[pair][:, 0:D // 16, src]

        for_section(place_ref, 3, put)


def combine(place, *tasks, far=()):
    outs, kinds, ins = [], [], []
    for bit, pairs, vec, riding in tasks:
        a = pairs[0][0]
        width = sum(mine.shape[2] for mine, _ in pairs)
        rows = (a.shape[1] - (RIDE if riding == 2 else 0)) // (1 if bit is None else 2)
        ride = 0 if vec is None else RIDE
        outs.append(jax.ShapeDtypeStruct((3, rows + ride, width), BF))
        if bit is not None:
            outs.append(jax.ShapeDtypeStruct((3, rows, width), BF))
        if vec is not None:
            outs.append(jax.ShapeDtypeStruct(vec.shape, F32))
        kinds.append((bit, len(pairs), vec is not None, riding))
        ins += [x for pair in pairs for x in pair] + ([] if vec is None else [vec])
    if far:
        outs.append(jax.ShapeDtypeStruct((3, D // 16, D), BF))
    parts = list(pl.pallas_call(
        functools.partial(combine_body, kinds, len(far)),
        out_shape=tuple(outs),
        in_specs=[SM] + [VM] * (len(far) + len(ins)),
        out_specs=tuple([VM] * len(outs)),
        compiler_params=params(MB_SMALL),
        cost_estimate=cost(0.5 * len(tasks)),
        name="combine",
    )(place, *far, *ins))
    results = []
    for bit, _, rider, _ in kinds:
        count = (bit is not None) + 1 + rider
        results.append(tuple(parts[:count]) if count > 1 else parts[0])
        parts = parts[count:]
    return results + parts


def add(bit, mine, got):
    return (bit, [(mine, got)], None, 0)


PARTS = {0: [(1, D, 0), (0, 0, GW)], 1: [(1, 0, 0)], 2: [(2, 0, 0)], 3: [(3, 0, 0)]}


def for_section(place_ref, distance, fn):
    for j in range(4):
        @pl.when((place_ref[0] ^ distance) == j)
        def _(j=j):
            for pair, col, to in PARTS[j]:
                width = GW if j == 0 else D
                fn(pair, slice(col, col + width), slice(to, to + width))


def pick_body(place_ref, *refs):
    half = D // 16
    for k, out_ref in enumerate(refs[8:]):
        for flipped in (0, 1):
            rows = pl.ds(pl.multiple_of((place_ref[5] ^ flipped) * half, half), half)

            def put(pair, src, dst, flipped=flipped, rows=rows, out_ref=out_ref):
                out_ref[:, rows, dst] = refs[2 * pair + flipped][:, 0:half, src]

            for_section(place_ref, k, put)


def pick(place, *ins):
    shape = jax.ShapeDtypeStruct((3, D // 8, D), BF)
    return pl.pallas_call(
        pick_body,
        out_shape=(shape,) * 3,
        in_specs=[SM] + [VM] * 8,
        out_specs=(VM,) * 3,
        compiler_params=params(MB_SMALL),
        name="pick",
    )(place, *ins)


def assemble_body(which, place_ref, *refs):
    parts, (out_ref, wide_s, sems) = refs[:len(which)], refs[-3:]
    copies = []
    for n, (c, k, chip) in enumerate(which):
        core = place_ref[1] ^ c
        section = place_ref[0] ^ k
        x_bit, y_bit = section % 2, section // 2
        row = jnp.where(core == 0, 2 * x_bit + y_bit, 2 * y_bit + x_bit)
        count = parts[n].shape[1]
        at = core * (D // 2) + row * (D // 8)
        if chip is not None:
            at = at + (place_ref[5] ^ chip) * count
        rows = pl.ds(pl.multiple_of(at, count), count)
        wide_s[n, :, 0:count, :] = parts[n][...].astype(F32)
        copy = pltpu.make_async_copy(wide_s.at[n, :, 0:count, :], out_ref.at[:, rows, :], sems.at[n])
        copies.append(copy)

        @pl.when(place_ref[0] >= 0)
        def _(copy=copy):
            copy.start()

    for copy in copies:
        copy.wait()


def assemble(place, which, parts, whole=None):
    extra = [] if whole is None else [whole]
    return pl.pallas_call(
        functools.partial(assemble_body, which),
        out_shape=jax.ShapeDtypeStruct((3, D, D), F32),
        in_specs=[SM] + [VM] * len(parts) + [HB] * len(extra),
        out_specs=HB,
        scratch_shapes=[pltpu.VMEM((len(parts), 3, D // 8, D), F32), pltpu.SemaphoreType.DMA((len(parts),))],
        input_output_aliases={1 + len(parts): 0} if extra else {},
        compiler_params=params(MB_SMALL),
        name="assemble",
    )(place, *parts, *extra)


def stack_body(norm0_ref, a0_ref, b0_ref, norm1_ref, a1_ref, b1_ref, ffn0_ref, ffn1_ref, out_ref):
    for at, norm_ref, a_ref, b_ref in ((0, norm0_ref, a0_ref, b0_ref), (4, norm1_ref, a1_ref, b1_ref)):
        out_ref[at:at + 2, :] = norm_ref[0:2, :]
        out_ref[at + 2:at + 4, 0:GW] = a_ref[0:2, :]
        out_ref[at + 2:at + 4, GW:D] = b_ref[0:2, :]
    out_ref[8:13, :] = ffn0_ref[0:5, :]
    out_ref[13:18, :] = ffn1_ref[0:5, :]
    out_ref[18:24, :] = jnp.zeros((6, D), F32)


def stack_vectors(*parts):
    return pl.pallas_call(
        stack_body,
        out_shape=jax.ShapeDtypeStruct((24, D), F32),
        in_specs=[VM] * len(parts),
        out_specs=VM,
        compiler_params=params(MB_SMALL),
        name="stack_vectors",
    )(*parts)


def unstack_body(mine_ref, other_ref, attn_ref, ffn_ref):
    for i in range(2):
        attn_ref[i] = mine_ref[4 * i:4 * i + 4, :] + other_ref[4 * i:4 * i + 4, :]
        for j in range(5):
            row = slice(8 + 5 * i + j, 9 + 5 * i + j)
            ffn_ref[j, i:i + 1, :] = mine_ref[row, :] + other_ref[row, :]


def unstack(mine, other):
    return pl.pallas_call(
        unstack_body,
        out_shape=(jax.ShapeDtypeStruct((2, 4, D), F32), jax.ShapeDtypeStruct((5, 2, D), F32)),
        in_specs=[VM] * 2,
        out_specs=(VM,) * 2,
        compiler_params=params(MB_SMALL),
        name="unstack",
    )(mine, other)


def swap_cores(value):
    count = lax.axis_size("dp")
    return lax.ppermute(value, "dp", [(i, i ^ 1) for i in range(count)])


def next_chip(value, bits):
    count = lax.axis_size("dp")
    return lax.ppermute(value, "dp", [(i, i ^ 2 * bits) for i in range(count)])


def plane_swap(value, step):
    count, sections = lax.axis_size("dp"), lax.axis_size("section")
    pairs = []
    for s in range(sections):
        for i in range(count):
            other = s ^ (1 if step == i % 2 else 2)
            pairs.append((s * count + i, other * count + i))
    return lax.ppermute(value, ("section", "dp"), pairs)


def flip(value, bits):
    count = lax.axis_size("section")
    return lax.ppermute(value, "section", [(i, i ^ bits) for i in range(count)])


def gather_pieces(own, core, par, ready):
    def part(p):
        return lax.dynamic_slice(own, (0, core * (D // 2) + p * WHOLE, 0), (3, WHOLE, D))

    mine = part(par)
    near, down = flip(mine, 1), flip(part(1 - par), 2)
    near, down, mine, *ready = together(near, down, mine, *ready)
    far_a, far_b = flip(near, 2), flip(down, 1)
    near_z, down_z, down_y = next_chip(near, 1), next_chip(down[:, :HALF_UNIT], 1), flip(mine[:, HALF_UNIT:], 2)
    mine = [[near, near_z], [down, down_z, down_y], [far_a, far_b]]
    return [piece for group in mine for piece in group + [swap_cores(x) for x in group]], ready


def line_groups():
    count = lax.axis_size("dp")
    return [[r * 8 + i for r in range(count // 8)] for i in range(8)]


def across_lines(value):
    if lax.axis_size("dp") == 8:
        return value
    return lax.psum(value.astype(F32), "dp", axis_index_groups=line_groups()).astype(value.dtype)


def together(*values):
    return lax.optimization_barrier(values)


def shards(inputs, cotangent, segments, matrices, attn_vectors, ffn_vectors):
    section = lax.axis_index("section")
    dp = lax.axis_index("dp")
    core, position = dp % 2, dp // 2
    par = position % 2
    x_bit, y_bit = section % 2, section // 2
    first = jnp.where(core == 0, x_bit, y_bit)
    second = jnp.where(core == 0, y_bit, x_bit)
    own = matrices[0]
    turn = dp // 2 % 2
    places = [jnp.stack([section ^ j, core, par, first, second, turn]).astype(jnp.int32) for j in range(4)]
    seg = lax.dynamic_slice(segments, (R * section, 0, 0), (R, 1, L))
    x = inputs.reshape(T, D)
    cot = cotangent.reshape(T, D)
    pieces, (*places, seg, cot) = gather_pieces(own, core, par, (*places, seg, cot))
    weights = (own, *pieces)
    here = places[0]
    av, fv = attn_vectors, ffn_vectors

    (gc1, gv3, l0, l1,
     q0, k0, v0, n0, q1, k1, v1, n1, c0, hid, mid, act, gp, summed, out, gb1, keep3, send3) = forward(here, x, av, fv, seg, cot, weights)
    got3 = swap_cores(send3)

    keep2a, send2a, gv2a, *grads2 = attn_bwd(0, here, n1, q1, k1, v1, l1, gc1, seg, "attn_bwd_1a")
    ((send3, keep3),) = combine(here, add(3, keep3, got3))
    send2a, send3 = together(send2a, send3)
    got3, got2a = plane_swap(send3, 0), swap_cores(send2a)
    gc1, keep3 = together(gc1, keep3)

    keep2b, send2b, gv2b, _, _, _, gn1 = attn_bwd_last(here, n1, q1, k1, v1, l1, gc1, seg, grads2, weights, "attn_bwd_1b")
    gn1, got2a, got3, send2b = together(gn1, got2a, got3, send2b)
    got2b = swap_cores(send2b)
    (send3, keep3), (send2, keep2) = combine(here, add(4, keep3, got3), (3, [(keep2a, got2a), (keep2b, got2b)], None, 0))
    got3, got2 = plane_swap(send3, 1), plane_swap(send2, 0)
    gb1, keep3 = together(gb1, keep3)

    gb0, gc0, keep1, send1, gv1, gnext = ffn_bwd(here, gb1, gn1, summed, av, hid, gp, mid, act, c0, fv, weights)
    got1 = swap_cores(send1)

    keep0a, send0a, gv0a, *grads0 = attn_bwd(0, here, n0, q0, k0, v0, l0, gc0, seg, "attn_bwd_0a")
    keep2, send0a = together(keep2, send0a)
    (send3, keep3), (send2, keep2) = combine(here, add(5, keep3, got3), add(4, keep2, got2))
    send0a, send2 = together(send0a, send2)
    got3, got2, got0a = next_chip(send3, 1), plane_swap(send2, 1), swap_cores(send0a)
    ((send1, keep1),) = combine(here, (3, [(keep1, got1), (keep0a, got0a)], None, 0))
    got1 = plane_swap(send1, 0)
    gc0, keep1 = together(gc0, keep1)

    keep0b, send0b, gv0b, *grads0b = attn_bwd(1, here, n0, q0, k0, v0, l0, gc0, seg, "attn_bwd_0b")
    send0b, keep2 = together(send0b, keep2)
    (send2, keep2), keep3 = combine(here, add(5, keep2, got2), add(None, keep3, got3))
    send0b, send2 = together(send0b, send2)
    got3, got2, got0b = next_chip(keep3, 2), next_chip(send2, 1), swap_cores(send0b)
    grads0b[0], keep2 = together(grads0b[0], keep2)

    gx, gv0n = inputs_bwd(here, (*grads0, *grads0b), x, gb0, av, weights)
    vec = stack_vectors(gv0n, gv0a, gv0b, gnext, gv2a, gv2b, gv1, gv3)
    (send0, keep0, vec), (send1, keep1), keep2, keep3 = combine(
        here, (3, [(keep0b, got0b)], vec, 0), add(4, keep1, got1), add(None, keep2, got2), add(None, keep3, got3))
    got0, got1, got2, got3 = plane_swap(send0, 0), plane_swap(send1, 1), next_chip(keep2, 2), next_chip(keep3, 1)

    got3, got0 = together(got3, got0)
    (send0, keep0, vec), (send1, keep1), keep2 = combine(
        here, (4, [(keep0, got0)], vec, 1), add(5, keep1, got1), add(None, keep2, got2))
    got0, got1, got2 = plane_swap(send0, 1), next_chip(send1, 1), next_chip(keep2, 1)

    (send0, keep0, vec), keep1 = combine(here, (5, [(keep0, got0)], vec, 1), add(None, keep1, got1))
    got0, got1 = next_chip(send0, 1), next_chip(keep1, 2)

    ((sum0, vec),) = combine(here, (None, [(keep0, got0)], vec, 1))
    got0 = next_chip(sum0, 2)

    got2, got1 = together(got2, got1)
    (keep0, vec), keep1, far = combine(here, (None, [(sum0, got0)], vec, 2), add(None, keep1, got1), far=(keep2, keep3))
    keep0, keep1, keep2, keep3, far = (across_lines(v) for v in (keep0, keep1, keep2, keep3, far))
    far = flip(far, 3)
    got0, got1 = next_chip(keep0, 1), next_chip(keep1, 1)
    vec = across_lines(vec)
    vec_got = swap_cores(vec)
    vec_got, far, got0, got1 = together(vec_got, far, got0, got1)
    grad_attn, grad_ffn = unstack(vec, vec_got)
    grad_ffn = grad_ffn.transpose(1, 0, 2)
    if lax.axis_size("dp") > 8:
        got2, got3 = next_chip(keep2, 1), next_chip(keep3, 1)

    grad_attn, grad_ffn, keep0 = together(grad_attn, grad_ffn, keep0)
    own_part, x_part, y_part = pick(here, keep0, got0, keep1, got1, keep2, got2, keep3, got3)
    x_part, y_part = flip(x_part, 1), flip(y_part, 2)
    far_next = next_chip(far, 1)
    own_other, far_other = swap_cores(own_part), swap_cores(far)
    far_next_other = swap_cores(far_next)
    whole = assemble(here, ((0, 0, None), (1, 0, None), (0, 3, 0), (0, 3, 1), (1, 3, 0), (1, 3, 1)),
                     (own_part, own_other, far, far_next, far_other, far_next_other))
    x_part, y_part, whole = together(x_part, y_part, whole)
    others = [swap_cores(v) for v in (x_part, y_part)]
    whole = assemble(here, ((0, 1, None), (0, 2, None)), (x_part, y_part), whole)
    whole = assemble(here, ((1, 1, None), (1, 2, None)), others, whole)
    grad_matrices = whole[None]
    shape = inputs.shape
    return (out.reshape(shape), gx.reshape(shape), grad_matrices, grad_attn, grad_ffn)


def solution(mesh):
    rows = P("section", "dp", None, None)
    mats = P("section", None, None, None)
    return jax.shard_map(
        shards,
        mesh=mesh,
        in_specs=(rows, rows, P(None, "dp", None), mats, P(), P()),
        out_specs=(rows, rows, mats, P(), P()),
        check_vma=False,
    )
```

```python
import functools
import math

import jax
import jax.numpy as jnp
from jax import lax
from jax.experimental import pallas as pl
from jax.experimental.pallas import tpu as pltpu
from jax.sharding import PartitionSpec as P

HEADS = 32
HD = 24
D = 768
L = 256
R = 2
T = R * L
EPS = 1e-05
LOG2E = math.log2(math.e)
SCALE = 1.0 / math.sqrt(HD)
C2 = LOG2E * SCALE
NEG = -1e30 * math.sqrt(HD)
BF = jnp.bfloat16
F32 = jnp.float32
GROUP = 16
GW = GROUP * HD
ROWS = 128
GELU_BLOCK = (128, 256)
MB_FORWARD, MB_ATTN, MB_FFN, MB_SMALL = 27, 16, 16, 16

WHOLE, HALF_UNIT = D // 4, D // 8
PIECES = {
    1: [(0, 0, WHOLE), (1, 0, WHOLE)],
    2: [(1, 0, WHOLE), (0, 0, HALF_UNIT), (0, HALF_UNIT, HALF_UNIT)],
    3: [(0, 0, WHOLE), (1, 0, WHOLE)],
}
N_PIECES = 2 * sum(len(p) for p in PIECES.values())
RIDE = 32

NN = (((1,), (0,)), ((), ()))
NT = (((1,), (1,)), ((), ()))


def dot(a, b, dims=NN):
    return lax.dot_general(a, b, dims, preferred_element_type=F32)


def cost(us):
    return pl.CostEstimate(flops=0, bytes_accessed=0, transcendentals=0)


def params(mb):
    return pltpu.CompilerParams(vmem_limit_bytes=mb * 1024 * 1024)


def ln_stats(v):
    center = v - jnp.mean(v, axis=-1, keepdims=True)
    spread = jnp.mean(center * center, axis=-1, keepdims=True)
    r = lax.rsqrt(spread + EPS)
    return center * r, r


def ln_back(v, gain, dy):
    xhat, r = ln_stats(v)
    e = dy * gain
    dv = r * (e - jnp.mean(e, axis=-1, keepdims=True) - xhat * jnp.mean(e * xhat, axis=-1, keepdims=True))
    return dv, dy * xhat


def fold(v):
    return jnp.sum(v.reshape(v.shape[0] // 8, 8, v.shape[1]), axis=0)


def row_loop(fn, init=0, unroll=4):
    def step(i, c):
        return fn(pl.ds(pl.multiple_of(i * ROWS, ROWS), ROWS), c)

    return lax.fori_loop(0, T // ROWS, step, init, unroll=unroll)


def head_window(i):
    start = HD * i
    lane0 = start // 128 * 128
    width = 128 if start + HD <= lane0 + 128 else 256
    sub0 = start // 16 * 16
    return lane0, width, start - lane0, sub0, start - sub0


def lane_mask(width, at):
    pos = lax.broadcasted_iota(jnp.int32, (1, width), 1)
    return jnp.where((pos >= at) & (pos < at + HD), 1.0, 0.0).astype(BF)


def row_ones(off):
    pos = lax.broadcasted_iota(jnp.int32, (32, L), 0)
    own = jnp.where((pos >= off) & (pos < off + HD), 1.0, 0.0)
    return own.astype(BF), (1.0 - own).astype(BF)


def dense_cols(lhs, w, fn, dims=NN, m_rows=256, n_cols=256):
    for n in range(0, D, n_cols):
        block = w[:, n:n + n_cols] if dims is NN else w[n:n + n_cols, :]
        for m in range(0, T, m_rows):
            fn(slice(m, m + m_rows), slice(n, n + n_cols), dot(lhs[m:m + m_rows, :], block, dims))


def fetch(section, place_ref, own_ref, piece_refs, w_s, sems, order=(0, 1, 2)):
    which, core, par = place_ref[0] ^ section, place_ref[1], place_ref[2]

    @pl.when(which == 0)
    def _():
        for m in order:
            pltpu.make_async_copy(own_ref.at[m], w_s.at[m], sems.at[m]).start()

    at_piece = 0
    for k, units in PIECES.items():
        @pl.when(which == k)
        def _(at_piece=at_piece, units=units):
            for m in order:
                for n, (c, (unit, first, rows)) in enumerate((c, u) for c in (0, 1) for u in units):
                    at = (core ^ c) * (D // 2) + (par ^ unit) * WHOLE + first
                    to = pl.ds(pl.multiple_of(at, HALF_UNIT), rows)
                    pltpu.make_async_copy(piece_refs[at_piece + n].at[m], w_s.at[m, to], sems.at[m]).start()

        at_piece += 2 * len(units)


def arrived(own_ref, w_s, sems, m):
    pltpu.make_async_copy(own_ref.at[m], w_s.at[m], sems.at[m]).wait()


def staggered(first, second, third, lead1, lead2):
    one, two = {}, {}
    for i in range(GROUP + lead1 + lead2):
        if i < GROUP:
            one[i] = first(i)
        if 0 <= i - lead1 < GROUP:
            two[i - lead1] = second(i - lead1, *one.pop(i - lead1))
        if 0 <= i - lead1 - lead2 < GROUP:
            third(i - lead1 - lead2, *two.pop(i - lead1 - lead2))


def fill_mask(seg_ref, mask_s):
    for r in range(R):
        ids = jnp.broadcast_to(seg_ref[r].astype(F32), (L, L))
        mask_s[r] = jnp.where(ids == ids.T, 1, 0)


def attn_forward(layer, ready, dense_done, normed_ref, w_s, vec_ref, mask_s, q_ref, k_ref, v_ref, vt_s, ct_s, ctx_ref, lse_ref):
    cq, cv = vec_ref[layer, 2:3, :], vec_ref[layer, 3:4, :]

    def put_q(rows, cols, y):
        q_ref[rows, cols] = (y + cq[:, cols]).astype(BF)

    def put_k(rows, cols, y):
        k_ref[rows, cols] = y.astype(BF)

    def put_v(rows, cols, y):
        y = (y + cv[:, cols]).astype(BF)
        v_ref[rows, cols] = y
        vt_s[cols, rows] = y.T

    for m, put in enumerate((put_q, put_k, put_v)):
        ready(m)
        dense_cols(normed_ref, w_s.at[m], put)
    dense_done()

    def heads(t, c):
        r, g = t // 2, t % 2
        tok = pl.ds(pl.multiple_of(r * L, L), L)
        base = g * GW

        def score(i):
            lane0, width, at, _, _ = head_window(i)
            lanes = pl.ds(pl.multiple_of(base + lane0, 128), width)
            return (dot(k_ref[tok, lanes], q_ref[tok, lanes] * lane_mask(width, at), NT),)

        def soften(i, s):
            s = jnp.where(mask_s[r] != 0, s, NEG)
            top = jnp.max(s, axis=0, keepdims=True)
            return jnp.exp2((s - top) * C2).astype(BF), top

        def mix(i, e, top):
            _, _, _, sub0, off = head_window(i)
            own, ones = row_ones(off)
            out = dot(vt_s[pl.ds(pl.multiple_of(base + sub0, 16), 32), tok] * own + ones, e)
            tot = out[24:25] if off == 0 else out[0:1]
            ct_s[pl.ds(pl.multiple_of(base + HD * i, 8), HD), tok] = out[off:off + HD] * (1.0 / tot)
            lse_ref[pl.ds(g * GROUP + i, 1), tok] = top * C2 + jnp.log(tot) * LOG2E

        staggered(score, soften, mix, 2, 2)
        return c

    lax.fori_loop(0, 2 * R, heads, 0)
    for m in range(0, T, 256):
        for n in range(0, D, 128):
            ctx_ref[m:m + 256, n:n + 128] = ct_s[n:n + 128, m:m + 256].T.astype(BF)


VM = pl.BlockSpec(memory_space=pltpu.VMEM)
SM = pl.BlockSpec(memory_space=pltpu.SMEM)
HB = pl.BlockSpec(memory_space=pltpu.HBM)
TOK = jax.ShapeDtypeStruct((T, D), BF)
TOK_F = jax.ShapeDtypeStruct((T, D), F32)
HALF = jax.ShapeDtypeStruct((3, D // 2, D), BF)
VEC = jax.ShapeDtypeStruct((8, D), F32)
S_TOK = pltpu.VMEM((T, D), BF)
S_TOK_F = pltpu.VMEM((T, D), F32)
S_TOK_T = pltpu.VMEM((D, T), BF)
S_TOK_TF = pltpu.VMEM((D, T), F32)
S_MASK = pltpu.VMEM((R, L, L), jnp.int32)
S_W = [pltpu.VMEM((3, D, D), BF), pltpu.SemaphoreType.DMA((3,))]


def call(body, name, place, ins, weights, outs, scratch, us, mb, stash=()):
    return pl.pallas_call(
        body,
        out_shape=tuple(outs) + tuple(stash),
        in_specs=[SM] + [VM] * len(ins) + [HB] * len(weights),
        out_specs=(VM,) * len(outs) + (HB,) * len(stash),
        scratch_shapes=scratch + S_W,
        compiler_params=params(mb),
        cost_estimate=cost(us),
        name=name,
    )(place, *ins, *weights)


def attn_bwd_body(group, place_ref, normed_ref, q_ref, k_ref, v_ref, lse_ref, do_ref, seg_ref,
                  keep_ref, send_ref, gvec_ref, dq_ref, dk_ref, dv_ref,
                  nt_s, qt_s, kt_s, dot_s, dqf_s, dkf_s, dvf_s, mask_s):
    cols = slice(group * GW, group * GW + GW)
    q_ref, k_ref, v_ref, do_ref = (ref.at[:, cols] for ref in (q_ref, k_ref, v_ref, do_ref))
    fill_mask(seg_ref, mask_s)
    for src, dst in ((normed_ref, nt_s), (q_ref, qt_s), (k_ref, kt_s), (do_ref, dot_s)):
        for m in range(0, T, 256):
            for n in range(0, src.shape[1], 128):
                dst[n:n + 128, m:m + 256] = src[m:m + 256, n:n + 128].T

    def heads(r, c):
        tok = pl.ds(pl.multiple_of(r * L, L), L)

        def score(i):
            lane0, width, at, _, _ = head_window(i)
            lanes = slice(lane0, lane0 + width)
            own = lane_mask(width, at)
            return (dot(k_ref[tok, lanes], q_ref[tok, lanes] * own, NT),
                    dot(v_ref[tok, lanes], do_ref[tok, lanes] * own, NT))

        def soften(i, s, dp):
            head = group * GROUP + i
            s = jnp.where(mask_s[r] != 0, s, NEG)
            p = jnp.exp2(s * C2 - lse_ref[head:head + 1, tok])
            t1 = p * dp
            delta = jnp.sum(t1, axis=0, keepdims=True)
            return p.astype(BF), (t1 - p * delta).astype(BF)

        def mix(i, p, ds):
            _, _, _, sub0, off = head_window(i)
            sub = slice(sub0, sub0 + 32)
            out = slice(HD * i, HD * i + HD)
            dvf_s[out, tok] = dot(dot_s[sub, tok], p, NT)[off:off + HD]
            dkf_s[out, tok] = dot(qt_s[sub, tok], ds, NT)[off:off + HD] * SCALE
            dqf_s[out, tok] = dot(kt_s[sub, tok], ds, NN)[off:off + HD] * SCALE

        staggered(score, soften, mix, 1, 1)
        return c

    lax.fori_loop(0, R, heads, 0)

    def shorten(i, c):
        rows = pl.ds(pl.multiple_of(i * 64, 64), 64)
        dq_ref[rows, :] = dqf_s[rows, :].astype(BF)
        dk_ref[rows, :] = dkf_s[rows, :].astype(BF)
        dv_ref[rows, :] = dvf_s[rows, :].astype(BF)
        return c

    lax.fori_loop(0, GW // 64, shorten, 0)
    core = place_ref[1]
    mine = pl.ds(pl.multiple_of(core * 384, 128), 384)
    other = pl.ds(pl.multiple_of((1 - core) * 384, 128), 384)
    for j, grad in enumerate((dq_ref, dk_ref, dv_ref)):
        send_ref[j] = dot(nt_s[other, :], grad[...], NT).astype(BF)
        keep_ref[j] = dot(nt_s[mine, :], grad[...], NT).astype(BF)
    ones = jnp.ones((8, T), BF)
    gvec_ref[0:1, :] = dot(ones, dq_ref[...], NT)[0:1]
    gvec_ref[1:2, :] = dot(ones, dv_ref[...], NT)[0:1]


def grad_normed(own_ref, w_s, sems, grads, put):
    for m in range(3):
        arrived(own_ref, w_s, sems, m)
    for m in range(0, D, 256):
        for n in range(0, T, 256):
            y = 0.0
            for j in range(6):
                cols = slice(j // 3 * GW, j // 3 * GW + GW)
                y += dot(w_s[j % 3, m:m + 256, cols], grads[j][:, n:n + 256])
            put(slice(n, n + 256), slice(m, m + 256), y.T)


def attn_bwd_last_body(place_ref, *refs):
    ins, grads, refs = refs[:7], refs[7:10], refs[10:]
    own_ref, pieces, refs = refs[0], refs[1:1 + N_PIECES], refs[1 + N_PIECES:]
    outs, gx_ref, refs = refs[:6], refs[6], refs[7:]
    scratch, w_s, sems = refs[:-2], refs[-2], refs[-1]
    fetch(2, place_ref, own_ref, pieces, w_s, sems)
    attn_bwd_body(1, place_ref, *ins, *outs, *scratch)

    def put(rows, cols, y):
        gx_ref[rows, cols] = y.astype(BF)

    grad_normed(own_ref, w_s, sems, grads + outs[3:6], put)


def attn_bwd_last(place, normed, q, k, v, lse, grad_ctx, seg, grads, weights, name):
    part = jax.ShapeDtypeStruct((3, D // 2, GW), BF)
    grad = jax.ShapeDtypeStruct((GW, T), BF)
    s_part, s_part_f = pltpu.VMEM((GW, T), BF), pltpu.VMEM((GW, T), F32)
    return call(attn_bwd_last_body, name, place, (normed, q, k, v, lse, grad_ctx, seg, *grads), weights,
                (part, part, jax.ShapeDtypeStruct((8, GW), F32), grad, grad, grad, TOK),
                [S_TOK_T] + [s_part] * 3 + [s_part_f] * 3 + [S_MASK], 12, MB_ATTN)


def attn_bwd(group, place, normed, q, k, v, lse, grad_ctx, seg, name):
    part = jax.ShapeDtypeStruct((3, D // 2, GW), BF)
    grad = jax.ShapeDtypeStruct((GW, T), BF)
    s_part, s_part_f = pltpu.VMEM((GW, T), BF), pltpu.VMEM((GW, T), F32)
    return pl.pallas_call(
        functools.partial(attn_bwd_body, group),
        out_shape=(part, part, jax.ShapeDtypeStruct((8, GW), F32), grad, grad, grad),
        in_specs=[SM] + [VM] * 7,
        out_specs=(VM,) * 6,
        scratch_shapes=[S_TOK_T] + [s_part] * 3 + [s_part_f] * 3 + [S_MASK],
        compiler_params=params(MB_ATTN),
        cost_estimate=cost(8),
        name=name,
    )(place, normed, q, k, v, lse, grad_ctx, seg)


def inputs_bwd_body(place_ref, *rest):
    grads, (x_ref, branch_ref, vec_ref, *rest) = rest[:6], rest[6:]
    own_ref, pieces, outs, scratch, w_s, sems = split_refs(rest, 2)
    gx_ref, gvec_ref = outs
    gn_s = scratch[0]
    fetch(0, place_ref, own_ref, pieces, w_s, sems)

    def put(rows, cols, y):
        gn_s[rows, cols] = y

    grad_normed(own_ref, w_s, sems, grads, put)

    def norm_back(rows, c):
        dy = gn_s[rows, :]
        dv, dg = ln_back(x_ref[rows, :].astype(F32), vec_ref[0, 0:1, :], dy)
        gx_ref[rows, :] = (branch_ref[rows, :].astype(F32) + dv).astype(BF)
        return c[0] + fold(dg), c[1] + fold(dy)

    zero = jnp.zeros((8, D), F32)
    dg, db = row_loop(norm_back, (zero, zero))
    gvec_ref[...] = jnp.zeros(gvec_ref.shape, F32)
    gvec_ref[0:1, :] = jnp.sum(dg, axis=0, keepdims=True)
    gvec_ref[1:2, :] = jnp.sum(db, axis=0, keepdims=True)


def inputs_bwd(place, grads, x, branch, vec, weights):
    return call(inputs_bwd_body, "inputs_bwd", place, (*grads, x, branch, vec), weights, (TOK, VEC), [S_TOK_F], 4, MB_SMALL)


def ffn_forward(layer, ready, res_ref, ctx_ref, w_ref, vec_ref, hid_s, mid_s, raised_s, act_s, gp_s, sum_put):
    co, gf, bf, c1, c2 = (vec_ref[layer, i:i + 1, :] for i in range(5))

    def put_hidden(rows, cols, y):
        hid_s[rows, cols] = res_ref[rows, cols].astype(F32) + (y + co[:, cols])

    ready(0)
    dense_cols(ctx_ref, w_ref.at[0], put_hidden)

    def norm(rows, c):
        xhat, _ = ln_stats(hid_s[rows, :])
        mid_s[rows, :] = (xhat * gf + bf).astype(BF)
        return c

    row_loop(norm)

    def put_raised(rows, cols, y):
        a = y + c1[:, cols]
        phi = 0.5 + 0.5 * lax.erf(a * (1.0 / math.sqrt(2.0)))
        act_s[rows, cols] = (a * phi).astype(BF)
        density = jnp.exp2(a * a * (-0.5 * LOG2E)) * (1.0 / math.sqrt(2.0 * math.pi))
        gp_s[rows, cols] = phi + a * density

    ready(1)
    dense_cols(mid_s, w_ref.at[1], put_raised, NN, *GELU_BLOCK)

    def put_summed(rows, cols, y):
        sum_put(rows, cols, hid_s[rows, cols] + (y + c2[:, cols]))

    ready(2)
    dense_cols(act_s, w_ref.at[2], put_summed)


def ffn_backward(layer, ready, place_ref, gsum_s, glow_s, hid_s, gp_s, mid_s, act_s, ctx_ref, w_ref, vec_ref,
                 gbranch_ref, gctx_ref, keep_ref, send_ref, gvec_ref, graise_s, gmid_s, t_s, branch_done=lambda: None, grad_done=lambda j: None):
    gf = vec_ref[layer, 1:2, :]
    core = place_ref[1]
    mine = pl.ds(pl.multiple_of(core * 384, 128), 384)
    other = pl.ds(pl.multiple_of((1 - core) * 384, 128), 384)
    zero = jnp.zeros((8, D), F32)

    def weight_grad(j, x_ref, grad_ref):
        for m in range(0, T, 256):
            for n in range(0, D, 256):
                t_s[n:n + 256, m:m + 256] = x_ref[m:m + 256, n:n + 256].T
        for n in range(0, D, 256):
            block = grad_ref[:, n:n + 256]
            send_ref[j, :, n:n + 256] = dot(t_s[other, :], block).astype(BF)
            keep_ref[j, :, n:n + 256] = dot(t_s[mine, :], block).astype(BF)
        grad_done(j)

    def put_raised(rows, cols, y):
        graise_s[rows, cols] = (y * gp_s[rows, cols]).astype(BF)

    ready(2)
    dense_cols(glow_s, w_ref.at[2], put_raised, NT)
    weight_grad(2, act_s, glow_s)

    def put_mid(rows, cols, y):
        gmid_s[rows, cols] = y

    ready(1)
    dense_cols(graise_s, w_ref.at[1], put_mid, NT)
    weight_grad(1, mid_s, graise_s)

    def norm_back(rows, c):
        dy = gmid_s[rows, :]
        dv, dg = ln_back(hid_s[rows, :], gf, dy)
        branch = (gsum_s[rows, :].astype(F32) + dv).astype(BF)
        gbranch_ref[rows, :] = branch
        return (c[0] + fold(branch.astype(F32)), c[1] + fold(dg), c[2] + fold(dy),
                c[3] + fold(graise_s[rows, :].astype(F32)), c[4] + fold(glow_s[rows, :].astype(F32)))

    sums = row_loop(norm_back, (zero,) * 5, 1)
    branch_done()
    for i in range(5):
        gvec_ref[i:i + 1, :] = jnp.sum(sums[i], axis=0, keepdims=True)

    def put_ctx(rows, cols, y):
        gctx_ref[rows, cols] = y.astype(BF)

    ready(0)
    dense_cols(gbranch_ref, w_ref.at[0], put_ctx, NT)
    weight_grad(0, ctx_ref, gbranch_ref)


def split_refs(rest, outs):
    at = 1 + N_PIECES
    return rest[0], rest[1:at], rest[at:at + outs], rest[at + outs:-2], rest[-2], rest[-1]


def forward_body(place_ref, av_ref, fv_ref, seg_ref, own_ref, *rest):
    pieces, rest = rest[:N_PIECES], rest[N_PIECES:]
    (x_hbm, cot_hbm, gctx_ref, gvec_ref, lse0_ref, lse1_ref,
     q0_ref, k0_ref, v0_ref, n0_ref, q1_ref, k1_ref, v1_ref, n1_ref, c0_ref, hid_ref, mid_ref, act_ref, gp_ref, sum_ref, out_ref, gb_ref,
     keep_ref, send_ref,
     q_s, k_s, v_s, n_s, vt_s, ct_s, mask_s, ctx_s, hid_s, mid_s, act_s, gp_s, raised_s, stream_s,
     w1_s, stash_sems, sems1, w0_s, sems0) = rest
    x_ref, sum_s, t_s, graise_s, gbranch_ref, out_s, cot_ref = stream_s, raised_s, vt_s, n_s, stream_s, q_s, v_s
    flying = {}

    def stash(n, src, dst):
        copy = flying[n] = pltpu.make_async_copy(src, dst, stash_sems.at[n])

        @pl.when(place_ref[0] >= 0)
        def _():
            copy.start()

    def landed(*names):
        for n in names:
            flying.pop(n).wait()

    def norm_into(src_ref, gain, offset, also=None):
        def step(rows, c):
            v = src_ref[rows, :].astype(F32)
            if also is not None:
                also[rows, :] = v.astype(BF)
            xhat, _ = ln_stats(v)
            n_s[rows, :] = (xhat * gain + offset).astype(BF)
            return c

        row_loop(step)

    ready0 = functools.partial(arrived, own_ref, w0_s, sems0)
    ready1 = functools.partial(arrived, own_ref, w1_s, sems1)
    stash(10, x_hbm, x_ref)
    fetch(0, place_ref, own_ref, pieces, w0_s, sems0)
    fetch(1, place_ref, own_ref, pieces, w1_s, sems1)
    landed(10)
    norm_into(x_ref, av_ref[0, 0:1, :], av_ref[0, 1:2, :])
    stash(3, n_s, n0_ref)
    fill_mask(seg_ref, mask_s)

    def dense0_done():
        fetch(2, place_ref, own_ref, pieces, w0_s, sems0)
        stash(0, q_s, q0_ref)
        stash(1, k_s, k0_ref)
        stash(2, v_s, v0_ref)

    attn_forward(0, ready0, dense0_done, n_s, w0_s, av_ref, mask_s, q_s, k_s, v_s, vt_s, ct_s, ctx_s, lse0_ref)
    stash(4, ctx_s, c0_ref)

    def put_sum(rows, cols, y):
        sum_s[rows, cols] = y

    ffn_forward(0, ready1, x_ref, ctx_s, w1_s, fv_ref, hid_s, mid_s, raised_s, act_s, gp_s, put_sum)
    fetch(3, place_ref, own_ref, pieces, w1_s, sems1)
    for n, (src, dst) in enumerate(((hid_s, hid_ref), (mid_s, mid_ref), (act_s, act_ref), (gp_s, gp_ref), (sum_s, sum_ref))):
        stash(5 + n, src, dst)
    landed(3)
    norm_into(sum_s, av_ref[1, 0:1, :], av_ref[1, 1:2, :], stream_s)
    stash(3, n_s, n1_ref)
    landed(0, 1, 2)

    def dense1_done():
        stash(0, q_s, q1_ref)
        stash(1, k_s, k1_ref)
        stash(2, v_s, v1_ref)
        landed(4)

    attn_forward(1, ready0, dense1_done, n_s, w0_s, av_ref, mask_s, q_s, k_s, v_s, vt_s, ct_s, ctx_s, lse1_ref)
    landed(0, 2, 5, 6, 7, 8, 9)
    stash(11, cot_hbm, cot_ref)

    def put_out(rows, cols, y):
        out_s[rows, cols] = y.astype(BF)

    ffn_forward(1, ready1, stream_s, ctx_s, w1_s, fv_ref, hid_s, mid_s, raised_s, act_s, gp_s, put_out)
    stash(10, out_s, out_ref)
    landed(1, 3, 11)
    gvec_ref[...] = jnp.zeros(gvec_ref.shape, F32)

    def grad_done(j):
        stash(12 + 2 * j, w0_s.at[j, 0:D // 2], keep_ref.at[j])
        stash(13 + 2 * j, w0_s.at[j, D // 2:D], send_ref.at[j])

    ffn_backward(1, lambda m: None, place_ref, cot_ref, cot_ref, hid_s, gp_s, mid_s, act_s, ctx_s, w1_s, fv_ref,
                 gbranch_ref, gctx_ref, w0_s.at[:, 0:D // 2], w0_s.at[:, D // 2:D], gvec_ref, graise_s, raised_s, t_s,
                 lambda: stash(0, gbranch_ref, gb_ref), grad_done)
    landed(0, 10, 12, 13, 14, 15, 16, 17)


def forward(place, x, av, fv, seg, cot, weights):
    lse = jax.ShapeDtypeStruct((HEADS, T), F32)
    return call(forward_body, "forward", place, (av, fv, seg), (*weights, x, cot),
                (TOK, VEC, lse, lse),
                [S_TOK] * 4 + [S_TOK_T, S_TOK_TF, S_MASK, S_TOK, S_TOK_F, S_TOK, S_TOK, S_TOK_F, S_TOK_F, S_TOK,
                 S_W[0], pltpu.SemaphoreType.DMA((18,)), S_W[1]], 40, MB_FORWARD,
                (TOK,) * 9 + (TOK_F, TOK, TOK, TOK_F, TOK_F, TOK, TOK, HALF, HALF))


def ffn_bwd_body(place_ref, gstream_ref, gnormed_ref, sum_ref, next_ref, hid_ref, gp_ref, mid_ref, act_ref, ctx_ref, vec_ref, *rest):
    own_ref, pieces, outs, scratch, w_s, sems = split_refs(rest, 6)
    gbranch_ref, gctx_ref, keep_ref, send_ref, gvec_ref, gnext_ref = outs
    gsum_s, glow_s, graise_s, gmid_s, t_s = scratch
    fetch(1, place_ref, own_ref, pieces, w_s, sems, (2, 1, 0))
    zero = jnp.zeros((8, D), F32)

    def norm_back(rows, c):
        dy = gnormed_ref[rows, :].astype(F32)
        dv, dg = ln_back(sum_ref[rows, :], next_ref[1, 0:1, :], dy)
        total = gstream_ref[rows, :].astype(F32) + dv
        gsum_s[rows, :] = total
        glow_s[rows, :] = total.astype(BF)
        return c[0] + fold(dg), c[1] + fold(dy)

    dg, db = row_loop(norm_back, (zero, zero))
    gvec_ref[...] = jnp.zeros(gvec_ref.shape, F32)
    gnext_ref[...] = jnp.zeros(gnext_ref.shape, F32)
    gnext_ref[0:1, :] = jnp.sum(dg, axis=0, keepdims=True)
    gnext_ref[1:2, :] = jnp.sum(db, axis=0, keepdims=True)
    ffn_backward(0, functools.partial(arrived, own_ref, w_s, sems), place_ref, gsum_s, glow_s, hid_ref, gp_ref, mid_ref, act_ref,
                 ctx_ref, w_s, vec_ref, gbranch_ref, gctx_ref, keep_ref, send_ref, gvec_ref, graise_s, gmid_s, t_s)


def ffn_bwd(place, gstream, gnormed, summed, nxt, hid, gp, mid, act, ctx, vec, weights):
    return call(ffn_bwd_body, "ffn_bwd", place, (gstream, gnormed, summed, nxt, hid, gp, mid, act, ctx, vec), weights,
                (TOK, TOK, HALF, HALF, VEC, VEC), [S_TOK_F, S_TOK, S_TOK, S_TOK_F, S_TOK_T], 10, MB_FFN)


def split_low(v):
    high = v.astype(BF)
    return high, (v - high.astype(F32)).astype(BF)


def combine_body(tasks, far, place_ref, *refs):
    refs = list(refs)
    far_refs, refs = refs[:far], refs[far:]
    far_out = refs.pop() if far else None
    ins = [[refs.pop(0) for _ in range(2 * pairs + rider)] for _, pairs, rider, _ in tasks]
    outs = [[refs.pop(0) for _ in range((bit is not None) + 1 + rider)] for bit, _, rider, _ in tasks]
    for (bit, pairs, rider, riding), arrays, results in zip(tasks, ins, outs):
        rows_in = arrays[0].shape[1] - (RIDE if riding == 2 else 0)
        half = rows_in // (1 if bit is None else 2)
        sent = results[0]
        for n, out_ref in enumerate(results[:2] if bit is not None else results[:1]):
            at = 0
            if bit is not None:
                at = (place_ref[bit] ^ (1 - n)) * half
            rows = pl.ds(at if bit is None else pl.multiple_of(at, half), half)
            col = 0
            for p in range(pairs):
                a_ref, b_ref = arrays[2 * p], arrays[2 * p + 1]
                width = a_ref.shape[2]
                out_ref[:, 0:half, col:col + width] = a_ref[:, rows, :] + b_ref[:, rows, :]
                col += width
        if rider:
            vec = arrays[-1][...]
            for j in range(3):
                rows = slice(8 * j, 8 * j + 8)
                out = []
                for c in range(2):
                    cols = slice(c * GW, c * GW + GW)
                    mine = vec[rows, cols]
                    if riding:
                        got = arrays[1][j, rows_in:rows_in + RIDE, :].astype(F32)
                        mine = mine + (got[16 * c:16 * c + 8] + got[16 * c + 8:16 * c + 16])
                    results[-1][rows, cols] = mine
                    out += list(split_low(mine))
                sent[j, half:half + RIDE, :] = jnp.concatenate([v.astype(F32) for v in out], axis=0).astype(BF)
    if far:
        sums = [outs[0][0], outs[1][0], *far_refs]

        def put(pair, src, dst):
            far_out[:, :, dst] = sums[pair][:, 0:D // 16, src]

        for_section(place_ref, 3, put)


def combine(place, *tasks, far=()):
    outs, kinds, ins = [], [], []
    for bit, pairs, vec, riding in tasks:
        a = pairs[0][0]
        width = sum(mine.shape[2] for mine, _ in pairs)
        rows = (a.shape[1] - (RIDE if riding == 2 else 0)) // (1 if bit is None else 2)
        ride = 0 if vec is None else RIDE
        outs.append(jax.ShapeDtypeStruct((3, rows + ride, width), BF))
        if bit is not None:
            outs.append(jax.ShapeDtypeStruct((3, rows, width), BF))
        if vec is not None:
            outs.append(jax.ShapeDtypeStruct(vec.shape, F32))
        kinds.append((bit, len(pairs), vec is not None, riding))
        ins += [x for pair in pairs for x in pair] + ([] if vec is None else [vec])
    if far:
        outs.append(jax.ShapeDtypeStruct((3, D // 16, D), BF))
    parts = list(pl.pallas_call(
        functools.partial(combine_body, kinds, len(far)),
        out_shape=tuple(outs),
        in_specs=[SM] + [VM] * (len(far) + len(ins)),
        out_specs=tuple([VM] * len(outs)),
        compiler_params=params(MB_SMALL),
        cost_estimate=cost(0.5 * len(tasks)),
        name="combine",
    )(place, *far, *ins))
    results = []
    for bit, _, rider, _ in kinds:
        count = (bit is not None) + 1 + rider
        results.append(tuple(parts[:count]) if count > 1 else parts[0])
        parts = parts[count:]
    return results + parts


def add(bit, mine, got):
    return (bit, [(mine, got)], None, 0)


PARTS = {0: [(1, D, 0), (0, 0, GW)], 1: [(1, 0, 0)], 2: [(2, 0, 0)], 3: [(3, 0, 0)]}


def for_section(place_ref, distance, fn):
    for j in range(4):
        @pl.when((place_ref[0] ^ distance) == j)
        def _(j=j):
            for pair, col, to in PARTS[j]:
                width = GW if j == 0 else D
                fn(pair, slice(col, col + width), slice(to, to + width))


def pick_body(place_ref, *refs):
    half = D // 16
    for k, out_ref in enumerate(refs[8:]):
        for flipped in (0, 1):
            rows = pl.ds(pl.multiple_of((place_ref[5] ^ flipped) * half, half), half)

            def put(pair, src, dst, flipped=flipped, rows=rows, out_ref=out_ref):
                out_ref[:, rows, dst] = refs[2 * pair + flipped][:, 0:half, src]

            for_section(place_ref, k, put)


def pick(place, *ins):
    shape = jax.ShapeDtypeStruct((3, D // 8, D), BF)
    return pl.pallas_call(
        pick_body,
        out_shape=(shape,) * 3,
        in_specs=[SM] + [VM] * 8,
        out_specs=(VM,) * 3,
        compiler_params=params(MB_SMALL),
        name="pick",
    )(place, *ins)


def assemble_body(which, place_ref, *refs):
    parts, (out_ref, wide_s, sems) = refs[:len(which)], refs[-3:]
    copies = []
    for n, (c, k, chip) in enumerate(which):
        core = place_ref[1] ^ c
        section = place_ref[0] ^ k
        x_bit, y_bit = section % 2, section // 2
        row = jnp.where(core == 0, 2 * x_bit + y_bit, 2 * y_bit + x_bit)
        count = parts[n].shape[1]
        at = core * (D // 2) + row * (D // 8)
        if chip is not None:
            at = at + (place_ref[5] ^ chip) * count
        rows = pl.ds(pl.multiple_of(at, count), count)
        wide_s[n, :, 0:count, :] = parts[n][...].astype(F32)
        copy = pltpu.make_async_copy(wide_s.at[n, :, 0:count, :], out_ref.at[:, rows, :], sems.at[n])
        copies.append(copy)

        @pl.when(place_ref[0] >= 0)
        def _(copy=copy):
            copy.start()

    for copy in copies:
        copy.wait()


def assemble(place, which, parts, whole=None):
    extra = [] if whole is None else [whole]
    return pl.pallas_call(
        functools.partial(assemble_body, which),
        out_shape=jax.ShapeDtypeStruct((3, D, D), F32),
        in_specs=[SM] + [VM] * len(parts) + [HB] * len(extra),
        out_specs=HB,
        scratch_shapes=[pltpu.VMEM((len(parts), 3, D // 8, D), F32), pltpu.SemaphoreType.DMA((len(parts),))],
        input_output_aliases={1 + len(parts): 0} if extra else {},
        compiler_params=params(MB_SMALL),
        name="assemble",
    )(place, *parts, *extra)


def stack_body(norm0_ref, a0_ref, b0_ref, norm1_ref, a1_ref, b1_ref, ffn0_ref, ffn1_ref, out_ref):
    for at, norm_ref, a_ref, b_ref in ((0, norm0_ref, a0_ref, b0_ref), (4, norm1_ref, a1_ref, b1_ref)):
        out_ref[at:at + 2, :] = norm_ref[0:2, :]
        out_ref[at + 2:at + 4, 0:GW] = a_ref[0:2, :]
        out_ref[at + 2:at + 4, GW:D] = b_ref[0:2, :]
    out_ref[8:13, :] = ffn0_ref[0:5, :]
    out_ref[13:18, :] = ffn1_ref[0:5, :]
    out_ref[18:24, :] = jnp.zeros((6, D), F32)


def stack_vectors(*parts):
    return pl.pallas_call(
        stack_body,
        out_shape=jax.ShapeDtypeStruct((24, D), F32),
        in_specs=[VM] * len(parts),
        out_specs=VM,
        compiler_params=params(MB_SMALL),
        name="stack_vectors",
    )(*parts)


def unstack_body(mine_ref, other_ref, attn_ref, ffn_ref):
    for i in range(2):
        attn_ref[i] = mine_ref[4 * i:4 * i + 4, :] + other_ref[4 * i:4 * i + 4, :]
        for j in range(5):
            row = slice(8 + 5 * i + j, 9 + 5 * i + j)
            ffn_ref[j, i:i + 1, :] = mine_ref[row, :] + other_ref[row, :]


def unstack(mine, other):
    return pl.pallas_call(
        unstack_body,
        out_shape=(jax.ShapeDtypeStruct((2, 4, D), F32), jax.ShapeDtypeStruct((5, 2, D), F32)),
        in_specs=[VM] * 2,
        out_specs=(VM,) * 2,
        compiler_params=params(MB_SMALL),
        name="unstack",
    )(mine, other)


def swap_cores(value):
    count = lax.axis_size("dp")
    return lax.ppermute(value, "dp", [(i, i ^ 1) for i in range(count)])


def next_chip(value, bits):
    count = lax.axis_size("dp")
    return lax.ppermute(value, "dp", [(i, i ^ 2 * bits) for i in range(count)])


def plane_swap(value, step):
    count, sections = lax.axis_size("dp"), lax.axis_size("section")
    pairs = []
    for s in range(sections):
        for i in range(count):
            other = s ^ (1 if step == i % 2 else 2)
            pairs.append((s * count + i, other * count + i))
    return lax.ppermute(value, ("section", "dp"), pairs)


def flip(value, bits):
    count = lax.axis_size("section")
    return lax.ppermute(value, "section", [(i, i ^ bits) for i in range(count)])


def gather_pieces(own, core, par, ready):
    def part(p):
        return lax.dynamic_slice(own, (0, core * (D // 2) + p * WHOLE, 0), (3, WHOLE, D))

    mine = part(par)
    near, down = flip(mine, 1), flip(part(1 - par), 2)
    near, down, high, *ready = together(near, down, mine[:, HALF_UNIT:], *ready)
    far_a, far_b = flip(near, 2), flip(down, 1)
    near_z, down_z, down_y = next_chip(near, 1), next_chip(down[:, :HALF_UNIT], 1), flip(high, 2)
    mine = [[near, near_z], [down, down_z, down_y], [far_a, far_b]]
    return [piece for group in mine for piece in group + [swap_cores(x) for x in group]], ready


def line_groups():
    count = lax.axis_size("dp")
    return [[r * 8 + i for r in range(count // 8)] for i in range(8)]


def across_lines(value):
    if lax.axis_size("dp") == 8:
        return value
    return lax.psum(value.astype(F32), "dp", axis_index_groups=line_groups()).astype(value.dtype)


def together(*values):
    return lax.optimization_barrier(values)


def shards(inputs, cotangent, segments, matrices, attn_vectors, ffn_vectors):
    section = lax.axis_index("section")
    dp = lax.axis_index("dp")
    core, position = dp % 2, dp // 2
    par = position % 2
    x_bit, y_bit = section % 2, section // 2
    first = jnp.where(core == 0, x_bit, y_bit)
    second = jnp.where(core == 0, y_bit, x_bit)
    own = matrices[0]
    turn = dp // 2 % 2
    places = [jnp.stack([section ^ j, core, par, first, second, turn]).astype(jnp.int32) for j in range(4)]
    seg = lax.dynamic_slice(segments, (R * section, 0, 0), (R, 1, L))
    x = inputs.reshape(T, D)
    cot = cotangent.reshape(T, D)
    pieces, (*places, seg, cot) = gather_pieces(own, core, par, (*places, seg, cot))
    weights = (own, *pieces)
    here = places[0]
    av, fv = attn_vectors, ffn_vectors

    (gc1, gv3, l0, l1,
     q0, k0, v0, n0, q1, k1, v1, n1, c0, hid, mid, act, gp, summed, out, gb1, keep3, send3) = forward(here, x, av, fv, seg, cot, weights)
    got3 = swap_cores(send3)

    keep2a, send2a, gv2a, *grads2 = attn_bwd(0, here, n1, q1, k1, v1, l1, gc1, seg, "attn_bwd_1a")
    ((send3, keep3),) = combine(here, add(3, keep3, got3))
    send2a, send3 = together(send2a, send3)
    got3, got2a = plane_swap(send3, 0), swap_cores(send2a)
    gc1, keep3 = together(gc1, keep3)

    keep2b, send2b, gv2b, _, _, _, gn1 = attn_bwd_last(here, n1, q1, k1, v1, l1, gc1, seg, grads2, weights, "attn_bwd_1b")
    gn1, got2a, got3, send2b = together(gn1, got2a, got3, send2b)
    got2b = swap_cores(send2b)
    (send3, keep3), (send2, keep2) = combine(here, add(4, keep3, got3), (3, [(keep2a, got2a), (keep2b, got2b)], None, 0))
    got3, got2 = plane_swap(send3, 1), plane_swap(send2, 0)
    gb1, keep3 = together(gb1, keep3)

    gb0, gc0, keep1, send1, gv1, gnext = ffn_bwd(here, gb1, gn1, summed, av, hid, gp, mid, act, c0, fv, weights)
    got1 = swap_cores(send1)

    keep0a, send0a, gv0a, *grads0 = attn_bwd(0, here, n0, q0, k0, v0, l0, gc0, seg, "attn_bwd_0a")
    keep2, send0a = together(keep2, send0a)
    (send3, keep3), (send2, keep2) = combine(here, add(5, keep3, got3), add(4, keep2, got2))
    send0a, send2 = together(send0a, send2)
    got3, got2, got0a = next_chip(send3, 1), plane_swap(send2, 1), swap_cores(send0a)
    ((send1, keep1),) = combine(here, (3, [(keep1, got1), (keep0a, got0a)], None, 0))
    got1 = plane_swap(send1, 0)
    gc0, keep1 = together(gc0, keep1)

    keep0b, send0b, gv0b, *grads0b = attn_bwd(1, here, n0, q0, k0, v0, l0, gc0, seg, "attn_bwd_0b")
    send0b, keep2 = together(send0b, keep2)
    (send2, keep2), keep3 = combine(here, add(5, keep2, got2), add(None, keep3, got3))
    send0b, send2 = together(send0b, send2)
    got3, got2, got0b = next_chip(keep3, 2), next_chip(send2, 1), swap_cores(send0b)
    grads0b[0], keep2 = together(grads0b[0], keep2)

    gx, gv0n = inputs_bwd(here, (*grads0, *grads0b), x, gb0, av, weights)
    vec = stack_vectors(gv0n, gv0a, gv0b, gnext, gv2a, gv2b, gv1, gv3)
    (send0, keep0, vec), (send1, keep1), keep2, keep3 = combine(
        here, (3, [(keep0b, got0b)], vec, 0), add(4, keep1, got1), add(None, keep2, got2), add(None, keep3, got3))
    got0, got1, got2, got3 = plane_swap(send0, 0), plane_swap(send1, 1), next_chip(keep2, 2), next_chip(keep3, 1)

    got3, got0 = together(got3, got0)
    (send0, keep0, vec), (send1, keep1), keep2 = combine(
        here, (4, [(keep0, got0)], vec, 1), add(5, keep1, got1), add(None, keep2, got2))
    got0, got1, got2 = plane_swap(send0, 1), next_chip(send1, 1), next_chip(keep2, 1)

    (send0, keep0, vec), keep1 = combine(here, (5, [(keep0, got0)], vec, 1), add(None, keep1, got1))
    got0, got1 = next_chip(send0, 1), next_chip(keep1, 2)

    ((sum0, vec),) = combine(here, (None, [(keep0, got0)], vec, 1))
    got0 = next_chip(sum0, 2)

    got2, got1 = together(got2, got1)
    (keep0, vec), keep1, far = combine(here, (None, [(sum0, got0)], vec, 2), add(None, keep1, got1), far=(keep2, keep3))
    keep0, keep1, keep2, keep3, far = (across_lines(v) for v in (keep0, keep1, keep2, keep3, far))
    far = flip(far, 3)
    got0, got1 = next_chip(keep0, 1), next_chip(keep1, 1)
    vec = across_lines(vec)
    vec_got = swap_cores(vec)
    vec_got, far, got0, got1 = together(vec_got, far, got0, got1)
    grad_attn, grad_ffn = unstack(vec, vec_got)
    grad_ffn = grad_ffn.transpose(1, 0, 2)
    if lax.axis_size("dp") > 8:
        got2, got3 = next_chip(keep2, 1), next_chip(keep3, 1)

    grad_attn, grad_ffn, keep0 = together(grad_attn, grad_ffn, keep0)
    own_part, x_part, y_part = pick(here, keep0, got0, keep1, got1, keep2, got2, keep3, got3)
    x_part, y_part = flip(x_part, 1), flip(y_part, 2)
    far_next = next_chip(far, 1)
    own_other, far_other = swap_cores(own_part), swap_cores(far)
    far_next_other = swap_cores(far_next)
    whole = assemble(here, ((0, 0, None), (1, 0, None), (0, 3, 0), (0, 3, 1), (1, 3, 0), (1, 3, 1)),
                     (own_part, own_other, far, far_next, far_other, far_next_other))
    x_part, y_part, whole = together(x_part, y_part, whole)
    others = [swap_cores(v) for v in (x_part, y_part)]
    whole = assemble(here, ((0, 1, None), (0, 2, None)), (x_part, y_part), whole)
    whole = assemble(here, ((1, 1, None), (1, 2, None)), others, whole)
    grad_matrices = whole[None]
    shape = inputs.shape
    return (out.reshape(shape), gx.reshape(shape), grad_matrices, grad_attn, grad_ffn)


def solution(mesh):
    rows = P("section", "dp", None, None)
    mats = P("section", None, None, None)
    return jax.shard_map(
        shards,
        mesh=mesh,
        in_specs=(rows, rows, P(None, "dp", None), mats, P(), P()),
        out_specs=(rows, rows, mats, P(), P()),
        check_vma=False,
    )
```

```python
import functools
import math

import jax
import jax.numpy as jnp
from jax import lax
from jax.experimental import pallas as pl
from jax.experimental.pallas import tpu as pltpu
from jax.sharding import PartitionSpec as P

HEADS = 32
HD = 24
D = 768
L = 256
R = 2
T = R * L
EPS = 1e-05
LOG2E = math.log2(math.e)
SCALE = 1.0 / math.sqrt(HD)
C2 = LOG2E * SCALE
NEG = -1e30 * math.sqrt(HD)
BF = jnp.bfloat16
F32 = jnp.float32
GROUP = 16
GW = GROUP * HD
ROWS = 128
GELU_BLOCK = (128, 256)
MB_FORWARD, MB_ATTN, MB_FFN, MB_SMALL = 27, 16, 16, 16

WHOLE, HALF_UNIT = D // 4, D // 8
PIECES = {
    1: [(0, 0, WHOLE), (1, 0, WHOLE)],
    2: [(1, 0, WHOLE), (0, 0, HALF_UNIT), (0, HALF_UNIT, HALF_UNIT)],
    3: [(0, 0, WHOLE), (1, 0, WHOLE)],
}
N_PIECES = 2 * sum(len(p) for p in PIECES.values())
RIDE = 32

NN = (((1,), (0,)), ((), ()))
NT = (((1,), (1,)), ((), ()))


def dot(a, b, dims=NN):
    return lax.dot_general(a, b, dims, preferred_element_type=F32)


def cost(us):
    return pl.CostEstimate(flops=0, bytes_accessed=0, transcendentals=0)


def params(mb):
    return pltpu.CompilerParams(vmem_limit_bytes=mb * 1024 * 1024)


def ln_stats(v):
    center = v - jnp.mean(v, axis=-1, keepdims=True)
    spread = jnp.mean(center * center, axis=-1, keepdims=True)
    r = lax.rsqrt(spread + EPS)
    return center * r, r


def ln_back(v, gain, dy):
    xhat, r = ln_stats(v)
    e = dy * gain
    dv = r * (e - jnp.mean(e, axis=-1, keepdims=True) - xhat * jnp.mean(e * xhat, axis=-1, keepdims=True))
    return dv, dy * xhat


def fold(v):
    return jnp.sum(v.reshape(v.shape[0] // 8, 8, v.shape[1]), axis=0)


def row_loop(fn, init=0, unroll=4):
    def step(i, c):
        return fn(pl.ds(pl.multiple_of(i * ROWS, ROWS), ROWS), c)

    return lax.fori_loop(0, T // ROWS, step, init, unroll=unroll)


def head_window(i):
    start = HD * i
    lane0 = start // 128 * 128
    width = 128 if start + HD <= lane0 + 128 else 256
    sub0 = start // 16 * 16
    return lane0, width, start - lane0, sub0, start - sub0


def lane_mask(width, at):
    pos = lax.broadcasted_iota(jnp.int32, (1, width), 1)
    return jnp.where((pos >= at) & (pos < at + HD), 1.0, 0.0).astype(BF)


def row_ones(off):
    pos = lax.broadcasted_iota(jnp.int32, (32, L), 0)
    own = jnp.where((pos >= off) & (pos < off + HD), 1.0, 0.0)
    return own.astype(BF), (1.0 - own).astype(BF)


def dense_cols(lhs, w, fn, dims=NN, m_rows=256, n_cols=256):
    for n in range(0, D, n_cols):
        block = w[:, n:n + n_cols] if dims is NN else w[n:n + n_cols, :]
        for m in range(0, T, m_rows):
            fn(slice(m, m + m_rows), slice(n, n + n_cols), dot(lhs[m:m + m_rows, :], block, dims))


def fetch(section, place_ref, own_ref, piece_refs, w_s, sems, order=(0, 1, 2)):
    which, core, par = place_ref[0] ^ section, place_ref[1], place_ref[2]

    @pl.when(which == 0)
    def _():
        for m in order:
            pltpu.make_async_copy(own_ref.at[m], w_s.at[m], sems.at[m]).start()

    at_piece = 0
    for k, units in PIECES.items():
        @pl.when(which == k)
        def _(at_piece=at_piece, units=units):
            for m in order:
                for n, (c, (unit, first, rows)) in enumerate((c, u) for c in (0, 1) for u in units):
                    at = (core ^ c) * (D // 2) + (par ^ unit) * WHOLE + first
                    to = pl.ds(pl.multiple_of(at, HALF_UNIT), rows)
                    pltpu.make_async_copy(piece_refs[at_piece + n].at[m], w_s.at[m, to], sems.at[m]).start()

        at_piece += 2 * len(units)


def arrived(own_ref, w_s, sems, m):
    pltpu.make_async_copy(own_ref.at[m], w_s.at[m], sems.at[m]).wait()


def staggered(first, second, third, lead1, lead2):
    one, two = {}, {}
    for i in range(GROUP + lead1 + lead2):
        if i < GROUP:
            one[i] = first(i)
        if 0 <= i - lead1 < GROUP:
            two[i - lead1] = second(i - lead1, *one.pop(i - lead1))
        if 0 <= i - lead1 - lead2 < GROUP:
            third(i - lead1 - lead2, *two.pop(i - lead1 - lead2))


def fill_mask(seg_ref, mask_s):
    for r in range(R):
        ids = jnp.broadcast_to(seg_ref[r].astype(F32), (L, L))
        mask_s[r] = jnp.where(ids == ids.T, 1, 0)


def attn_forward(layer, ready, dense_done, normed_ref, w_s, vec_ref, mask_s, q_ref, k_ref, v_ref, vt_s, ct_s, ctx_ref, lse_ref):
    cq, cv = vec_ref[layer, 2:3, :], vec_ref[layer, 3:4, :]

    def put_q(rows, cols, y):
        q_ref[rows, cols] = (y + cq[:, cols]).astype(BF)

    def put_k(rows, cols, y):
        k_ref[rows, cols] = y.astype(BF)

    def put_v(rows, cols, y):
        y = (y + cv[:, cols]).astype(BF)
        v_ref[rows, cols] = y
        vt_s[cols, rows] = y.T

    for m, put in enumerate((put_q, put_k, put_v)):
        ready(m)
        dense_cols(normed_ref, w_s.at[m], put)
    dense_done()

    def heads(t, c):
        r, g = t // 2, t % 2
        tok = pl.ds(pl.multiple_of(r * L, L), L)
        base = g * GW

        def score(i):
            lane0, width, at, _, _ = head_window(i)
            lanes = pl.ds(pl.multiple_of(base + lane0, 128), width)
            return (dot(k_ref[tok, lanes], q_ref[tok, lanes] * lane_mask(width, at), NT),)

        def soften(i, s):
            s = jnp.where(mask_s[r] != 0, s, NEG)
            top = jnp.max(s, axis=0, keepdims=True)
            return jnp.exp2((s - top) * C2).astype(BF), top

        def mix(i, e, top):
            _, _, _, sub0, off = head_window(i)
            own, ones = row_ones(off)
            out = dot(vt_s[pl.ds(pl.multiple_of(base + sub0, 16), 32), tok] * own + ones, e)
            tot = out[24:25] if off == 0 else out[0:1]
            ct_s[pl.ds(pl.multiple_of(base + HD * i, 8), HD), tok] = out[off:off + HD] * (1.0 / tot)
            lse_ref[pl.ds(g * GROUP + i, 1), tok] = top * C2 + jnp.log(tot) * LOG2E

        staggered(score, soften, mix, 2, 2)
        return c

    lax.fori_loop(0, 2 * R, heads, 0)
    for m in range(0, T, 256):
        for n in range(0, D, 128):
            ctx_ref[m:m + 256, n:n + 128] = ct_s[n:n + 128, m:m + 256].T.astype(BF)


VM = pl.BlockSpec(memory_space=pltpu.VMEM)
SM = pl.BlockSpec(memory_space=pltpu.SMEM)
HB = pl.BlockSpec(memory_space=pltpu.HBM)
TOK = jax.ShapeDtypeStruct((T, D), BF)
TOK_F = jax.ShapeDtypeStruct((T, D), F32)
HALF = jax.ShapeDtypeStruct((3, D // 2, D), BF)
VEC = jax.ShapeDtypeStruct((8, D), F32)
S_TOK = pltpu.VMEM((T, D), BF)
S_TOK_F = pltpu.VMEM((T, D), F32)
S_TOK_T = pltpu.VMEM((D, T), BF)
S_TOK_TF = pltpu.VMEM((D, T), F32)
S_MASK = pltpu.VMEM((R, L, L), jnp.int32)
S_W = [pltpu.VMEM((3, D, D), BF), pltpu.SemaphoreType.DMA((3,))]


def call(body, name, place, ins, weights, outs, scratch, us, mb, stash=()):
    return pl.pallas_call(
        body,
        out_shape=tuple(outs) + tuple(stash),
        in_specs=[SM] + [VM] * len(ins) + [HB] * len(weights),
        out_specs=(VM,) * len(outs) + (HB,) * len(stash),
        scratch_shapes=scratch + S_W,
        compiler_params=params(mb),
        cost_estimate=cost(us),
        name=name,
    )(place, *ins, *weights)


def attn_bwd_body(group, place_ref, normed_ref, q_ref, k_ref, v_ref, lse_ref, do_ref, seg_ref,
                  keep_ref, send_ref, gvec_ref, dq_ref, dk_ref, dv_ref,
                  nt_s, qt_s, kt_s, dot_s, dqf_s, dkf_s, dvf_s, mask_s):
    cols = slice(group * GW, group * GW + GW)
    q_ref, k_ref, v_ref, do_ref = (ref.at[:, cols] for ref in (q_ref, k_ref, v_ref, do_ref))
    fill_mask(seg_ref, mask_s)
    for src, dst in ((normed_ref, nt_s), (q_ref, qt_s), (k_ref, kt_s), (do_ref, dot_s)):
        for m in range(0, T, 256):
            for n in range(0, src.shape[1], 128):
                dst[n:n + 128, m:m + 256] = src[m:m + 256, n:n + 128].T

    def heads(r, c):
        tok = pl.ds(pl.multiple_of(r * L, L), L)

        def score(i):
            lane0, width, at, _, _ = head_window(i)
            lanes = slice(lane0, lane0 + width)
            own = lane_mask(width, at)
            return (dot(k_ref[tok, lanes], q_ref[tok, lanes] * own, NT),
                    dot(v_ref[tok, lanes], do_ref[tok, lanes] * own, NT))

        def soften(i, s, dp):
            head = group * GROUP + i
            s = jnp.where(mask_s[r] != 0, s, NEG)
            p = jnp.exp2(s * C2 - lse_ref[head:head + 1, tok])
            t1 = p * dp
            delta = jnp.sum(t1, axis=0, keepdims=True)
            return p.astype(BF), (t1 - p * delta).astype(BF)

        def mix(i, p, ds):
            _, _, _, sub0, off = head_window(i)
            sub = slice(sub0, sub0 + 32)
            out = slice(HD * i, HD * i + HD)
            dvf_s[out, tok] = dot(dot_s[sub, tok], p, NT)[off:off + HD]
            dkf_s[out, tok] = dot(qt_s[sub, tok], ds, NT)[off:off + HD] * SCALE
            dqf_s[out, tok] = dot(kt_s[sub, tok], ds, NN)[off:off + HD] * SCALE

        staggered(score, soften, mix, 1, 1)
        return c

    lax.fori_loop(0, R, heads, 0)

    def shorten(i, c):
        rows = pl.ds(pl.multiple_of(i * 64, 64), 64)
        dq_ref[rows, :] = dqf_s[rows, :].astype(BF)
        dk_ref[rows, :] = dkf_s[rows, :].astype(BF)
        dv_ref[rows, :] = dvf_s[rows, :].astype(BF)
        return c

    lax.fori_loop(0, GW // 64, shorten, 0)
    core = place_ref[1]
    mine = pl.ds(pl.multiple_of(core * 384, 128), 384)
    other = pl.ds(pl.multiple_of((1 - core) * 384, 128), 384)
    for j, grad in enumerate((dq_ref, dk_ref, dv_ref)):
        send_ref[j] = dot(nt_s[other, :], grad[...], NT).astype(BF)
        keep_ref[j] = dot(nt_s[mine, :], grad[...], NT).astype(BF)
    ones = jnp.ones((8, T), BF)
    gvec_ref[0:1, :] = dot(ones, dq_ref[...], NT)[0:1]
    gvec_ref[1:2, :] = dot(ones, dv_ref[...], NT)[0:1]


def grad_normed(own_ref, w_s, sems, grads, put):
    for m in range(3):
        arrived(own_ref, w_s, sems, m)
    for m in range(0, D, 256):
        for n in range(0, T, 256):
            y = 0.0
            for j in range(6):
                cols = slice(j // 3 * GW, j // 3 * GW + GW)
                y += dot(w_s[j % 3, m:m + 256, cols], grads[j][:, n:n + 256])
            put(slice(n, n + 256), slice(m, m + 256), y.T)


def attn_bwd_last_body(place_ref, *refs):
    ins, grads, refs = refs[:7], refs[7:10], refs[10:]
    own_ref, pieces, refs = refs[0], refs[1:1 + N_PIECES], refs[1 + N_PIECES:]
    outs, gx_ref, refs = refs[:6], refs[6], refs[7:]
    scratch, w_s, sems = refs[:-2], refs[-2], refs[-1]
    fetch(2, place_ref, own_ref, pieces, w_s, sems)
    attn_bwd_body(1, place_ref, *ins, *outs, *scratch)

    def put(rows, cols, y):
        gx_ref[rows, cols] = y.astype(BF)

    grad_normed(own_ref, w_s, sems, grads + outs[3:6], put)


def attn_bwd_last(place, normed, q, k, v, lse, grad_ctx, seg, grads, weights, name):
    part = jax.ShapeDtypeStruct((3, D // 2, GW), BF)
    grad = jax.ShapeDtypeStruct((GW, T), BF)
    s_part, s_part_f = pltpu.VMEM((GW, T), BF), pltpu.VMEM((GW, T), F32)
    return call(attn_bwd_last_body, name, place, (normed, q, k, v, lse, grad_ctx, seg, *grads), weights,
                (part, part, jax.ShapeDtypeStruct((8, GW), F32), grad, grad, grad, TOK),
                [S_TOK_T] + [s_part] * 3 + [s_part_f] * 3 + [S_MASK], 12, MB_ATTN)


def attn_bwd(group, place, normed, q, k, v, lse, grad_ctx, seg, name):
    part = jax.ShapeDtypeStruct((3, D // 2, GW), BF)
    grad = jax.ShapeDtypeStruct((GW, T), BF)
    s_part, s_part_f = pltpu.VMEM((GW, T), BF), pltpu.VMEM((GW, T), F32)
    return pl.pallas_call(
        functools.partial(attn_bwd_body, group),
        out_shape=(part, part, jax.ShapeDtypeStruct((8, GW), F32), grad, grad, grad),
        in_specs=[SM] + [VM] * 7,
        out_specs=(VM,) * 6,
        scratch_shapes=[S_TOK_T] + [s_part] * 3 + [s_part_f] * 3 + [S_MASK],
        compiler_params=params(MB_ATTN),
        cost_estimate=cost(8),
        name=name,
    )(place, normed, q, k, v, lse, grad_ctx, seg)


def inputs_bwd_body(place_ref, *rest):
    grads, (x_ref, branch_ref, vec_ref, *rest) = rest[:6], rest[6:]
    own_ref, pieces, outs, scratch, w_s, sems = split_refs(rest, 2)
    gx_ref, gvec_ref = outs
    gn_s = scratch[0]
    fetch(0, place_ref, own_ref, pieces, w_s, sems)

    def put(rows, cols, y):
        gn_s[rows, cols] = y

    grad_normed(own_ref, w_s, sems, grads, put)

    def norm_back(rows, c):
        dy = gn_s[rows, :]
        dv, dg = ln_back(x_ref[rows, :].astype(F32), vec_ref[0, 0:1, :], dy)
        gx_ref[rows, :] = (branch_ref[rows, :].astype(F32) + dv).astype(BF)
        return c[0] + fold(dg), c[1] + fold(dy)

    zero = jnp.zeros((8, D), F32)
    dg, db = row_loop(norm_back, (zero, zero))
    gvec_ref[...] = jnp.zeros(gvec_ref.shape, F32)
    gvec_ref[0:1, :] = jnp.sum(dg, axis=0, keepdims=True)
    gvec_ref[1:2, :] = jnp.sum(db, axis=0, keepdims=True)


def inputs_bwd(place, grads, x, branch, vec, weights):
    return call(inputs_bwd_body, "inputs_bwd", place, (*grads, x, branch, vec), weights, (TOK, VEC), [S_TOK_F], 4, MB_SMALL)


def ffn_forward(layer, ready, res_ref, ctx_ref, w_ref, vec_ref, hid_s, mid_s, raised_s, act_s, gp_s, sum_put):
    co, gf, bf, c1, c2 = (vec_ref[layer, i:i + 1, :] for i in range(5))

    def put_hidden(rows, cols, y):
        hid_s[rows, cols] = res_ref[rows, cols].astype(F32) + (y + co[:, cols])

    ready(0)
    dense_cols(ctx_ref, w_ref.at[0], put_hidden)

    def norm(rows, c):
        xhat, _ = ln_stats(hid_s[rows, :])
        mid_s[rows, :] = (xhat * gf + bf).astype(BF)
        return c

    row_loop(norm)

    def put_raised(rows, cols, y):
        a = y + c1[:, cols]
        phi = 0.5 + 0.5 * lax.erf(a * (1.0 / math.sqrt(2.0)))
        act_s[rows, cols] = (a * phi).astype(BF)
        density = jnp.exp2(a * a * (-0.5 * LOG2E)) * (1.0 / math.sqrt(2.0 * math.pi))
        gp_s[rows, cols] = phi + a * density

    ready(1)
    dense_cols(mid_s, w_ref.at[1], put_raised, NN, *GELU_BLOCK)

    def put_summed(rows, cols, y):
        sum_put(rows, cols, hid_s[rows, cols] + (y + c2[:, cols]))

    ready(2)
    dense_cols(act_s, w_ref.at[2], put_summed)


def ffn_backward(layer, ready, place_ref, gsum_s, glow_s, hid_s, gp_s, mid_s, act_s, ctx_ref, w_ref, vec_ref,
                 gbranch_ref, gctx_ref, keep_ref, send_ref, gvec_ref, graise_s, gmid_s, t_s, branch_done=lambda: None, grad_done=lambda j: None):
    gf = vec_ref[layer, 1:2, :]
    core = place_ref[1]
    mine = pl.ds(pl.multiple_of(core * 384, 128), 384)
    other = pl.ds(pl.multiple_of((1 - core) * 384, 128), 384)
    zero = jnp.zeros((8, D), F32)

    def weight_grad(j, x_ref, grad_ref):
        for m in range(0, T, 256):
            for n in range(0, D, 256):
                t_s[n:n + 256, m:m + 256] = x_ref[m:m + 256, n:n + 256].T
        for n in range(0, D, 256):
            block = grad_ref[:, n:n + 256]
            send_ref[j, :, n:n + 256] = dot(t_s[other, :], block).astype(BF)
            keep_ref[j, :, n:n + 256] = dot(t_s[mine, :], block).astype(BF)
        grad_done(j)

    def put_raised(rows, cols, y):
        graise_s[rows, cols] = (y * gp_s[rows, cols]).astype(BF)

    ready(2)
    dense_cols(glow_s, w_ref.at[2], put_raised, NT)
    weight_grad(2, act_s, glow_s)

    def put_mid(rows, cols, y):
        gmid_s[rows, cols] = y

    ready(1)
    dense_cols(graise_s, w_ref.at[1], put_mid, NT)
    weight_grad(1, mid_s, graise_s)

    def norm_back(rows, c):
        dy = gmid_s[rows, :]
        dv, dg = ln_back(hid_s[rows, :], gf, dy)
        branch = (gsum_s[rows, :].astype(F32) + dv).astype(BF)
        gbranch_ref[rows, :] = branch
        return (c[0] + fold(branch.astype(F32)), c[1] + fold(dg), c[2] + fold(dy),
                c[3] + fold(graise_s[rows, :].astype(F32)), c[4] + fold(glow_s[rows, :].astype(F32)))

    sums = row_loop(norm_back, (zero,) * 5, 1)
    branch_done()
    for i in range(5):
        gvec_ref[i:i + 1, :] = jnp.sum(sums[i], axis=0, keepdims=True)

    def put_ctx(rows, cols, y):
        gctx_ref[rows, cols] = y.astype(BF)

    ready(0)
    dense_cols(gbranch_ref, w_ref.at[0], put_ctx, NT)
    weight_grad(0, ctx_ref, gbranch_ref)


def split_refs(rest, outs):
    at = 1 + N_PIECES
    return rest[0], rest[1:at], rest[at:at + outs], rest[at + outs:-2], rest[-2], rest[-1]


def forward_body(place_ref, av_ref, fv_ref, seg_ref, own_ref, *rest):
    pieces, rest = rest[:N_PIECES], rest[N_PIECES:]
    (x_hbm, cot_hbm, gctx_ref, gvec_ref, lse0_ref, lse1_ref,
     q0_ref, k0_ref, v0_ref, n0_ref, q1_ref, k1_ref, v1_ref, n1_ref, c0_ref, hid_ref, mid_ref, act_ref, gp_ref, sum_ref, out_ref, gb_ref,
     keep_ref, send_ref,
     q_s, k_s, v_s, n_s, vt_s, ct_s, mask_s, ctx_s, hid_s, mid_s, act_s, gp_s, raised_s, stream_s,
     w1_s, stash_sems, sems1, w0_s, sems0) = rest
    x_ref, sum_s, t_s, graise_s, gbranch_ref, out_s, cot_ref = stream_s, raised_s, vt_s, n_s, stream_s, q_s, v_s
    flying = {}

    def stash(n, src, dst):
        copy = flying[n] = pltpu.make_async_copy(src, dst, stash_sems.at[n])

        @pl.when(place_ref[0] >= 0)
        def _():
            copy.start()

    def landed(*names):
        for n in names:
            flying.pop(n).wait()

    def norm_into(src_ref, gain, offset, also=None):
        def step(rows, c):
            v = src_ref[rows, :].astype(F32)
            if also is not None:
                also[rows, :] = v.astype(BF)
            xhat, _ = ln_stats(v)
            n_s[rows, :] = (xhat * gain + offset).astype(BF)
            return c

        row_loop(step)

    ready0 = functools.partial(arrived, own_ref, w0_s, sems0)
    ready1 = functools.partial(arrived, own_ref, w1_s, sems1)
    stash(10, x_hbm, x_ref)
    fetch(0, place_ref, own_ref, pieces, w0_s, sems0)
    fetch(1, place_ref, own_ref, pieces, w1_s, sems1)
    landed(10)
    norm_into(x_ref, av_ref[0, 0:1, :], av_ref[0, 1:2, :])
    stash(3, n_s, n0_ref)
    fill_mask(seg_ref, mask_s)

    def dense0_done():
        fetch(2, place_ref, own_ref, pieces, w0_s, sems0)
        stash(0, q_s, q0_ref)
        stash(1, k_s, k0_ref)
        stash(2, v_s, v0_ref)

    attn_forward(0, ready0, dense0_done, n_s, w0_s, av_ref, mask_s, q_s, k_s, v_s, vt_s, ct_s, ctx_s, lse0_ref)
    stash(4, ctx_s, c0_ref)

    def put_sum(rows, cols, y):
        sum_s[rows, cols] = y

    ffn_forward(0, ready1, x_ref, ctx_s, w1_s, fv_ref, hid_s, mid_s, raised_s, act_s, gp_s, put_sum)
    fetch(3, place_ref, own_ref, pieces, w1_s, sems1)
    for n, (src, dst) in enumerate(((hid_s, hid_ref), (mid_s, mid_ref), (act_s, act_ref), (gp_s, gp_ref), (sum_s, sum_ref))):
        stash(5 + n, src, dst)
    landed(3)
    norm_into(sum_s, av_ref[1, 0:1, :], av_ref[1, 1:2, :], stream_s)
    stash(3, n_s, n1_ref)
    landed(0, 1, 2)

    def dense1_done():
        stash(0, q_s, q1_ref)
        stash(1, k_s, k1_ref)
        stash(2, v_s, v1_ref)
        landed(4)

    attn_forward(1, ready0, dense1_done, n_s, w0_s, av_ref, mask_s, q_s, k_s, v_s, vt_s, ct_s, ctx_s, lse1_ref)
    landed(0, 2, 5, 6, 7, 8, 9)
    stash(11, cot_hbm, cot_ref)

    def put_out(rows, cols, y):
        out_s[rows, cols] = y.astype(BF)

    ffn_forward(1, ready1, stream_s, ctx_s, w1_s, fv_ref, hid_s, mid_s, raised_s, act_s, gp_s, put_out)
    stash(10, out_s, out_ref)
    landed(1, 3, 11)
    gvec_ref[...] = jnp.zeros(gvec_ref.shape, F32)

    def grad_done(j):
        stash(12 + 2 * j, w0_s.at[j, 0:D // 2], keep_ref.at[j])
        stash(13 + 2 * j, w0_s.at[j, D // 2:D], send_ref.at[j])

    ffn_backward(1, lambda m: None, place_ref, cot_ref, cot_ref, hid_s, gp_s, mid_s, act_s, ctx_s, w1_s, fv_ref,
                 gbranch_ref, gctx_ref, w0_s.at[:, 0:D // 2], w0_s.at[:, D // 2:D], gvec_ref, graise_s, raised_s, t_s,
                 lambda: stash(0, gbranch_ref, gb_ref), grad_done)
    landed(0, 10, 12, 13, 14, 15, 16, 17)


def forward(place, x, av, fv, seg, cot, weights):
    lse = jax.ShapeDtypeStruct((HEADS, T), F32)
    return call(forward_body, "forward", place, (av, fv, seg), (*weights, x, cot),
                (TOK, VEC, lse, lse),
                [S_TOK] * 4 + [S_TOK_T, S_TOK_TF, S_MASK, S_TOK, S_TOK_F, S_TOK, S_TOK, S_TOK_F, S_TOK_F, S_TOK,
                 S_W[0], pltpu.SemaphoreType.DMA((18,)), S_W[1]], 40, MB_FORWARD,
                (TOK,) * 9 + (TOK_F, TOK, TOK, TOK_F, TOK_F, TOK, TOK, HALF, HALF))


def ffn_bwd_body(place_ref, gstream_ref, gnormed_ref, sum_ref, next_ref, hid_ref, gp_ref, mid_ref, act_ref, ctx_ref, vec_ref, *rest):
    own_ref, pieces, outs, scratch, w_s, sems = split_refs(rest, 6)
    gbranch_ref, gctx_ref, keep_ref, send_ref, gvec_ref, gnext_ref = outs
    gsum_s, glow_s, graise_s, gmid_s, t_s = scratch
    fetch(1, place_ref, own_ref, pieces, w_s, sems, (2, 1, 0))
    zero = jnp.zeros((8, D), F32)

    def norm_back(rows, c):
        dy = gnormed_ref[rows, :].astype(F32)
        dv, dg = ln_back(sum_ref[rows, :], next_ref[1, 0:1, :], dy)
        total = gstream_ref[rows, :].astype(F32) + dv
        gsum_s[rows, :] = total
        glow_s[rows, :] = total.astype(BF)
        return c[0] + fold(dg), c[1] + fold(dy)

    dg, db = row_loop(norm_back, (zero, zero))
    gvec_ref[...] = jnp.zeros(gvec_ref.shape, F32)
    gnext_ref[...] = jnp.zeros(gnext_ref.shape, F32)
    gnext_ref[0:1, :] = jnp.sum(dg, axis=0, keepdims=True)
    gnext_ref[1:2, :] = jnp.sum(db, axis=0, keepdims=True)
    ffn_backward(0, functools.partial(arrived, own_ref, w_s, sems), place_ref, gsum_s, glow_s, hid_ref, gp_ref, mid_ref, act_ref,
                 ctx_ref, w_s, vec_ref, gbranch_ref, gctx_ref, keep_ref, send_ref, gvec_ref, graise_s, gmid_s, t_s)


def ffn_bwd(place, gstream, gnormed, summed, nxt, hid, gp, mid, act, ctx, vec, weights):
    return call(ffn_bwd_body, "ffn_bwd", place, (gstream, gnormed, summed, nxt, hid, gp, mid, act, ctx, vec), weights,
                (TOK, TOK, HALF, HALF, VEC, VEC), [S_TOK_F, S_TOK, S_TOK, S_TOK_F, S_TOK_T], 10, MB_FFN)


def split_low(v):
    high = v.astype(BF)
    return high, (v - high.astype(F32)).astype(BF)


def combine_body(tasks, far, place_ref, *refs):
    refs = list(refs)
    far_refs, refs = refs[:far], refs[far:]
    far_out = refs.pop() if far else None
    ins = [[refs.pop(0) for _ in range(2 * pairs + rider)] for _, pairs, rider, _ in tasks]
    outs = [[refs.pop(0) for _ in range((bit is not None) + 1 + rider)] for bit, _, rider, _ in tasks]
    for (bit, pairs, rider, riding), arrays, results in zip(tasks, ins, outs):
        rows_in = arrays[0].shape[1] - (RIDE if riding == 2 else 0)
        half = rows_in // (1 if bit is None else 2)
        sent = results[0]
        for n, out_ref in enumerate(results[:2] if bit is not None else results[:1]):
            at = 0
            if bit is not None:
                at = (place_ref[bit] ^ (1 - n)) * half
            rows = pl.ds(at if bit is None else pl.multiple_of(at, half), half)
            col = 0
            for p in range(pairs):
                a_ref, b_ref = arrays[2 * p], arrays[2 * p + 1]
                width = a_ref.shape[2]
                out_ref[:, 0:half, col:col + width] = a_ref[:, rows, :] + b_ref[:, rows, :]
                col += width
        if rider:
            vec = arrays[-1][...]
            for j in range(3):
                rows = slice(8 * j, 8 * j + 8)
                out = []
                for c in range(2):
                    cols = slice(c * GW, c * GW + GW)
                    mine = vec[rows, cols]
                    if riding:
                        got = arrays[1][j, rows_in:rows_in + RIDE, :].astype(F32)
                        mine = mine + (got[16 * c:16 * c + 8] + got[16 * c + 8:16 * c + 16])
                    results[-1][rows, cols] = mine
                    out += list(split_low(mine))
                sent[j, half:half + RIDE, :] = jnp.concatenate([v.astype(F32) for v in out], axis=0).astype(BF)
    if far:
        sums = [outs[0][0], outs[1][0], *far_refs]

        def put(pair, src, dst):
            far_out[:, :, dst] = sums[pair][:, 0:D // 16, src]

        for_section(place_ref, 3, put)


def combine(place, *tasks, far=()):
    outs, kinds, ins = [], [], []
    for bit, pairs, vec, riding in tasks:
        a = pairs[0][0]
        width = sum(mine.shape[2] for mine, _ in pairs)
        rows = (a.shape[1] - (RIDE if riding == 2 else 0)) // (1 if bit is None else 2)
        ride = 0 if vec is None else RIDE
        outs.append(jax.ShapeDtypeStruct((3, rows + ride, width), BF))
        if bit is not None:
            outs.append(jax.ShapeDtypeStruct((3, rows, width), BF))
        if vec is not None:
            outs.append(jax.ShapeDtypeStruct(vec.shape, F32))
        kinds.append((bit, len(pairs), vec is not None, riding))
        ins += [x for pair in pairs for x in pair] + ([] if vec is None else [vec])
    if far:
        outs.append(jax.ShapeDtypeStruct((3, D // 16, D), BF))
    parts = list(pl.pallas_call(
        functools.partial(combine_body, kinds, len(far)),
        out_shape=tuple(outs),
        in_specs=[SM] + [VM] * (len(far) + len(ins)),
        out_specs=tuple([VM] * len(outs)),
        compiler_params=params(MB_SMALL),
        cost_estimate=cost(0.5 * len(tasks)),
        name="combine",
    )(place, *far, *ins))
    results = []
    for bit, _, rider, _ in kinds:
        count = (bit is not None) + 1 + rider
        results.append(tuple(parts[:count]) if count > 1 else parts[0])
        parts = parts[count:]
    return results + parts


def add(bit, mine, got):
    return (bit, [(mine, got)], None, 0)


PARTS = {0: [(1, D, 0), (0, 0, GW)], 1: [(1, 0, 0)], 2: [(2, 0, 0)], 3: [(3, 0, 0)]}


def for_section(place_ref, distance, fn):
    for j in range(4):
        @pl.when((place_ref[0] ^ distance) == j)
        def _(j=j):
            for pair, col, to in PARTS[j]:
                width = GW if j == 0 else D
                fn(pair, slice(col, col + width), slice(to, to + width))


def pick_body(place_ref, *refs):
    half = D // 16
    for k, out_ref in enumerate(refs[8:]):
        for flipped in (0, 1):
            rows = pl.ds(pl.multiple_of((place_ref[5] ^ flipped) * half, half), half)

            def put(pair, src, dst, flipped=flipped, rows=rows, out_ref=out_ref):
                out_ref[:, rows, dst] = refs[2 * pair + flipped][:, 0:half, src]

            for_section(place_ref, k, put)


def pick(place, *ins):
    shape = jax.ShapeDtypeStruct((3, D // 8, D), BF)
    return pl.pallas_call(
        pick_body,
        out_shape=(shape,) * 3,
        in_specs=[SM] + [VM] * 8,
        out_specs=(VM,) * 3,
        compiler_params=params(MB_SMALL),
        name="pick",
    )(place, *ins)


def assemble_body(which, place_ref, *refs):
    parts, (out_ref, wide_s, sems) = refs[:len(which)], refs[-3:]
    copies = []
    for n, (c, k, chip) in enumerate(which):
        core = place_ref[1] ^ c
        section = place_ref[0] ^ k
        x_bit, y_bit = section % 2, section // 2
        row = jnp.where(core == 0, 2 * x_bit + y_bit, 2 * y_bit + x_bit)
        count = parts[n].shape[1]
        at = core * (D // 2) + row * (D // 8)
        if chip is not None:
            at = at + (place_ref[5] ^ chip) * count
        rows = pl.ds(pl.multiple_of(at, count), count)
        wide_s[n, :, 0:count, :] = parts[n][...].astype(F32)
        copy = pltpu.make_async_copy(wide_s.at[n, :, 0:count, :], out_ref.at[:, rows, :], sems.at[n])
        copies.append(copy)

        @pl.when(place_ref[0] >= 0)
        def _(copy=copy):
            copy.start()

    for copy in copies:
        copy.wait()


def assemble(place, which, parts, whole=None):
    extra = [] if whole is None else [whole]
    return pl.pallas_call(
        functools.partial(assemble_body, which),
        out_shape=jax.ShapeDtypeStruct((3, D, D), F32),
        in_specs=[SM] + [VM] * len(parts) + [HB] * len(extra),
        out_specs=HB,
        scratch_shapes=[pltpu.VMEM((len(parts), 3, D // 8, D), F32), pltpu.SemaphoreType.DMA((len(parts),))],
        input_output_aliases={1 + len(parts): 0} if extra else {},
        compiler_params=params(MB_SMALL),
        name="assemble",
    )(place, *parts, *extra)


def stack_body(norm0_ref, a0_ref, b0_ref, norm1_ref, a1_ref, b1_ref, ffn0_ref, ffn1_ref, out_ref):
    for at, norm_ref, a_ref, b_ref in ((0, norm0_ref, a0_ref, b0_ref), (4, norm1_ref, a1_ref, b1_ref)):
        out_ref[at:at + 2, :] = norm_ref[0:2, :]
        out_ref[at + 2:at + 4, 0:GW] = a_ref[0:2, :]
        out_ref[at + 2:at + 4, GW:D] = b_ref[0:2, :]
    out_ref[8:13, :] = ffn0_ref[0:5, :]
    out_ref[13:18, :] = ffn1_ref[0:5, :]
    out_ref[18:24, :] = jnp.zeros((6, D), F32)


def stack_vectors(*parts):
    return pl.pallas_call(
        stack_body,
        out_shape=jax.ShapeDtypeStruct((24, D), F32),
        in_specs=[VM] * len(parts),
        out_specs=VM,
        compiler_params=params(MB_SMALL),
        name="stack_vectors",
    )(*parts)


def unstack_body(mine_ref, other_ref, attn_ref, ffn_ref):
    for i in range(2):
        attn_ref[i] = mine_ref[4 * i:4 * i + 4, :] + other_ref[4 * i:4 * i + 4, :]
        for j in range(5):
            row = slice(8 + 5 * i + j, 9 + 5 * i + j)
            ffn_ref[j, i:i + 1, :] = mine_ref[row, :] + other_ref[row, :]


def unstack(mine, other):
    return pl.pallas_call(
        unstack_body,
        out_shape=(jax.ShapeDtypeStruct((2, 4, D), F32), jax.ShapeDtypeStruct((5, 2, D), F32)),
        in_specs=[VM] * 2,
        out_specs=(VM,) * 2,
        compiler_params=params(MB_SMALL),
        name="unstack",
    )(mine, other)


def swap_cores(value):
    count = lax.axis_size("dp")
    return lax.ppermute(value, "dp", [(i, i ^ 1) for i in range(count)])


def next_chip(value, bits):
    count = lax.axis_size("dp")
    return lax.ppermute(value, "dp", [(i, i ^ 2 * bits) for i in range(count)])


def plane_swap(value, step):
    count, sections = lax.axis_size("dp"), lax.axis_size("section")
    pairs = []
    for s in range(sections):
        for i in range(count):
            other = s ^ (1 if step == i % 2 else 2)
            pairs.append((s * count + i, other * count + i))
    return lax.ppermute(value, ("section", "dp"), pairs)


def flip(value, bits):
    count = lax.axis_size("section")
    return lax.ppermute(value, "section", [(i, i ^ bits) for i in range(count)])


def gather_pieces(own, core, par, ready):
    def part(p):
        return lax.dynamic_slice(own, (0, core * (D // 2) + p * WHOLE, 0), (3, WHOLE, D))

    mine = part(par)
    near, down = flip(mine, 1), flip(part(1 - par), 2)
    near, down, high, *ready = together(near, down, mine[:, HALF_UNIT:], *ready)
    far_a, far_b = flip(near, 2), flip(down, 1)
    near_z, down_z, down_y = next_chip(near, 1), next_chip(down[:, :HALF_UNIT], 1), flip(high, 2)
    mine = [[near, near_z], [down, down_z, down_y], [far_a, far_b]]
    return [piece for group in mine for piece in group + [swap_cores(x) for x in group]], ready


def line_groups():
    count = lax.axis_size("dp")
    return [[r * 8 + i for r in range(count // 8)] for i in range(8)]


def across_lines(value):
    if lax.axis_size("dp") == 8:
        return value
    return lax.psum(value.astype(F32), "dp", axis_index_groups=line_groups()).astype(value.dtype)


def together(*values):
    return lax.optimization_barrier(values)


def shards(inputs, cotangent, segments, matrices, attn_vectors, ffn_vectors):
    section = lax.axis_index("section")
    dp = lax.axis_index("dp")
    core, position = dp % 2, dp // 2
    par = position % 2
    x_bit, y_bit = section % 2, section // 2
    first = jnp.where(core == 0, x_bit, y_bit)
    second = jnp.where(core == 0, y_bit, x_bit)
    own = matrices[0]
    turn = dp // 2 % 2
    places = [jnp.stack([section ^ j, core, par, first, second, turn]).astype(jnp.int32) for j in range(4)]
    seg = lax.dynamic_slice(segments, (R * section, 0, 0), (R, 1, L))
    x = inputs.reshape(T, D)
    cot = cotangent.reshape(T, D)
    pieces, (*places, seg, cot) = gather_pieces(own, core, par, (*places, seg, cot))
    weights = (own, *pieces)
    here = places[0]
    av, fv = attn_vectors, ffn_vectors

    (gc1, gv3, l0, l1,
     q0, k0, v0, n0, q1, k1, v1, n1, c0, hid, mid, act, gp, summed, out, gb1, keep3, send3) = forward(here, x, av, fv, seg, cot, weights)
    got3 = swap_cores(send3)

    keep2a, send2a, gv2a, *grads2 = attn_bwd(0, here, n1, q1, k1, v1, l1, gc1, seg, "attn_bwd_1a")
    ((send3, keep3),) = combine(here, add(3, keep3, got3))
    send2a, send3 = together(send2a, send3)
    got3, got2a = plane_swap(send3, 0), swap_cores(send2a)
    gc1, keep3 = together(gc1, keep3)

    keep2b, send2b, gv2b, _, _, _, gn1 = attn_bwd_last(here, n1, q1, k1, v1, l1, gc1, seg, grads2, weights, "attn_bwd_1b")
    gn1, got2a, got3, send2b = together(gn1, got2a, got3, send2b)
    got2b = swap_cores(send2b)
    (send3, keep3), (send2, keep2) = combine(here, add(4, keep3, got3), (3, [(keep2a, got2a), (keep2b, got2b)], None, 0))
    got3, got2 = plane_swap(send3, 1), plane_swap(send2, 0)
    gb1, keep3 = together(gb1, keep3)

    gb0, gc0, keep1, send1, gv1, gnext = ffn_bwd(here, gb1, gn1, summed, av, hid, gp, mid, act, c0, fv, weights)
    got1 = swap_cores(send1)

    keep0a, send0a, gv0a, *grads0 = attn_bwd(0, here, n0, q0, k0, v0, l0, gc0, seg, "attn_bwd_0a")
    keep2, send0a = together(keep2, send0a)
    (send3, keep3), (send2, keep2) = combine(here, add(5, keep3, got3), add(4, keep2, got2))
    send0a, send2 = together(send0a, send2)
    got3, got2, got0a = next_chip(send3, 1), plane_swap(send2, 1), swap_cores(send0a)
    ((send1, keep1),) = combine(here, (3, [(keep1, got1), (keep0a, got0a)], None, 0))
    got1 = plane_swap(send1, 0)
    gc0, keep1 = together(gc0, keep1)

    keep0b, send0b, gv0b, *grads0b = attn_bwd(1, here, n0, q0, k0, v0, l0, gc0, seg, "attn_bwd_0b")
    send0b, keep2 = together(send0b, keep2)
    (send2, keep2), keep3 = combine(here, add(5, keep2, got2), add(None, keep3, got3))
    send0b, send2 = together(send0b, send2)
    got3, got2, got0b = next_chip(keep3, 2), next_chip(send2, 1), swap_cores(send0b)
    grads0b[0], keep2 = together(grads0b[0], keep2)

    gx, gv0n = inputs_bwd(here, (*grads0, *grads0b), x, gb0, av, weights)
    vec = stack_vectors(gv0n, gv0a, gv0b, gnext, gv2a, gv2b, gv1, gv3)
    (send0, keep0, vec), (send1, keep1), keep2, keep3 = combine(
        here, (3, [(keep0b, got0b)], vec, 0), add(4, keep1, got1), add(None, keep2, got2), add(None, keep3, got3))
    got0, got1, got2, got3 = plane_swap(send0, 0), plane_swap(send1, 1), next_chip(keep2, 2), next_chip(keep3, 1)

    got3, got0 = together(got3, got0)
    (send0, keep0, vec), (send1, keep1), keep2 = combine(
        here, (4, [(keep0, got0)], vec, 1), add(5, keep1, got1), add(None, keep2, got2))
    got0, got1, got2 = plane_swap(send0, 1), next_chip(send1, 1), next_chip(keep2, 1)

    (send0, keep0, vec), keep1 = combine(here, (5, [(keep0, got0)], vec, 1), add(None, keep1, got1))
    got0, got1 = next_chip(send0, 1), next_chip(keep1, 2)

    ((sum0, vec),) = combine(here, (None, [(keep0, got0)], vec, 1))
    got0 = next_chip(sum0, 2)

    got2, got1 = together(got2, got1)
    (keep0, vec), keep1, far = combine(here, (None, [(sum0, got0)], vec, 2), add(None, keep1, got1), far=(keep2, keep3))
    keep0, keep1, keep2, keep3, far = (across_lines(v) for v in (keep0, keep1, keep2, keep3, far))
    far = flip(far, 3)
    got0, got1 = next_chip(keep0, 1), next_chip(keep1, 1)
    vec = across_lines(vec)
    vec_got = swap_cores(vec)
    vec_got, far, got0, got1 = together(vec_got, far, got0, got1)
    grad_attn, grad_ffn = unstack(vec, vec_got)
    grad_ffn = grad_ffn.transpose(1, 0, 2)
    if lax.axis_size("dp") > 8:
        got2, got3 = next_chip(keep2, 1), next_chip(keep3, 1)

    own_part, x_part, y_part = pick(here, keep0, got0, keep1, got1, keep2, got2, keep3, got3)
    x_part, y_part = flip(x_part, 1), flip(y_part, 2)
    far_next = next_chip(far, 1)
    own_other, far_other = swap_cores(own_part), swap_cores(far)
    far_next_other = swap_cores(far_next)
    whole = assemble(here, ((0, 0, None), (1, 0, None), (0, 3, 0), (0, 3, 1), (1, 3, 0), (1, 3, 1)),
                     (own_part, own_other, far, far_next, far_other, far_next_other))
    grad_attn, grad_ffn, x_part, y_part, whole = together(grad_attn, grad_ffn, x_part, y_part, whole)
    others = [swap_cores(v) for v in (x_part, y_part)]
    whole = assemble(here, ((0, 1, None), (0, 2, None)), (x_part, y_part), whole)
    whole = assemble(here, ((1, 1, None), (1, 2, None)), others, whole)
    grad_matrices = whole[None]
    shape = inputs.shape
    return (out.reshape(shape), gx.reshape(shape), grad_matrices, grad_attn, grad_ffn)


def solution(mesh):
    rows = P("section", "dp", None, None)
    mats = P("section", None, None, None)
    return jax.shard_map(
        shards,
        mesh=mesh,
        in_specs=(rows, rows, P(None, "dp", None), mats, P(), P()),
        out_specs=(rows, rows, mats, P(), P()),
        check_vma=False,
    )
```
